32 devices in a mesh: section: 2 (over x), dp: 16 (over z, y, core).
Axes of the slice: x: 2, y: 2, z: 4, core: 2. Of those that a mesh axis runs over, the one named last changes fastest.
Arguments:
- inputs: bfloat16 [2, 32, 256, 768], P(None, 'dp')
- keep_mask: int32 [2, 32, 256], P(None, 'dp'), may hold values 0 or 1
- lengths: int32 [2, 32], P(None, 'dp'), may hold values from 128 to 256, as said below
- slot_order: int32 [32], P('dp'), may hold values from 0 to 1, as said below
- cotangent: bfloat16 [32, 256, 768], P('dp'), may hold values from -6 to 6
- query_projection: bfloat16 [2, 768, 2304], P('section', 'dp')
- query_output: bfloat16 [2, 768, 768], P('section', 'dp'), may hold values from -0.4375 to 0.4375
- query_expand: bfloat16 [2, 768, 3072], P('section', 'dp'), may hold values from -0.21875 to 0.21875
- query_contract: bfloat16 [2, 3072, 768], P('section', 'dp'), may hold values from -0.109375 to 0.109375
- query_gains: bfloat16 [2, 2, 768], P('section', None, 'dp'), may hold values from 0.5 to 1.5
- query_biases: bfloat16 [2, 6, 768], P('section', None, 'dp'), may hold values from -1.75 to 1.75
- query_offsets: bfloat16 [2, 3072], P('section', 'dp'), may hold values from -1.75 to 1.75
- momentum_projection: bfloat16 [2, 768, 2304], P('section', 'dp')
- momentum_output: bfloat16 [2, 768, 768], P('section', 'dp'), may hold values from -0.4375 to 0.4375
- momentum_expand: bfloat16 [2, 768, 3072], P('section', 'dp'), may hold values from -0.21875 to 0.21875
- momentum_contract: bfloat16 [2, 3072, 768], P('section', 'dp'), may hold values from -0.109375 to 0.109375
- momentum_gains: bfloat16 [2, 2, 768], P('section', None, 'dp'), may hold values from 0.5 to 1.5
- momentum_biases: bfloat16 [2, 6, 768], P('section', None, 'dp'), may hold values from -1.75 to 1.75
- momentum_offsets: bfloat16 [2, 3072], P('section', 'dp'), may hold values from -1.75 to 1.75
Outputs:
- pooled: float32 [2, 2, 32, 768], P('section')
- grad_input: float32 [2, 32, 256, 768], P('section', 'dp')
- grad_projection: float32 [2, 768, 2304], P('section', 'dp')
- grad_output: float32 [2, 768, 768], P('section', 'dp')
- grad_expand: float32 [2, 768, 3072], P('section', 'dp')
- grad_contract: float32 [2, 3072, 768], P('section', 'dp')
- grad_gains: float32 [2, 2, 768], P('section', None, 'dp')
- grad_biases: float32 [2, 6, 768], P('section', None, 'dp')
- grad_offsets: float32 [2, 3072], P('section', 'dp')
The draws below stay inside these ranges and needn't reach their ends.
Inputs may be any that keep to these rules, and one draw needn't show every extreme that they name: `lengths`: one crop of each view has all 256 positions. `slot_order`: each aligned block of 2 entries, one device's crops, is a permutation of 0 to 1.
All inputs are finite; a program needn't handle non-finite values. No bound on the sum of `keep_mask` on one device may be relied on, other than what follows from the above.
Results may differ from the reference program's by a relative error of at most 0.02.
Values may be sent and summed in bfloat16 or wider, within the bound.
No kernel may reach another device: no remote copies, remote signals or barrier semaphores. Data moves between devices by JAX's collectives and lax.ppermute only.
A program may use at most 256 MiB of HBM per device.

```python
import jax
import jax.numpy as jnp
from jax import lax

D = 768
HD = 64
FF = 3072
CROP = 256
CROPS_DEV = 2
CROPS_ALL = 32
SECTIONS = 2


def draw_inputs(key, part):
    key = jax.random.fold_in(key, 31)
    common_key, noise_key = jax.random.split(key)
    common = 0.2 * jax.random.normal(common_key, (2, CROPS_ALL, 1, D), jnp.float32)
    noise = jax.random.normal(noise_key, (2, CROPS_ALL, CROP, D), jnp.float32)
    return jnp.clip(common + noise, -6.0, 6.0).astype(jnp.bfloat16)


def scale_thirds(noise):
    columns = jnp.arange(3 * D, dtype=jnp.int32)[None, None, :]
    factor = jnp.where(columns < 2 * D, 1.4, 1.0) * D ** (-0.5)
    return (noise * factor).astype(jnp.bfloat16)


def draw_query_projection(key, part):
    key = jax.random.fold_in(key, 41)
    noise = jnp.clip(jax.random.normal(key, (SECTIONS, D, 3 * D), jnp.float32), -4.0, 4.0)
    return scale_thirds(noise)


def draw_momentum_projection(key, part):
    key = jax.random.fold_in(key, 43)
    noise = jnp.clip(jax.random.normal(key, (SECTIONS, D, 3 * D), jnp.float32), -4.0, 4.0)
    return scale_thirds(noise)


def draw_lengths(key, part):
    key = jax.random.fold_in(key, 11)
    first_key, second_key = jax.random.split(key)
    counts = jax.random.randint(first_key, (2, CROPS_ALL), CROP // 2, CROP + 1)
    chosen = jax.random.randint(second_key, (2, 1), 0, CROPS_ALL)
    places = jnp.arange(CROPS_ALL)[None, :]
    return jnp.where(places == chosen, CROP, counts).astype(jnp.int32)


def draw_slot_order(key, part):
    key = jax.random.fold_in(key, 23)
    device_keys = jax.random.split(key, CROPS_ALL // CROPS_DEV)
    orders = jax.vmap(lambda single: jax.random.permutation(single, CROPS_DEV))(device_keys)
    return orders.reshape(CROPS_ALL).astype(jnp.int32)


def set_ends(values, stream_key, low, largest):
    shape = values.shape
    index_at = [jax.random.randint(jax.random.fold_in(stream_key, axis), (), 0, shape[axis]) for axis in range(len(shape))]
    values = values.at[tuple(index_at)].set(low)
    longest = shape.index(max(shape))
    index_at[longest] = (index_at[longest] + 1) % shape[longest]
    return values.at[tuple(index_at)].set(largest)


def strengthened(drawn, stream_key, source, target, shards_of, factor):
    def block_of(dim):
        return (jnp.arange(drawn.shape[dim]) // (drawn.shape[dim] // shards_of)).reshape((-1,) + (1,) * (drawn.ndim - 1 - dim))

    first = jax.random.permutation(stream_key, shards_of)[block_of(target)]
    second = (block_of(target) + shards_of // 2) % shards_of
    return jnp.where((block_of(source) == first) | (block_of(source) == second), factor * drawn, drawn)


def block_levels(own_key, dims, cuts, least, largest):
    loudness = 1.0
    for axis_at, shards_of in cuts:
        steps = jax.random.uniform(jax.random.fold_in(jax.random.fold_in(own_key, 6), axis_at), (shards_of,), jnp.float32, least / len(cuts), largest / len(cuts))
        loudness = loudness * jnp.repeat(jnp.exp(steps), dims[axis_at] // shards_of).reshape((-1,) + (1,) * (len(dims) - 1 - axis_at))
    return loudness


def gaussian(own_key, dims, spread, most, cuts=(), kind=jnp.bfloat16):
    gain = block_levels(own_key, dims, cuts, -0.22, 0.18) if cuts else 1.0
    values = jax.random.normal(own_key, dims, jnp.float32) * spread * gain
    return jnp.minimum(jnp.maximum(values, -most), most).astype(kind)


def noise_with(rng, extent, scale, most, shards, heavy, held_as=jnp.bfloat16):
    drawn = scale * jax.random.normal(rng, extent, jnp.float32)
    if shards:
        drawn = drawn * block_levels(rng, extent, shards, -0.22, 0.18)
    return jnp.clip(strengthened(drawn, jax.random.fold_in(rng, 3), *heavy), -most, most).astype(held_as)


def setup_inputs(seed: int = 0) -> dict:
    key_of = jax.random.split(jax.random.key(seed), 20)
    return {
        "inputs": draw_inputs(jax.random.fold_in(key_of[19], 71), 0),
        "keep_mask": set_ends((jax.random.randint(key_of[1], (2, CROPS_ALL, CROP), 0, 10) < 9).astype(jnp.int32), jax.random.fold_in(key_of[1], 1), 0, 1),
        "lengths": draw_lengths(jax.random.fold_in(key_of[19], 71), 0),
        "slot_order": draw_slot_order(jax.random.fold_in(key_of[19], 71), 0),
        "cotangent": noise_with(key_of[4], (CROPS_ALL, CROP, D), 1.0, 6.0, ((0, 16),), (0, 2, 16, 2.0)),
        "query_projection": draw_query_projection(jax.random.fold_in(key_of[19], 71), 0),
        "query_output": gaussian(key_of[6], (SECTIONS, D, D), (D // 4) ** -0.5, 0.4375, ((0, 2), (1, 16))),
        "query_expand": gaussian(key_of[7], (SECTIONS, D, FF), D ** -0.5, 0.21875, ((0, 2), (1, 16))),
        "query_contract": gaussian(key_of[8], (SECTIONS, FF, D), FF ** -0.5, 0.109375, ((0, 2), (1, 16))),
        "query_gains": jnp.clip(1.0 + 0.1 * jax.random.normal(key_of[9], (SECTIONS, 2, D), jnp.float32), 0.5, 1.5).astype(jnp.bfloat16),
        "query_biases": gaussian(key_of[10], (SECTIONS, 6, D), 0.3, 1.75, ((0, 2), (2, 16))),
        "query_offsets": gaussian(key_of[11], (SECTIONS, FF), 0.3, 1.75, ((0, 2), (1, 16))),
        "momentum_projection": draw_momentum_projection(jax.random.fold_in(key_of[19], 71), 0),
        "momentum_output": gaussian(key_of[13], (SECTIONS, D, D), (D // 4) ** -0.5, 0.4375, ((0, 2), (1, 16))),
        "momentum_expand": gaussian(key_of[14], (SECTIONS, D, FF), D ** -0.5, 0.21875, ((0, 2), (1, 16))),
        "momentum_contract": gaussian(key_of[15], (SECTIONS, FF, D), FF ** -0.5, 0.109375, ((0, 2), (1, 16))),
        "momentum_gains": jnp.clip(1.0 + 0.1 * jax.random.normal(key_of[16], (SECTIONS, 2, D), jnp.float32), 0.5, 1.5).astype(jnp.bfloat16),
        "momentum_biases": gaussian(key_of[17], (SECTIONS, 6, D), 0.3, 1.75, ((0, 2), (2, 16))),
        "momentum_offsets": gaussian(key_of[18], (SECTIONS, FF), 0.3, 1.75, ((0, 2), (1, 16))),
    }


@jax.custom_vjp
def low(v):
    return lax.optimization_barrier(v.astype(jnp.bfloat16)).astype(jnp.float32)

@jax.custom_vjp
def low_back(v):
    return v

def low_keep(v):
    return (low(v), None)

def low_pass(kept, grad):
    return (grad,)

def back_keep(v):
    return (v, None)

def back_low(kept, grad):
    return (low(grad),)
low.defvjp(low_keep, low_pass)
low_back.defvjp(back_keep, back_low)
epsilon = 1e-12
highest_level = lax.Precision.HIGHEST

def layer_norm(values, norm_gain, norm_offset_vector):
    centred = values - lax.optimization_barrier(jnp.mean(values, axis=-1, keepdims=True))
    variance = lax.optimization_barrier(jnp.mean(centred * centred, axis=-1, keepdims=True))
    return centred * lax.rsqrt(variance + epsilon) * norm_gain + norm_offset_vector

def encode(block_in, validity, params):
    w_proj, w_out, w_expand, w_contract, norm_gains, biases, offsets = params
    crop_count, length, features = block_in.shape
    head_count = features // HD
    rows_flat = block_in.reshape(crop_count * length, features)
    mixture = jnp.dot(rows_flat, w_proj, precision=highest_level)
    queries = low_back(low(mixture[:, :features] + biases[0])).reshape(crop_count, length, head_count, HD)
    key_rows = low_back(low(mixture[:, features:2 * features])).reshape(crop_count, length, head_count, HD)
    values = low_back(low(mixture[:, 2 * features:] + biases[1])).reshape(crop_count, length, head_count, HD)
    scores = low_back(jnp.einsum('clhd,cmhd->chlm', queries, key_rows, precision=highest_level) * HD ** (-0.5))
    scores = jnp.where(validity[:, None, None, :] > 0, scores, -1e+30)
    attn_weights = low(jax.nn.softmax(scores, axis=-1))
    attended = jnp.einsum('chlm,cmhd->clhd', attn_weights, values, precision=highest_level)
    attended = low_back(low(attended.reshape(crop_count * length, features)))
    output = low_back(jnp.dot(attended, w_out, precision=highest_level) + biases[2])
    hidden = layer_norm(rows_flat + output, norm_gains[0], biases[3])
    upward = low_back(jnp.dot(low(hidden), w_expand, precision=highest_level) + offsets)
    active = low(jax.nn.gelu(upward, approximate=False))
    branch = low_back(jnp.dot(active, w_contract, precision=highest_level) + biases[4])
    result = layer_norm(hidden + branch, norm_gains[1], biases[5])
    return result.reshape(crop_count, length, features)

def query_loss(query_in, bridge, params, validity, cotan_rows):
    first_params = tuple((member[0] for member in params))
    second_params = tuple((member[1] for member in params))
    first_out = encode(query_in, validity, first_params)
    second = encode(low_back(low(first_out)) + bridge, validity, second_params)
    loss_value = jnp.sum(second * cotan_rows * validity[..., None])
    return (loss_value, (first_out, second))

def pool_rows(result, validity):
    summed = lax.optimization_barrier(jnp.sum(result * validity[..., None], axis=1))
    return summed / lax.optimization_barrier(jnp.sum(validity, axis=1))[:, None]

def reference(inputs, keep_mask, lengths, slot_order, cotangent, query_projection, query_output, query_expand, query_contract, query_gains, query_biases, query_offsets, momentum_projection, momentum_output, momentum_expand, momentum_contract, momentum_gains, momentum_biases, momentum_offsets):
    query_params = tuple((member.astype(jnp.float32) for member in (query_projection, query_output, query_expand, query_contract, query_gains, query_biases, query_offsets)))
    momentum_params = tuple((member.astype(jnp.float32) for member in (momentum_projection, momentum_output, momentum_expand, momentum_contract, momentum_gains, momentum_biases, momentum_offsets)))
    momentum_first = tuple((member[0] for member in momentum_params))
    momentum_second = tuple((member[1] for member in momentum_params))
    positions = jnp.arange(CROP, dtype=jnp.int32)[None, None, :]
    validity = ((positions < lengths[:, :, None]) & ((keep_mask > 0) | (positions == 0))).astype(jnp.float32)
    group_size = 16
    groups = CROPS_ALL // group_size

    def regroup(array):
        return array.reshape((groups, group_size) + array.shape[1:])
    pieces_all = (regroup(inputs[0].astype(jnp.float32)), regroup(inputs[1].astype(jnp.float32)), regroup(validity[0]), regroup(validity[1]), regroup(cotangent.astype(jnp.float32)))
    zero_grads = tuple((jnp.zeros_like(member) for member in query_params))

    def one_group(running_grads, pieces):
        query_rows, momentum_rows, query_mask, momentum_mask, cotan_rows = pieces

        def group_loss(rows_in, bridge_in, params_in):
            return query_loss(rows_in, bridge_in, params_in, query_mask, cotan_rows)
        bridge = jnp.zeros_like(query_rows)
        loss_value, pullback, outs_pair = jax.vjp(group_loss, query_rows, bridge, query_params, has_aux=True)
        grad_rows, grad_bridge, grad_params = pullback(jnp.ones_like(loss_value))
        first_out, second = outs_pair
        mom_first = encode(momentum_rows, momentum_mask, momentum_first)
        mom_second = encode(low(mom_first), momentum_mask, momentum_second)
        pooled_group = jnp.stack([jnp.stack([pool_rows(first_out, query_mask), pool_rows(mom_first, momentum_mask)]), jnp.stack([pool_rows(second, query_mask), pool_rows(mom_second, momentum_mask)])])
        running_grads = tuple((before + addend for before, addend in zip(running_grads, grad_params)))
        return (running_grads, (pooled_group, jnp.stack([grad_rows, grad_bridge])))
    grads, stacked = lax.scan(one_group, zero_grads, pieces_all)
    grouped_pooled_rows, grad_groups = stacked
    pooled_crops = jnp.moveaxis(grouped_pooled_rows, 0, 2).reshape(2, 2, CROPS_ALL, D)
    grad_input = jnp.moveaxis(grad_groups, 0, 1).reshape(2, CROPS_ALL, CROP, D)
    crop_of_slot = jnp.arange(CROPS_ALL, dtype=jnp.int32) // CROPS_DEV * CROPS_DEV + slot_order
    pooled = pooled_crops[:, :, crop_of_slot]
    return (pooled, grad_input, grads[0], grads[1], grads[2], grads[3], grads[4], grads[5], grads[6])
```

```python
import jax
import jax.numpy as jnp
from jax import lax
from jax.sharding import PartitionSpec as P

HD = 64
MB = 2


epsilon = 1e-12
highest_level = lax.Precision.HIGHEST


def passed_along(block, axis, distance):
    devices = range(lax.axis_size(axis))
    route = [(i - distance, i) for i in devices if i - distance in devices]
    return lax.ppermute(block, axis, route)


def layer_norm(values, norm_gain, norm_offset_vector):
    centred = values - jnp.mean(values, axis=-1, keepdims=True)
    variance = jnp.mean(centred * centred, axis=-1, keepdims=True)
    return centred * lax.rsqrt(variance + epsilon) * norm_gain + norm_offset_vector


def exact_gelu(values):
    return jax.nn.gelu(values, approximate=False)


def take_micro(array, position, count, axis):
    return lax.dynamic_slice_in_dim(array, position * count, count, axis)


def split_heads(matrix, crop_count, length):
    return matrix.reshape(crop_count, length, -1, HD)


def attention_scores(queries, key_rows, validity):
    scores = jnp.einsum(
        "clhd,cmhd->chlm", queries, key_rows, preferred_element_type=jnp.float32
    ) * HD ** (-0.5)
    return jnp.where(validity[:, None, None, :] > 0, scores, -1e30)


def column_sum(matrix):
    return jnp.sum(matrix.astype(jnp.float32), axis=0)


def pool_rows(result, validity):
    summed = jnp.sum(result * validity[..., None], axis=1)
    return summed / jnp.sum(validity, axis=1)[:, None]


def forward_block(block_in, validity, params):
    w_proj, w_out, w_expand, w_contract, norm_gains, biases, offsets = params
    norm_gains = norm_gains.astype(jnp.float32)
    biases = biases.astype(jnp.float32)
    offsets = offsets.astype(jnp.float32)
    crop_count, length, features = block_in.shape
    rows_flat = block_in.reshape(crop_count * length, features)
    mixture = jnp.dot(rows_flat, w_proj, preferred_element_type=jnp.float32)
    queries = (mixture[:, :features] + biases[0]).astype(jnp.bfloat16)
    key_rows = mixture[:, features : 2 * features].astype(jnp.bfloat16)
    values = (mixture[:, 2 * features :] + biases[1]).astype(jnp.bfloat16)
    scores = attention_scores(
        split_heads(queries, crop_count, length),
        split_heads(key_rows, crop_count, length),
        validity,
    )
    top_score = jnp.max(scores, axis=-1, keepdims=True)
    exponent = jnp.exp(scores - top_score)
    denominator = jnp.sum(exponent, axis=-1, keepdims=True)
    attn_weights = (exponent / denominator).astype(jnp.bfloat16)
    log_total = top_score + jnp.log(denominator)
    attended = jnp.einsum(
        "chlm,cmhd->clhd",
        attn_weights,
        split_heads(values, crop_count, length),
        preferred_element_type=jnp.float32,
    )
    attended = attended.reshape(crop_count * length, features).astype(jnp.bfloat16)
    pre_first = (
        rows_flat.astype(jnp.float32)
        + jnp.dot(attended, w_out, preferred_element_type=jnp.float32)
        + biases[2]
    )
    hidden = layer_norm(pre_first, norm_gains[0], biases[3])
    upward = (
        jnp.dot(hidden.astype(jnp.bfloat16), w_expand, preferred_element_type=jnp.float32) + offsets
    )
    active = exact_gelu(upward).astype(jnp.bfloat16)
    pre_second = (
        hidden + jnp.dot(active, w_contract, preferred_element_type=jnp.float32) + biases[4]
    )
    result = layer_norm(pre_second, norm_gains[1], biases[5])
    saved_activations = (
        rows_flat,
        queries,
        key_rows,
        values,
        log_total,
        attended,
        pre_first,
        upward,
        active,
        pre_second,
    )
    return (result.reshape(crop_count, length, features), saved_activations)


def backward_block(grad_result, validity, params, saved_activations):
    w_proj, w_out, w_expand, w_contract, norm_gains, biases, offsets = params
    (
        rows_flat,
        queries,
        key_rows,
        values,
        log_total,
        attended,
        pre_first,
        upward,
        active,
        pre_second,
    ) = saved_activations
    norm_gains = norm_gains.astype(jnp.float32)
    biases = biases.astype(jnp.float32)
    crop_count, length, features = grad_result.shape
    row_total = crop_count * length
    grad_flat = grad_result.reshape(row_total, features)
    second_pull = jax.vjp(layer_norm, pre_second, norm_gains[1], biases[5])[1]
    grad_pre2, grad_gain2, grad_shift2 = second_pull(grad_flat)
    grad_branch = grad_pre2.astype(jnp.bfloat16)
    grad_contract = jnp.einsum("rf,rd->fd", active, grad_branch, preferred_element_type=jnp.float32)
    grad_active = jnp.einsum(
        "rd,fd->rf", grad_branch, w_contract, preferred_element_type=jnp.float32
    )
    grad_upward = jax.vjp(exact_gelu, upward)[1](grad_active)[0].astype(jnp.bfloat16)
    hidden, first_pull = jax.vjp(layer_norm, pre_first, norm_gains[0], biases[3])
    grad_expand = jnp.einsum(
        "rd,rf->df", hidden.astype(jnp.bfloat16), grad_upward, preferred_element_type=jnp.float32
    )
    grad_hidden = grad_pre2 + jnp.einsum(
        "rf,df->rd", grad_upward, w_expand, preferred_element_type=jnp.float32
    )
    grad_pre1, grad_gain1, grad_shift1 = first_pull(grad_hidden)
    grad_output = grad_pre1.astype(jnp.bfloat16)
    grad_w_out = jnp.einsum("rd,re->de", attended, grad_output, preferred_element_type=jnp.float32)
    grad_attended = jnp.einsum(
        "re,de->rd", grad_output, w_out, preferred_element_type=jnp.float32
    ).astype(jnp.bfloat16)
    heads_q = split_heads(queries, crop_count, length)
    heads_k = split_heads(key_rows, crop_count, length)
    heads_v = split_heads(values, crop_count, length)
    heads_grad = split_heads(grad_attended, crop_count, length)
    scores = attention_scores(heads_q, heads_k, validity)
    chances = jnp.exp(scores - log_total)
    grad_values = jnp.einsum(
        "chlm,clhd->cmhd",
        chances.astype(jnp.bfloat16),
        heads_grad,
        preferred_element_type=jnp.float32,
    )
    grad_chances = jnp.einsum(
        "clhd,cmhd->chlm", heads_grad, heads_v, preferred_element_type=jnp.float32
    )
    inner_sum = jnp.sum(grad_chances * chances, axis=-1, keepdims=True)
    grad_scores = (chances * (grad_chances - inner_sum)).astype(jnp.bfloat16)
    grad_queries = jnp.einsum(
        "chlm,cmhd->clhd", grad_scores, heads_k, preferred_element_type=jnp.float32
    ) * HD ** (-0.5)
    grad_keys = jnp.einsum(
        "chlm,clhd->cmhd", grad_scores, heads_q, preferred_element_type=jnp.float32
    ) * HD ** (-0.5)
    grad_mixture = jnp.concatenate(
        [
            grad_queries.reshape(row_total, features),
            grad_keys.reshape(row_total, features),
            grad_values.reshape(row_total, features),
        ],
        axis=1,
    ).astype(jnp.bfloat16)
    grad_proj = jnp.einsum("rd,re->de", rows_flat, grad_mixture, preferred_element_type=jnp.float32)
    grad_in = grad_pre1 + jnp.einsum(
        "re,de->rd", grad_mixture, w_proj, preferred_element_type=jnp.float32
    )
    grad_biases = jnp.stack(
        [
            column_sum(grad_mixture[:, :features]),
            column_sum(grad_mixture[:, 2 * features :]),
            column_sum(grad_output),
            grad_shift1,
            column_sum(grad_branch),
            grad_shift2,
        ]
    )
    grad_gains = jnp.stack([grad_gain1, grad_gain2])
    grad_offsets = column_sum(grad_upward)
    return (
        grad_in.reshape(crop_count, length, features),
        (grad_proj, grad_w_out, grad_expand, grad_contract, grad_gains, grad_biases, grad_offsets),
    )


def pack_columns(w_proj, w_out, w_expand, w_contract, norm_gains, biases, offsets):
    rows, features = w_out.shape
    folded = w_contract.reshape(-1, rows, features)
    groups = folded.shape[0]
    vectors = jnp.concatenate([norm_gains, biases, offsets.reshape(groups, rows)], axis=0)
    vectors = jnp.pad(vectors, ((0, 128 - vectors.shape[0]), (0, 0)))
    return jnp.concatenate(
        [
            w_proj,
            w_out,
            w_expand,
            jnp.moveaxis(folded, 0, 1).reshape(rows, groups * features),
            vectors.T,
        ],
        axis=1,
    )


def unpack_columns(packed, shards_of):
    features = packed.shape[0]
    rows = features // shards_of
    w_proj = packed[:, : 3 * features]
    w_out = packed[:, 3 * features : 4 * features]
    w_expand = packed[:, 4 * features : 8 * features]
    folded = packed[:, 8 * features : 12 * features].reshape(shards_of, rows, -1, features)
    w_contract = jnp.moveaxis(folded, 2, 1).reshape(-1, features)
    vectors = packed[:, 12 * features :]
    lines = vectors[:, :8].T
    offsets = jnp.moveaxis(vectors[:, 8:12].reshape(shards_of, rows, -1), 2, 1).reshape(-1)
    return (w_proj, w_out, w_expand, w_contract, lines[:2], lines[2:8], offsets)


def halving_sum(block, shards_of):
    here = lax.axis_index("dp")
    levels = shards_of.bit_length() - 1
    current = block.reshape((2,) * levels + block.shape[1:])
    for level in range(levels):
        axis = levels - 1 - level
        mine = (here >> level) & 1
        send = lax.dynamic_index_in_dim(current, 1 - mine, axis, keepdims=False)
        keep = lax.dynamic_index_in_dim(current, mine, axis, keepdims=False)
        route = [(i, i ^ (1 << level)) for i in range(shards_of)]
        got = lax.ppermute(send, "dp", route)
        current = (keep.astype(jnp.float32) + got.astype(jnp.float32)).astype(jnp.bfloat16)
    return current


def scatter_sum(terms, shards_of):
    grad_proj, grad_out, grad_expand, grad_contract, grad_gains, grad_biases, grad_offsets = terms
    features = grad_out.shape[0]
    rows = features // shards_of
    groups = grad_contract.shape[0] // features

    def folded(matrix):
        return matrix.astype(jnp.bfloat16).reshape(shards_of, rows, -1)

    contract = grad_contract.astype(jnp.bfloat16).reshape(shards_of, groups, rows, features)
    contract = jnp.moveaxis(contract, 1, 2).reshape(shards_of, rows, groups * features)
    lines = jnp.concatenate([grad_gains, grad_biases], axis=0).T.reshape(shards_of, rows, 8)
    marks = jnp.moveaxis(grad_offsets.reshape(shards_of, groups, rows), 1, 2)
    vectors = jnp.concatenate([lines, marks], axis=2)
    coarse = vectors.astype(jnp.bfloat16)
    fine = (vectors - coarse.astype(jnp.float32)).astype(jnp.bfloat16)
    vectors = jnp.concatenate([coarse, fine], axis=2)
    vectors = jnp.pad(vectors, ((0, 0), (0, 0), (0, 128 - vectors.shape[2])))
    half = 2 * features
    expand = folded(grad_expand)
    proj = folded(grad_proj)
    chunks = [
        contract[:, :, :half],
        contract[:, :, half:],
        expand[:, :, :half],
        expand[:, :, half:],
        jnp.concatenate([folded(grad_out), proj[:, :, :features]], axis=2),
        jnp.concatenate([proj[:, :, features:], vectors], axis=2),
    ]
    sums = [halving_sum(chunk, shards_of).astype(jnp.float32) for chunk in chunks]
    contract_sum = jnp.concatenate(sums[:2], axis=1).reshape(rows, groups, features)
    contract_sum = jnp.moveaxis(contract_sum, 1, 0).reshape(groups * rows, features)
    expand_sum = jnp.concatenate(sums[2:4], axis=1)
    out_sum = sums[4][:, :features]
    proj_sum = jnp.concatenate([sums[4][:, features:], sums[5][:, :half]], axis=1)
    vector_sum = sums[5][:, half : half + 12] + sums[5][:, half + 12 : half + 24]
    lines = vector_sum.T
    return (
        proj_sum,
        out_sum,
        expand_sum,
        contract_sum,
        lines[:2],
        lines[2:8],
        lines[8:].reshape(groups * rows),
    )


def shards(
    inputs,
    keep_mask,
    lengths,
    slot_order,
    cotangent,
    query_projection,
    query_output,
    query_expand,
    query_contract,
    query_gains,
    query_biases,
    query_offsets,
    momentum_projection,
    momentum_output,
    momentum_expand,
    momentum_contract,
    momentum_gains,
    momentum_biases,
    momentum_offsets,
):
    section_index = lax.axis_index("section")
    first_section = section_index == 0
    crop_count = inputs.shape[1]
    crop_len = inputs.shape[2]
    features = inputs.shape[3]
    per_micro = crop_count // MB
    n_dp = lax.axis_size("dp")
    share = features // n_dp
    query_all = pack_columns(
        query_projection[0],
        query_output[0],
        query_expand[0],
        query_contract[0],
        query_gains[0],
        query_biases[0],
        query_offsets[0],
    )
    momentum_all = pack_columns(
        momentum_projection[0],
        momentum_output[0],
        momentum_expand[0],
        momentum_contract[0],
        momentum_gains[0],
        momentum_biases[0],
        momentum_offsets[0],
    )
    width = query_all.shape[1]
    early = 3 * features
    momentum_early = momentum_all[:, :early]
    momentum_late = momentum_all[:, early:]
    gathered_first = lax.all_gather(
        jnp.concatenate([query_all, momentum_early], axis=1), "dp", axis=0, tiled=True
    )
    momentum_late, gathered_first = lax.optimization_barrier((momentum_late, gathered_first))
    gathered_second = lax.all_gather(momentum_late, "dp", axis=0, tiled=True)
    query_params = unpack_columns(gathered_first[:, :width], n_dp)
    momentum_params = unpack_columns(
        jnp.concatenate([gathered_first[:, width:], gathered_second], axis=1), n_dp
    )
    selector = slot_order[:, None] == jnp.arange(crop_count, dtype=jnp.int32)[None, :]
    lower_selection = selector.astype(jnp.bfloat16)
    full_selection = selector.astype(jnp.float32)
    positions = lax.broadcasted_iota(jnp.int32, keep_mask.shape, 2)
    validity = ((positions < lengths[:, :, None]) & ((keep_mask > 0) | (positions == 0))).astype(
        jnp.float32
    )
    slot_inputs = jnp.einsum(
        "sc,vcld->vsld", lower_selection, inputs, preferred_element_type=jnp.float32
    ).astype(jnp.bfloat16)
    slot_valid = jnp.einsum("sc,vcl->vsl", full_selection, validity, precision=highest_level)
    slot_cotangent = jnp.einsum(
        "yj,jgf->ygf", lower_selection, cotangent, preferred_element_type=jnp.float32
    ).astype(jnp.bfloat16)
    received = jnp.zeros((2, per_micro, crop_len, features), jnp.bfloat16)
    stored_ticks = []
    pooled_ticks = []
    for moment in range(MB + 1):
        micro_index = jnp.clip(moment - section_index, 0, MB - 1)
        local_in = take_micro(slot_inputs, micro_index, per_micro, 1)
        valid_now = take_micro(slot_valid, micro_index, per_micro, 1)
        block_in = jnp.where(first_section, local_in, received)
        query_out, saved_activations = forward_block(block_in[0], valid_now[0], query_params)
        momentum_out = forward_block(block_in[1], valid_now[1], momentum_params)[0]
        stored_ticks.append(saved_activations)
        pooled_ticks.append(
            jnp.stack([pool_rows(query_out, valid_now[0]), pool_rows(momentum_out, valid_now[1])])
        )
        if moment < MB:
            received = passed_along(
                jnp.stack([query_out, momentum_out]).astype(jnp.bfloat16), "section", 1
            )
    pooled_all = jnp.stack(pooled_ticks)
    pooled_live = lax.dynamic_slice_in_dim(pooled_all, section_index, MB, 0)
    pooled_slots = jnp.moveaxis(pooled_live, 1, 0).reshape(2, crop_count, features)
    pooled = lax.all_gather(pooled_slots, "dp", axis=1, tiled=True)[None]
    stored_stack = jax.tree.map(lambda *members: jnp.stack(members), *stored_ticks)
    back_received = jnp.zeros((per_micro, crop_len, features), jnp.bfloat16)
    grad_ticks = []
    pending = None
    for moment in range(MB + 1):
        micro_index = moment - 1 + section_index
        is_live = (micro_index >= 0) & (micro_index < MB)
        clipped = jnp.clip(micro_index, 0, MB - 1)
        valid_now = take_micro(slot_valid[0], clipped, per_micro, 0)
        own_grad = (
            take_micro(slot_cotangent, clipped, per_micro, 0).astype(jnp.float32)
            * valid_now[..., None]
        )
        incoming = jnp.where(first_section, back_received.astype(jnp.float32), own_grad)
        incoming = jnp.where(is_live, incoming, 0.0)
        forward_tick = jnp.clip(moment - 1 + 2 * section_index, 0, MB)
        saved_activations = jax.tree.map(
            lambda stacked: lax.dynamic_index_in_dim(stacked, forward_tick, 0, False), stored_stack
        )
        grad_in, grad_terms = backward_block(incoming, valid_now, query_params, saved_activations)
        grad_ticks.append(grad_in)
        pending = (
            grad_terms
            if pending is None
            else tuple((before + addend for before, addend in zip(pending, grad_terms)))
        )
        if moment < MB:
            back_received = passed_along(grad_in.astype(jnp.bfloat16), "section", -1)
    totals = scatter_sum(pending, n_dp)
    grad_all = jnp.stack(grad_ticks)
    live_gradient = lax.dynamic_slice_in_dim(grad_all, 1 - section_index, MB, 0).reshape(
        crop_count, crop_len, features
    )
    crop_gradients = jnp.einsum(
        "ka,kxo->axo", full_selection, live_gradient, precision=highest_level
    )
    grad_input = crop_gradients[None]
    return (
        pooled,
        grad_input,
        totals[0][None],
        totals[1][None],
        totals[2][None],
        totals[3][None],
        totals[4][None],
        totals[5][None],
        totals[6][None],
    )


def solution(mesh):
    in_specs = (
        P(None, "dp", None, None),
        P(None, "dp", None),
        P(None, "dp"),
        P("dp"),
        P("dp", None, None),
        P("section", "dp", None),
        P("section", "dp", None),
        P("section", "dp", None),
        P("section", "dp", None),
        P("section", None, "dp"),
        P("section", None, "dp"),
        P("section", "dp"),
        P("section", "dp", None),
        P("section", "dp", None),
        P("section", "dp", None),
        P("section", "dp", None),
        P("section", None, "dp"),
        P("section", None, "dp"),
        P("section", "dp"),
    )
    out_specs = (
        P("section", None, None, None),
        P("section", "dp", None, None),
        P("section", "dp", None),
        P("section", "dp", None),
        P("section", "dp", None),
        P("section", "dp", None),
        P("section", None, "dp"),
        P("section", None, "dp"),
        P("section", "dp"),
    )
    return jax.shard_map(shards, mesh=mesh, in_specs=in_specs, out_specs=out_specs, check_vma=False)
```

```python
import functools

import jax
import jax.numpy as jnp
from jax import lax
from jax.experimental import pallas as pl
from jax.experimental.pallas import tpu as pltpu
from jax.sharding import PartitionSpec as P

HD = 64
BLOCK = 48
STRIP = 32
VMEM_LIMIT = 56 * 1024 * 1024

epsilon = 1e-12
SCALE = HD ** (-0.5)

ANY = pl.BlockSpec(memory_space=pl.ANY)
VMEM = pl.BlockSpec(memory_space=pltpu.VMEM)
SMEM = pl.BlockSpec(memory_space=pltpu.SMEM)


def dot_nn(a, b):
    return jnp.dot(a, b, preferred_element_type=jnp.float32)


def dot_nt(a, b):
    return lax.dot_general(a, b, (((1,), (1,)), ((), ())), preferred_element_type=jnp.float32)


def dot_tn(a, b):
    return lax.dot_general(a, b, (((0,), (0,)), ((), ())), preferred_element_type=jnp.float32)


def gelu_parts(values):
    size = jnp.abs(values)
    inverse = 1.0 / (1.0 + (0.3275911 * 0.5**0.5) * size)
    series = 0.5 * 1.061405429
    for factor in (-1.453152027, 1.421413741, -0.284496736, 0.254829592):
        series = series * inverse + 0.5 * factor
    bell = jnp.exp(-0.5 * (values * values))
    tail = series * inverse * bell
    phi = jnp.where(values >= 0, 1.0 - tail, tail)
    return values * phi, phi + values * bell * 0.3989422804014327


def each_strip(rows, body, carry=None):
    def step(i, held):
        return body(pl.ds(pl.multiple_of(i * STRIP, STRIP), STRIP), held)

    return lax.fori_loop(0, rows // STRIP, step, carry)


def by_eights(values):
    return jnp.sum(values.reshape(-1, 8, values.shape[-1]), axis=0)


def normalised(values):
    centred = values - jnp.mean(values, axis=-1, keepdims=True)
    variance = jnp.mean(centred * centred, axis=-1, keepdims=True)
    scale = lax.rsqrt(variance + epsilon)
    return centred * scale, scale


def weight_copies(layout, packs, buffers, sems):
    copies = {}
    for at, (name, pack, source, width, target) in enumerate(layout):
        block = packs[pack].at[:, :, pl.ds(source, width)]
        if name == "contract":
            place = buffers[name].at[:, target]
        else:
            place = buffers[name].at[:, :, pl.ds(target, width)]
        copies.setdefault(name, []).append(pltpu.make_async_copy(block, place, sems.at[at]))
    return copies


def flat(block):
    return block.reshape(-1, block.shape[-1])


def forward_kernel(layout, pack_count, crops, saved_count, kept_count, *refs):
    flag, vrow, vcol, lines, offs, x_hbm = refs[:6]
    packs = refs[6 : 6 + pack_count]
    refs = refs[6 + pack_count + kept_count :]
    y_out, pooled_out = refs[:2]
    saved = refs[2 : 2 + saved_count]
    (
        x_buf, w_proj, w_out, w_expand, w_contract, mix, probs, att, low, hat1, hat2,
        rstd1, rstd2, act, slope, wide, hidden, w_sems, io_sems,
    ) = refs[2 + saved_count :]
    rows, features = x_buf.shape
    buffers = {"proj": w_proj, "out": w_out, "expand": w_expand, "contract": w_contract}

    @pl.when(flag[0] == 1)
    def _():
        copies = weight_copies(layout, packs, buffers, w_sems)
        for name in ("proj", "out", "expand", "contract"):
            for copy in copies[name]:
                copy.start()

        def arrive(name):
            for copy in copies[name]:
                copy.wait()

        for crop in range(crops):
            fetch = pltpu.make_async_copy(x_hbm.at[crop], x_buf, io_sems.at[0])
            fetch.start()
            fetch.wait()
            if crop == 0:
                arrive("proj")
            for third in range(3):
                columns = pl.ds(third * features, features)
                part = dot_nn(x_buf[...], flat(w_proj[:, :, columns]))
                if third != 1:
                    part = part + lines[2 + third // 2 : 3 + third // 2, :]
                mix[:, columns] = part.astype(jnp.bfloat16)
            head_low = lax.broadcasted_iota(jnp.int32, (rows, 2 * HD), 1) < HD
            valid = jnp.broadcast_to(vrow[crop] > 0, (rows, rows))

            def pair_step(pair, _):
                at = pl.multiple_of(pair * 2 * HD, 2 * HD)
                q = mix[:, pl.ds(at, 2 * HD)]
                k = mix[:, pl.ds(at + features, 2 * HD)]
                v = mix[:, pl.ds(at + 2 * features, 2 * HD)]
                outs = []
                for side in range(2):
                    lanes = head_low if side == 0 else jnp.logical_not(head_low)
                    own = jnp.where(lanes, q.astype(jnp.float32) * SCALE, 0.0).astype(jnp.bfloat16)
                    scores = jnp.where(valid, dot_nt(own, k), -1e30)
                    top = jnp.max(scores, axis=-1, keepdims=True)
                    weights = jnp.exp(scores - top)
                    total = jnp.sum(weights, axis=-1, keepdims=True)
                    weights = (weights * (1.0 / total)).astype(jnp.bfloat16)
                    if saved_count:
                        probs[2 * pair + side] = weights
                    outs.append(dot_nn(weights, v))
                att[:, pl.ds(at, 2 * HD)] = jnp.where(head_low, outs[0], outs[1]).astype(jnp.bfloat16)

            lax.fori_loop(0, features // (2 * HD), pair_step, None)
            sends = []

            def keep(index, source):
                if saved_count:
                    copy = pltpu.make_async_copy(source, saved[index], io_sems.at[1 + index])
                    copy.start()
                    sends.append(copy)

            keep(0, mix)
            keep(1, probs)
            keep(2, att)
            if crop == 0:
                arrive("out")
            wide[...] = dot_nn(att[...], flat(w_out[...]))

            def first_norm(at, _):
                total = x_buf[at, :].astype(jnp.float32) + wide[at, :] + lines[4:5, :]
                hat, scale = normalised(total)
                value = hat * lines[0:1, :] + lines[5:6, :]
                hidden[at, :] = value
                low[at, :] = value.astype(jnp.bfloat16)
                if saved_count:
                    hat1[at, :] = hat.astype(jnp.bfloat16)
                    rstd1[at, :] = jnp.broadcast_to(scale, (STRIP, 128))

            each_strip(rows, first_norm)
            keep(3, low)
            keep(4, hat1)
            keep(5, rstd1)
            if crop == 0:
                arrive("expand")
            groups = w_expand.shape[2] // features
            ahead = None
            for group in range(groups):
                columns = pl.ds(group * features, features)
                wide[...] = dot_nn(low[...], flat(w_expand[:, :, columns]))

                def activate(at, _):
                    value, gradient = gelu_parts(wide[at, :] + offs[:, columns])
                    act[at, columns] = value.astype(jnp.bfloat16)
                    if saved_count:
                        slope[at, columns] = gradient.astype(jnp.bfloat16)

                each_strip(rows, activate)
                if crop == 0 and group == 0:
                    arrive("contract")
                stack = w_contract.shape[0] // groups
                hidden[...] += dot_nn(
                    act[:, columns], flat(w_contract[group * stack : (group + 1) * stack])
                )
            keep(6, act)
            keep(7, slope)

            def second_norm(at, held):
                hat, scale = normalised(hidden[at, :] + lines[6:7, :])
                value = hat * lines[1:2, :] + lines[7:8, :]
                y_out[crop, at, :] = value.astype(jnp.bfloat16)
                if saved_count:
                    hat2[at, :] = hat.astype(jnp.bfloat16)
                    rstd2[at, :] = jnp.broadcast_to(scale, (STRIP, 128))
                return held + by_eights(value * vcol[crop, at, :])

            total = each_strip(rows, second_norm, jnp.zeros((8, features), jnp.float32))
            count = jnp.sum(vrow[crop], axis=-1, keepdims=True)
            pooled_out[crop] = jnp.sum(total, axis=0, keepdims=True) / count
            keep(8, hat2)
            keep(9, rstd2)
            for copy in sends:
                copy.wait()


def forward_block(flag, x, vrow, vcol, lines, offs, packs, layout, save, kept=()):
    crops, rows, features = x.shape
    hidden_size = offs.shape[-1]
    heads = features // HD
    blocks = features // BLOCK
    bf16, f32 = jnp.bfloat16, jnp.float32
    shapes = []
    if save:
        shapes = [
            ((rows, 3 * features), bf16),
            ((heads, rows, rows), bf16),
            ((rows, features), bf16),
            ((rows, features), bf16),
            ((rows, features), bf16),
            ((rows, 128), f32),
            ((rows, hidden_size), bf16),
            ((rows, hidden_size), bf16),
            ((rows, features), bf16),
            ((rows, 128), f32),
        ]
    kept = tuple(kept)
    out_shape = [
        jax.ShapeDtypeStruct((crops, rows, features), bf16),
        jax.ShapeDtypeStruct((crops, 1, features), f32),
    ] + [jax.ShapeDtypeStruct(*shape) for shape in shapes]
    flops = 2 * crops * rows * (4 * features * features + 2 * features * hidden_size)
    first_kept = 6 + len(packs)
    result = pl.pallas_call(
        functools.partial(forward_kernel, layout, len(packs), crops, len(shapes), len(kept)),
        out_shape=out_shape,
        in_specs=[SMEM] + [VMEM] * 4 + [ANY] * (1 + len(packs) + len(kept)),
        out_specs=[VMEM, VMEM] + [ANY] * len(shapes),
        scratch_shapes=[
            pltpu.VMEM((rows, features), bf16),
            pltpu.VMEM((blocks, BLOCK, 3 * features), bf16),
            pltpu.VMEM((blocks, BLOCK, features), bf16),
            pltpu.VMEM((blocks, BLOCK, hidden_size), bf16),
            pltpu.VMEM((blocks, hidden_size // features, BLOCK, features), bf16),
            pltpu.VMEM((rows, 3 * features), bf16),
            pltpu.VMEM((heads, rows, rows) if save else (8, 128), bf16),
            pltpu.VMEM((rows, features), bf16),
            pltpu.VMEM((rows, features), bf16),
            pltpu.VMEM((rows, features), bf16),
            pltpu.VMEM((rows, features), bf16),
            pltpu.VMEM((rows, 128), f32),
            pltpu.VMEM((rows, 128), f32),
            pltpu.VMEM((rows, hidden_size), bf16),
            pltpu.VMEM((rows, hidden_size) if save else (8, 128), bf16),
            pltpu.VMEM((rows, features), f32),
            pltpu.VMEM((rows, features), f32),
            pltpu.SemaphoreType.DMA((len(layout),)),
            pltpu.SemaphoreType.DMA((11,)),
        ],
        input_output_aliases={first_kept + i: 2 + i for i in range(len(kept))},
        compiler_params=pltpu.CompilerParams(vmem_limit_bytes=VMEM_LIMIT),
        cost_estimate=pl.CostEstimate(flops=flops, bytes_accessed=20_000_000, transcendentals=0),
        name="forward_save" if save else "forward_only",
    )(flag, vrow, vcol, lines, offs, x, *packs, *kept)
    return result[0], result[1], tuple(result[2:])


def backward_kernel(layout, pack_count, kept_count, *refs):
    flag, vcol, lines, g_hbm = refs[:4]
    packs = refs[4 : 4 + pack_count]
    saved = refs[4 + pack_count : 14 + pack_count]
    refs = refs[14 + pack_count + kept_count :]
    vec_out, offs_out, dx_low = refs[:3]
    dx_out, branch_out, upward_out, output_out, mixture_out = refs[3:8]
    (
        g_buf, w_proj, w_out, w_expand, w_contract, mix, probs, hat1, hat2, rstd1, rstd2, slope,
        dbranch, dupward, doutput, datt, dmix, wide, total, w_sems, in_sems, out_sems,
    ) = refs[8:]
    rows, features = g_buf.shape
    groups = w_expand.shape[2] // features
    buffers = {"proj": w_proj, "out": w_out, "expand": w_expand, "contract": w_contract}

    @pl.when(flag[0] == 1)
    def _():
        copies = weight_copies(layout, packs, buffers, w_sems)
        fetches = {}
        for at, (name, source, place) in enumerate(
            (
                ("g", g_hbm, g_buf),
                ("hat2", saved[8], hat2),
                ("rstd2", saved[9], rstd2),
                ("slope", saved[7], slope),
                ("hat1", saved[4], hat1),
                ("rstd1", saved[5], rstd1),
                ("mix", saved[0], mix),
                ("probs", saved[1], probs),
            )
        ):
            fetches[name] = [pltpu.make_async_copy(source, place, in_sems.at[at])]
        fetches.update(copies)
        for name in (
            "g", "hat2", "rstd2", "contract", "slope", "expand", "hat1", "rstd1", "out", "mix",
            "probs", "proj",
        ):
            for copy in fetches[name]:
                copy.start()

        def arrive(*names):
            for name in names:
                for copy in fetches[name]:
                    copy.wait()

        sends = []

        def send(index, source, place):
            copy = pltpu.make_async_copy(source, place, out_sems.at[index])
            copy.start()
            sends.append(copy)

        zero = jnp.zeros((8, features), jnp.float32)

        def norm_back(gradient, hat, scale, gain):
            weighted = gradient * gain
            mean = jnp.mean(weighted, axis=-1, keepdims=True)
            slant = jnp.mean(weighted * hat, axis=-1, keepdims=True)
            return scale * (weighted - mean - hat * slant)

        arrive("g", "hat2", "rstd2")

        def second_norm(at, held):
            gradient = g_buf[at, :].astype(jnp.float32) * vcol[at, :]
            hat = hat2[at, :].astype(jnp.float32)
            moved = norm_back(gradient, hat, rstd2[at, 0:1], lines[1:2, :])
            total[at, :] = moved
            rounded = moved.astype(jnp.bfloat16)
            dbranch[at, :] = rounded
            return (
                held[0] + by_eights(gradient * hat),
                held[1] + by_eights(gradient),
                held[2] + by_eights(rounded.astype(jnp.float32)),
            )

        sums = each_strip(rows, second_norm, (zero, zero, zero))
        for line, partial in zip((1, 7, 6), sums):
            vec_out[line : line + 1, :] = jnp.sum(partial, axis=0, keepdims=True)
        send(0, dbranch, branch_out)
        arrive("contract", "slope")
        stack = w_contract.shape[0] // groups
        for group in range(groups):
            columns = pl.ds(group * features, features)
            wide[...] = dot_nt(
                dbranch[...], flat(w_contract[group * stack : (group + 1) * stack])
            )

            def through(at, held):
                rounded = (wide[at, :] * slope[at, columns].astype(jnp.float32)).astype(jnp.bfloat16)
                dupward[at, columns] = rounded
                return held + by_eights(rounded.astype(jnp.float32))

            partial = each_strip(rows, through, zero)
            offs_out[:, columns] = jnp.sum(partial, axis=0, keepdims=True)
            if group == 0:
                arrive("expand")
            total[...] += dot_nt(dupward[:, columns], flat(w_expand[:, :, columns]))
        send(1, dupward, upward_out)
        arrive("hat1", "rstd1")

        def first_norm(at, held):
            gradient = total[at, :]
            hat = hat1[at, :].astype(jnp.float32)
            moved = norm_back(gradient, hat, rstd1[at, 0:1], lines[0:1, :])
            total[at, :] = moved
            rounded = moved.astype(jnp.bfloat16)
            doutput[at, :] = rounded
            return (
                held[0] + by_eights(gradient * hat),
                held[1] + by_eights(gradient),
                held[2] + by_eights(rounded.astype(jnp.float32)),
            )

        sums = each_strip(rows, first_norm, (zero, zero, zero))
        for line, partial in zip((0, 5, 4), sums):
            vec_out[line : line + 1, :] = jnp.sum(partial, axis=0, keepdims=True)
        send(2, doutput, output_out)
        arrive("out")
        datt[...] = dot_nt(doutput[...], flat(w_out[...])).astype(jnp.bfloat16)
        arrive("mix", "probs")
        head_low = lax.broadcasted_iota(jnp.int32, (rows, 2 * HD), 1) < HD

        def pair_step(pair, _):
            at = pl.multiple_of(pair * 2 * HD, 2 * HD)
            q = mix[:, pl.ds(at, 2 * HD)]
            k = mix[:, pl.ds(at + features, 2 * HD)]
            v = mix[:, pl.ds(at + 2 * features, 2 * HD)]
            pull = datt[:, pl.ds(at, 2 * HD)]
            parts = []
            for side in range(2):
                lanes = head_low if side == 0 else jnp.logical_not(head_low)
                own = jnp.where(lanes, pull, jnp.zeros_like(pull))
                weights = probs[2 * pair + side]
                dweights = dot_nt(own, v)
                wide_weights = weights.astype(jnp.float32)
                product = dweights * wide_weights
                inner = jnp.sum(product, axis=-1, keepdims=True)
                dscores = (product - wide_weights * inner).astype(jnp.bfloat16)
                parts.append((dot_nn(dscores, k), dot_tn(dscores, q), dot_tn(weights, pull)))
            for place, (first, second) in enumerate(zip(*parts)):
                merged = jnp.where(head_low, first, second)
                if place < 2:
                    merged = merged * SCALE
                dmix[:, pl.ds(at + place * features, 2 * HD)] = merged.astype(jnp.bfloat16)

        lax.fori_loop(0, features // (2 * HD), pair_step, None)
        send(3, dmix, mixture_out)

        def mixture_sums(at, held):
            return (
                held[0] + by_eights(dmix[at, 0:features].astype(jnp.float32)),
                held[1] + by_eights(dmix[at, 2 * features : 3 * features].astype(jnp.float32)),
            )

        sums = each_strip(rows, mixture_sums, (zero, zero))
        for line, partial in zip((2, 3), sums):
            vec_out[line : line + 1, :] = jnp.sum(partial, axis=0, keepdims=True)
        arrive("proj")
        for third in range(3):
            columns = pl.ds(third * features, features)
            total[...] += dot_nt(dmix[:, columns], flat(w_proj[:, :, columns]))
        dx_low[...] = total[...].astype(jnp.bfloat16)
        send(4, total, dx_out)
        for copy in sends:
            copy.wait()


def backward_block(flag, gradient, vcol, lines, packs, layout, saved, kept=()):
    rows, features = gradient.shape
    hidden_size = saved[6].shape[-1]
    heads = features // HD
    blocks = features // BLOCK
    bf16, f32 = jnp.bfloat16, jnp.float32
    kept = tuple(kept)
    out_shape = [
        jax.ShapeDtypeStruct((8, features), f32),
        jax.ShapeDtypeStruct((1, hidden_size), f32),
        jax.ShapeDtypeStruct((rows, features), bf16),
        jax.ShapeDtypeStruct((rows, features), f32),
        jax.ShapeDtypeStruct((rows, features), bf16),
        jax.ShapeDtypeStruct((rows, hidden_size), bf16),
        jax.ShapeDtypeStruct((rows, features), bf16),
        jax.ShapeDtypeStruct((rows, 3 * features), bf16),
    ]
    flops = 2 * rows * (4 * features * features + 2 * features * hidden_size)
    first_kept = 4 + len(packs) + 10
    result = pl.pallas_call(
        functools.partial(backward_kernel, layout, len(packs), len(kept)),
        out_shape=out_shape,
        in_specs=[SMEM] + [VMEM] * 2 + [ANY] * (1 + len(packs) + 10 + len(kept)),
        out_specs=[VMEM] * 3 + [ANY] * 5,
        scratch_shapes=[
            pltpu.VMEM((rows, features), bf16),
            pltpu.VMEM((blocks, BLOCK, 3 * features), bf16),
            pltpu.VMEM((blocks, BLOCK, features), bf16),
            pltpu.VMEM((blocks, BLOCK, hidden_size), bf16),
            pltpu.VMEM((blocks, hidden_size // features, BLOCK, features), bf16),
            pltpu.VMEM((rows, 3 * features), bf16),
            pltpu.VMEM((heads, rows, rows), bf16),
            pltpu.VMEM((rows, features), bf16),
            pltpu.VMEM((rows, features), bf16),
            pltpu.VMEM((rows, 128), f32),
            pltpu.VMEM((rows, 128), f32),
            pltpu.VMEM((rows, hidden_size), bf16),
            pltpu.VMEM((rows, features), bf16),
            pltpu.VMEM((rows, hidden_size), bf16),
            pltpu.VMEM((rows, features), bf16),
            pltpu.VMEM((rows, features), bf16),
            pltpu.VMEM((rows, 3 * features), bf16),
            pltpu.VMEM((rows, features), f32),
            pltpu.VMEM((rows, features), f32),
            pltpu.SemaphoreType.DMA((len(layout),)),
            pltpu.SemaphoreType.DMA((8,)),
            pltpu.SemaphoreType.DMA((5,)),
        ],
        input_output_aliases={first_kept + i: 3 + i for i in range(len(kept))},
        compiler_params=pltpu.CompilerParams(vmem_limit_bytes=VMEM_LIMIT),
        cost_estimate=pl.CostEstimate(flops=flops, bytes_accessed=25_000_000, transcendentals=0),
        name="backward_data",
    )(flag, vcol, lines, gradient, *packs, *saved, *kept)
    return result[:3], tuple(result[3:])


def contract_kernel(core, act0, act1, grad0, grad1, *refs):
    outs, (piece,) = refs[:4], refs[4:]
    features = grad0.shape[1]
    groups = act0.shape[1] // features
    span = outs[0].shape[2] // features
    stack = 2 * outs[0].shape[0] // groups
    for part in range(groups):
        columns = pl.ds(part * features, features)
        piece[...] = (
            dot_tn(act0[:, columns], grad0[...]) + dot_tn(act1[:, columns], grad1[...])
        ).astype(jnp.bfloat16)
        for block in range(stack):
            place = (part * stack + block) // 2
            for group in range(groups):
                rows = pl.ds((block * groups + group) * BLOCK, BLOCK)
                at = pl.ds((group % span) * features, features)
                keep, send = outs[2 * (group // span)], outs[2 * (group // span) + 1]

                @pl.when(core[0] == block % 2)
                def _():
                    keep[place, :, at] = piece[rows, :]

                @pl.when(core[0] != block % 2)
                def _():
                    send[place, :, at] = piece[rows, :]


def row_kernel(plan, core, *refs):
    count = len({source for entry in plan for source in entry[:2]})
    sources, outs, (piece,) = refs[: 2 * count], refs[2 * count : -1], refs[-1:]
    features = piece.shape[0]
    width = piece.shape[1]
    for left, right, column, target, to in plan:
        columns = pl.ds(column, width)
        piece[...] = (
            dot_tn(sources[2 * left][...], sources[2 * right][:, columns])
            + dot_tn(sources[2 * left + 1][...], sources[2 * right + 1][:, columns])
        ).astype(jnp.bfloat16)
        keep, send = outs[2 * target], outs[2 * target + 1]
        for block in range(features // BLOCK):
            rows = pl.ds(block * BLOCK, BLOCK)

            @pl.when(core[0] == block % 2)
            def _():
                keep[block // 2, :, pl.ds(to, width)] = piece[rows, :]

            @pl.when(core[0] != block % 2)
            def _():
                send[block // 2, :, pl.ds(to, width)] = piece[rows, :]


def weight_gradient(kernel, core, operands, targets, features, width, name):
    blocks = features // BLOCK // 2
    shape = jax.ShapeDtypeStruct((blocks, BLOCK, 2 * features), jnp.bfloat16)
    return pl.pallas_call(
        kernel,
        out_shape=[shape] * (2 * targets),
        in_specs=[SMEM] + [VMEM] * len(operands),
        out_specs=[VMEM] * (2 * targets),
        scratch_shapes=[pltpu.VMEM((features, width), jnp.bfloat16)],
        compiler_params=pltpu.CompilerParams(vmem_limit_bytes=VMEM_LIMIT),
        cost_estimate=pl.CostEstimate(
            flops=4 * targets * features * features * 512, bytes_accessed=9_000_000, transcendentals=0
        ),
        name=name,
    )(core, *operands)


def pack_vectors(norm_gains, biases, offsets, rows):
    vectors = jnp.concatenate([norm_gains, biases, offsets.reshape(-1, rows)], axis=0)
    return jnp.pad(vectors, ((0, 128 - vectors.shape[0]), (0, 0))).T


def fold_rows(matrix, rows):
    folded = matrix.reshape(-1, rows, matrix.shape[-1])
    return jnp.moveaxis(folded, 0, 1).reshape(rows, -1)


def refold(columns, shards_of, features):
    rows = features // shards_of
    if rows == BLOCK:
        return columns
    natural = jnp.moveaxis(columns.reshape(shards_of, rows, -1, features), 2, 1)
    natural = natural.reshape(features // BLOCK, -1, BLOCK, features)
    return jnp.moveaxis(natural, 1, 2).reshape(features, -1)


def unfold(blocks, shards_of, features):
    rows = features // shards_of
    if rows == BLOCK:
        return blocks
    natural = jnp.moveaxis(blocks.reshape(features // BLOCK, BLOCK, -1, features), 2, 1)
    natural = natural.reshape(shards_of, -1, rows, features)
    return jnp.moveaxis(natural, 1, 2).reshape(shards_of, rows, -1)


def vector_rows(columns, shards_of):
    features = columns.shape[0]
    lines = columns[:, :8].astype(jnp.float32).T
    offsets = columns[:, 8:12].astype(jnp.float32).reshape(shards_of, features // shards_of, -1)
    return lines, jnp.moveaxis(offsets, 2, 1).reshape(1, -1)


def swapped(block, level):
    route = [(i, i ^ (1 << level)) for i in range(lax.axis_size("dp"))]
    return lax.ppermute(block, "dp", route)


def added(first, second):
    return (first.astype(jnp.float32) + second.astype(jnp.float32)).astype(jnp.bfloat16)


def halving_sum(current, first_level, levels):
    here = lax.axis_index("dp")
    current = current.reshape((2,) * (levels - first_level) + current.shape[1:])
    for level in range(first_level, levels):
        axis = levels - 1 - level
        mine = (here >> level) & 1
        send = lax.dynamic_index_in_dim(current, 1 - mine, axis, keepdims=False)
        keep = lax.dynamic_index_in_dim(current, mine, axis, keepdims=False)
        current = added(keep, swapped(send, level))
    return current


def scattered(keep, send, shards_of, features, contracted):
    levels = shards_of.bit_length() - 1
    if features == BLOCK * shards_of:
        return halving_sum(added(keep, swapped(send, 0)), 1, levels)
    blocks = jnp.stack([keep, send], axis=1).reshape(-1, BLOCK, keep.shape[-1])
    if contracted:
        blocks = unfold(blocks, shards_of, features)
    else:
        blocks = blocks.reshape(shards_of, features // shards_of, -1)
    return halving_sum(blocks, 0, levels)


def doubled(block):
    here = lax.axis_index("dp")
    for level in range(lax.axis_size("dp").bit_length() - 1):
        other = swapped(block, level)
        upper = ((here >> level) & 1) == 1
        block = jnp.concatenate(
            [jnp.where(upper, other, block), jnp.where(upper, block, other)], axis=0
        )
    return block


def shards(
    inputs,
    keep_mask,
    lengths,
    slot_order,
    cotangent,
    query_projection,
    query_output,
    query_expand,
    query_contract,
    query_gains,
    query_biases,
    query_offsets,
    momentum_projection,
    momentum_output,
    momentum_expand,
    momentum_contract,
    momentum_gains,
    momentum_biases,
    momentum_offsets,
):
    first_section = lax.axis_index("section") == 0
    shards_of = lax.axis_size("dp")
    crop_count, crop_len, features = inputs.shape[1:]
    rows = features // shards_of
    hidden_size = query_expand.shape[2]
    groups = hidden_size // features
    blocks = features // BLOCK

    own = jnp.concatenate(
        [
            query_projection[0],
            query_output[0],
            query_expand[0],
            fold_rows(query_contract[0], rows),
            pack_vectors(query_gains[0], query_biases[0], query_offsets[0], rows),
            pack_vectors(momentum_gains[0], momentum_biases[0], momentum_offsets[0], rows),
            momentum_output[0],
            momentum_projection[0, :, features : 2 * features],
        ],
        axis=1,
    )
    gathered = lax.all_gather(own, "dp", axis=0, tiled=True)
    rest = jnp.concatenate(
        [
            momentum_projection[0, :, :features],
            momentum_projection[0, :, 2 * features :],
            momentum_expand[0],
            fold_rows(momentum_contract[0], rows),
        ],
        axis=1,
    )
    rest, gathered = lax.optimization_barrier((rest, gathered))
    late = lax.all_gather(rest, "dp", axis=0, tiled=True)

    inner = 4 * features + hidden_size
    vectors_at = inner + groups * features
    query_lines, query_offs = vector_rows(gathered[:, vectors_at : vectors_at + 128], shards_of)
    momentum_lines, momentum_offs = vector_rows(
        gathered[:, vectors_at + 128 : vectors_at + 256], shards_of
    )
    if rows != BLOCK:
        gathered = jnp.concatenate(
            [
                gathered[:, :inner],
                refold(gathered[:, inner:vectors_at], shards_of, features),
                gathered[:, vectors_at:],
            ],
            axis=1,
        )
        split = 2 * features + hidden_size
        late = jnp.concatenate(
            [late[:, :split], refold(late[:, split:], shards_of, features)], axis=1
        )
    gathered = gathered.reshape(blocks, BLOCK, -1)
    late = late.reshape(blocks, BLOCK, -1)
    query_layout = (
        ("proj", 0, 0, 3 * features, 0),
        ("out", 0, 3 * features, features, 0),
        ("expand", 0, 4 * features, hidden_size, 0),
    ) + tuple(("contract", 0, inner + i * features, features, i) for i in range(groups))
    early_at = vectors_at + 256
    momentum_layout = (
        ("proj", 0, early_at + features, features, features),
        ("proj", 1, 0, features, 0),
        ("proj", 1, features, features, 2 * features),
        ("out", 0, early_at, features, 0),
        ("expand", 1, 2 * features, hidden_size, 0),
    ) + tuple(
        ("contract", 1, 2 * features + hidden_size + i * features, features, i)
        for i in range(groups)
    )

    positions = lax.broadcasted_iota(jnp.int32, keep_mask.shape, 2)
    validity = ((positions < lengths[:, :, None]) & ((keep_mask > 0) | (positions == 0))).astype(
        jnp.float32
    )
    across = validity[:, :, None, :]
    down = validity[:, :, :, None]
    in_first = first_section.astype(jnp.int32).reshape(1)
    in_second = 1 - in_first

    def query_forward(flag, block_in, crop, kept=()):
        return forward_block(
            flag,
            block_in,
            across[0, crop : crop + 1],
            down[0, crop : crop + 1],
            query_lines,
            query_offs,
            (gathered,),
            query_layout,
            True,
            kept,
        )

    def query_backward(flag, gradient, weight, saved, kept=()):
        return backward_block(
            flag, gradient, weight, query_lines, (gathered,), query_layout, saved, kept
        )

    def momentum_forward(flag, block_in):
        return forward_block(
            flag,
            block_in,
            across[1],
            down[1],
            momentum_lines,
            momentum_offs,
            (gathered, late),
            momentum_layout,
            False,
        )[:2]

    crops = range(crop_count)
    started = [query_forward(in_first, inputs[0, c : c + 1], c) for c in crops]
    passed = [lax.ppermute(started[c][0], "section", [(0, 1)]) for c in crops]
    pools, saved, pulled, returned = [], [], [], []
    for c in crops:
        _, pool, kept = query_forward(in_second, passed[c], c, started[c][2])
        pools.append(jnp.where(first_section, started[c][1], pool))
        saved.append(kept)
        pulled.append(query_backward(in_second, cotangent[c], down[0, c], kept))
        returned.append(lax.ppermute(pulled[c][0][2], "section", [(1, 0)]))
    ones = jnp.ones((crop_len, 1), jnp.float32)
    vectors, marks, terms = 0.0, 0.0, []
    for c in crops:
        ends, kept = query_backward(in_first, returned[c], ones, saved[c], pulled[c][1])
        terms.append(kept)
        vectors = vectors + jnp.where(first_section, ends[0], pulled[c][0][0])
        marks = marks + jnp.where(first_section, ends[1], pulled[c][0][1])
    grad_input = jnp.stack([term[0] for term in terms])[None]

    core = lax.axis_index("dp") & 1 if rows == BLOCK else jnp.int32(0)
    core = jnp.asarray(core, jnp.int32).reshape(1)
    block_ins = [jnp.where(first_section, inputs[0, c], passed[c][0]) for c in crops]
    contract_sums = weight_gradient(
        contract_kernel,
        core,
        [kept[6] for kept in saved] + [term[1] for term in terms],
        groups // 2,
        features,
        features,
        "grad_contract",
    )
    expand_sums = weight_gradient(
        functools.partial(
            row_kernel,
            tuple((0, 1, i * features, i // 2, i % 2 * features) for i in range(groups)),
        ),
        core,
        [kept[3] for kept in saved] + [term[2] for term in terms],
        groups // 2,
        features,
        features,
        "grad_expand",
    )
    project_sums = weight_gradient(
        functools.partial(
            row_kernel,
            (
                (0, 1, 0, 0, 0),
                (2, 3, 0, 0, features),
                (2, 3, features, 1, 0),
                (2, 3, 2 * features, 1, features),
            ),
        ),
        core,
        [kept[2] for kept in saved]
        + [term[3] for term in terms]
        + block_ins
        + [term[4] for term in terms],
        2,
        features,
        features,
        "grad_projection",
    )

    def halves(sums, contracted=False):
        return [
            scattered(sums[2 * i], sums[2 * i + 1], shards_of, features, contracted)
            for i in range(len(sums) // 2)
        ]

    contract_parts = halves(contract_sums, True)
    expand_parts = halves(expand_sums)
    project_parts = halves(project_sums)
    columns = jnp.concatenate(
        [
            vectors.T.reshape(shards_of, rows, 8),
            jnp.moveaxis(marks.reshape(shards_of, groups, rows), 1, 2),
        ],
        axis=2,
    )
    coarse = columns.astype(jnp.bfloat16)
    fine = (columns - coarse.astype(jnp.float32)).astype(jnp.bfloat16)
    both = jnp.concatenate([coarse, fine], axis=2)
    both = jnp.pad(both, ((0, 0), (0, 0), (0, 128 - both.shape[2])))
    both = halving_sum(both, 0, shards_of.bit_length() - 1).astype(jnp.float32)
    small = (both[:, :12] + both[:, 12:24]).T

    key_out, key_pool = momentum_forward(in_first, inputs[1])
    key_in = lax.ppermute(key_out, "section", [(0, 1)])
    key_pool_second = momentum_forward(in_second, key_in)[1]
    key_pool = jnp.where(first_section, key_pool, key_pool_second)
    pooled = jnp.concatenate([jnp.concatenate(pools, axis=0)[:, None], key_pool[:, None]], axis=1)
    order = (slot_order[:, None] == jnp.arange(crop_count, dtype=jnp.int32)[None, :])[..., None]
    pooled = pooled.reshape(crop_count, -1)
    pooled = jnp.sum(jnp.where(order, pooled[None], 0.0), axis=1)
    pooled = doubled(pooled).reshape(-1, 2, features)
    pooled = jnp.moveaxis(pooled, 1, 0)[None]

    def wide(parts):
        return jnp.concatenate(parts, axis=1).astype(jnp.float32)

    contract_sum = jnp.moveaxis(wide(contract_parts).reshape(rows, groups, features), 1, 0)
    project_sum = wide(project_parts)
    return (
        pooled,
        grad_input,
        project_sum[None, :, features:],
        project_sum[None, :, :features],
        wide(expand_parts)[None],
        contract_sum.reshape(1, groups * rows, features),
        small[None, :2],
        small[None, 2:8],
        small[8:].reshape(1, groups * rows),
    )


def solution(mesh):
    in_specs = (
        P(None, "dp", None, None),
        P(None, "dp", None),
        P(None, "dp"),
        P("dp"),
        P("dp", None, None),
        P("section", "dp", None),
        P("section", "dp", None),
        P("section", "dp", None),
        P("section", "dp", None),
        P("section", None, "dp"),
        P("section", None, "dp"),
        P("section", "dp"),
        P("section", "dp", None),
        P("section", "dp", None),
        P("section", "dp", None),
        P("section", "dp", None),
        P("section", None, "dp"),
        P("section", None, "dp"),
        P("section", "dp"),
    )
    out_specs = (
        P("section", None, None, None),
        P("section", "dp", None, None),
        P("section", "dp", None),
        P("section", "dp", None),
        P("section", "dp", None),
        P("section", "dp", None),
        P("section", None, "dp"),
        P("section", None, "dp"),
        P("section", "dp"),
    )
    return jax.shard_map(shards, mesh=mesh, in_specs=in_specs, out_specs=out_specs, check_vma=False)
```

```python
import functools

import jax
import jax.numpy as jnp
from jax import lax
from jax.experimental import pallas as pl
from jax.experimental.pallas import tpu as pltpu
from jax.sharding import PartitionSpec as P

HD = 64
BLOCK = 48
STRIP = 32
VMEM_LIMIT = 56 * 1024 * 1024

epsilon = 1e-12
SCALE = HD ** (-0.5)

ANY = pl.BlockSpec(memory_space=pl.ANY)
VMEM = pl.BlockSpec(memory_space=pltpu.VMEM)
SMEM = pl.BlockSpec(memory_space=pltpu.SMEM)


def dot_nn(a, b):
    return jnp.dot(a, b, preferred_element_type=jnp.float32)


def dot_nt(a, b):
    return lax.dot_general(a, b, (((1,), (1,)), ((), ())), preferred_element_type=jnp.float32)


def dot_tn(a, b):
    return lax.dot_general(a, b, (((0,), (0,)), ((), ())), preferred_element_type=jnp.float32)


def gelu_parts(values):
    size = jnp.abs(values)
    inverse = 1.0 / (1.0 + (0.3275911 * 0.5**0.5) * size)
    series = 0.5 * 1.061405429
    for factor in (-1.453152027, 1.421413741, -0.284496736, 0.254829592):
        series = series * inverse + 0.5 * factor
    bell = jnp.exp(-0.5 * (values * values))
    tail = series * inverse * bell
    phi = jnp.where(values >= 0, 1.0 - tail, tail)
    return values * phi, phi + values * bell * 0.3989422804014327


def each_strip(rows, body, carry=None):
    def step(i, held):
        return body(pl.ds(pl.multiple_of(i * STRIP, STRIP), STRIP), held)

    return lax.fori_loop(0, rows // STRIP, step, carry)


def by_eights(values):
    return jnp.sum(values.reshape(-1, 8, values.shape[-1]), axis=0)


def normalised(values):
    centred = values - jnp.mean(values, axis=-1, keepdims=True)
    variance = jnp.mean(centred * centred, axis=-1, keepdims=True)
    scale = lax.rsqrt(variance + epsilon)
    return centred * scale, scale


def weight_copies(layout, packs, buffers, sems):
    copies = {}
    for at, (name, pack, source, width, target) in enumerate(layout):
        block = packs[pack].at[:, :, pl.ds(source, width)]
        if name == "contract":
            place = buffers[name].at[:, target]
        else:
            place = buffers[name].at[:, :, pl.ds(target, width)]
        copies.setdefault(name, []).append(pltpu.make_async_copy(block, place, sems.at[at]))
    return copies


def flat(block):
    return block.reshape(-1, block.shape[-1])


def forward_kernel(layout, pack_count, view, first, crops, saved_count, kept_count, *refs):
    flag, vrow, vcol, lines, offs, x_hbm = refs[:6]
    packs = refs[6 : 6 + pack_count]
    refs = refs[6 + pack_count + kept_count :]
    y_out, pooled_out = refs[:2]
    saved = refs[2 : 2 + saved_count]
    (
        x_buf, w_proj, w_out, w_expand, w_contract, mix, probs, att, low, hat1, hat2,
        rstd1, rstd2, act, slope, wide, hidden, w_sems, io_sems,
    ) = refs[2 + saved_count :]
    rows, features = x_buf.shape
    buffers = {"proj": w_proj, "out": w_out, "expand": w_expand, "contract": w_contract}

    @pl.when(flag[0] == 1)
    def _():
        copies = weight_copies(layout, packs, buffers, w_sems)
        for name in ("proj", "out", "expand", "contract"):
            for copy in copies[name]:
                copy.start()

        def arrive(name):
            for copy in copies[name]:
                copy.wait()

        for crop in range(crops):
            source = x_hbm.at[view, first + crop] if len(x_hbm.shape) == 4 else x_hbm.at[crop]
            fetch = pltpu.make_async_copy(source, x_buf, io_sems.at[0])
            fetch.start()
            fetch.wait()
            if crop == 0:
                arrive("proj")
            for third in range(3):
                columns = pl.ds(third * features, features)
                part = dot_nn(x_buf[...], flat(w_proj[:, :, columns]))
                if third != 1:
                    part = part + lines[2 + third // 2 : 3 + third // 2, :]
                mix[:, columns] = part.astype(jnp.bfloat16)
            head_low = lax.broadcasted_iota(jnp.int32, (rows, 2 * HD), 1) < HD
            valid = jnp.broadcast_to(vrow[view, first + crop] > 0, (rows, rows))

            def pair_step(pair, _):
                at = pl.multiple_of(pair * 2 * HD, 2 * HD)
                q = mix[:, pl.ds(at, 2 * HD)]
                k = mix[:, pl.ds(at + features, 2 * HD)]
                v = mix[:, pl.ds(at + 2 * features, 2 * HD)]
                outs = []
                for side in range(2):
                    lanes = head_low if side == 0 else jnp.logical_not(head_low)
                    own = jnp.where(lanes, q.astype(jnp.float32) * SCALE, 0.0).astype(jnp.bfloat16)
                    scores = jnp.where(valid, dot_nt(own, k), -1e30)
                    top = jnp.max(scores, axis=-1, keepdims=True)
                    weights = jnp.exp(scores - top)
                    total = jnp.sum(weights, axis=-1, keepdims=True)
                    weights = (weights * (1.0 / total)).astype(jnp.bfloat16)
                    if saved_count:
                        probs[2 * pair + side] = weights
                    outs.append(dot_nn(weights, v))
                att[:, pl.ds(at, 2 * HD)] = jnp.where(head_low, outs[0], outs[1]).astype(jnp.bfloat16)

            lax.fori_loop(0, features // (2 * HD), pair_step, None)
            sends = []

            def keep(index, source):
                if saved_count:
                    copy = pltpu.make_async_copy(source, saved[index], io_sems.at[1 + index])
                    copy.start()
                    sends.append(copy)

            keep(0, mix)
            keep(1, probs)
            keep(2, att)
            if crop == 0:
                arrive("out")
            wide[...] = dot_nn(att[...], flat(w_out[...]))

            def first_norm(at, _):
                total = x_buf[at, :].astype(jnp.float32) + wide[at, :] + lines[4:5, :]
                hat, scale = normalised(total)
                value = hat * lines[0:1, :] + lines[5:6, :]
                hidden[at, :] = value
                low[at, :] = value.astype(jnp.bfloat16)
                if saved_count:
                    hat1[at, :] = hat.astype(jnp.bfloat16)
                    rstd1[at, :] = jnp.broadcast_to(scale, (STRIP, 128))

            each_strip(rows, first_norm)
            keep(3, low)
            keep(4, hat1)
            keep(5, rstd1)
            if crop == 0:
                arrive("expand")
            groups = w_expand.shape[2] // features
            ahead = None
            for group in range(groups):
                columns = pl.ds(group * features, features)
                wide[...] = dot_nn(low[...], flat(w_expand[:, :, columns]))

                def activate(at, _):
                    value, gradient = gelu_parts(wide[at, :] + offs[:, columns])
                    act[at, columns] = value.astype(jnp.bfloat16)
                    if saved_count:
                        slope[at, columns] = gradient.astype(jnp.bfloat16)

                each_strip(rows, activate)
                if crop == 0 and group == 0:
                    arrive("contract")
                stack = w_contract.shape[0] // groups
                hidden[...] += dot_nn(
                    act[:, columns], flat(w_contract[group * stack : (group + 1) * stack])
                )
            keep(6, act)
            keep(7, slope)

            def second_norm(at, held):
                hat, scale = normalised(hidden[at, :] + lines[6:7, :])
                value = hat * lines[1:2, :] + lines[7:8, :]
                y_out[crop, at, :] = value.astype(jnp.bfloat16)
                if saved_count:
                    hat2[at, :] = hat.astype(jnp.bfloat16)
                    rstd2[at, :] = jnp.broadcast_to(scale, (STRIP, 128))
                return held + by_eights(value * vcol[view, first + crop, at, :])

            total = each_strip(rows, second_norm, jnp.zeros((8, features), jnp.float32))
            count = jnp.sum(vrow[view, first + crop], axis=-1, keepdims=True)
            pooled_out[crop] = jnp.sum(total, axis=0, keepdims=True) / count
            keep(8, hat2)
            keep(9, rstd2)
            for copy in sends:
                copy.wait()


def forward_block(flag, x, vrow, vcol, lines, offs, packs, layout, save, view, first, crops, kept=()):
    rows, features = x.shape[-2:]
    hidden_size = offs.shape[-1]
    heads = features // HD
    blocks = features // BLOCK
    bf16, f32 = jnp.bfloat16, jnp.float32
    shapes = []
    if save:
        shapes = [
            ((rows, 3 * features), bf16),
            ((heads, rows, rows), bf16),
            ((rows, features), bf16),
            ((rows, features), bf16),
            ((rows, features), bf16),
            ((rows, 128), f32),
            ((rows, hidden_size), bf16),
            ((rows, hidden_size), bf16),
            ((rows, features), bf16),
            ((rows, 128), f32),
        ]
    kept = tuple(kept)
    out_shape = [
        jax.ShapeDtypeStruct((crops, rows, features), bf16),
        jax.ShapeDtypeStruct((crops, 1, features), f32),
    ] + [jax.ShapeDtypeStruct(*shape) for shape in shapes]
    flops = 2 * crops * rows * (4 * features * features + 2 * features * hidden_size)
    first_kept = 6 + len(packs)
    result = pl.pallas_call(
        functools.partial(
            forward_kernel, layout, len(packs), view, first, crops, len(shapes), len(kept)
        ),
        out_shape=out_shape,
        in_specs=[SMEM] + [VMEM] * 4 + [ANY] * (1 + len(packs) + len(kept)),
        out_specs=[VMEM, VMEM] + [ANY] * len(shapes),
        scratch_shapes=[
            pltpu.VMEM((rows, features), bf16),
            pltpu.VMEM((blocks, BLOCK, 3 * features), bf16),
            pltpu.VMEM((blocks, BLOCK, features), bf16),
            pltpu.VMEM((blocks, BLOCK, hidden_size), bf16),
            pltpu.VMEM((blocks, hidden_size // features, BLOCK, features), bf16),
            pltpu.VMEM((rows, 3 * features), bf16),
            pltpu.VMEM((heads, rows, rows) if save else (8, 128), bf16),
            pltpu.VMEM((rows, features), bf16),
            pltpu.VMEM((rows, features), bf16),
            pltpu.VMEM((rows, features), bf16),
            pltpu.VMEM((rows, features), bf16),
            pltpu.VMEM((rows, 128), f32),
            pltpu.VMEM((rows, 128), f32),
            pltpu.VMEM((rows, hidden_size), bf16),
            pltpu.VMEM((rows, hidden_size) if save else (8, 128), bf16),
            pltpu.VMEM((rows, features), f32),
            pltpu.VMEM((rows, features), f32),
            pltpu.SemaphoreType.DMA((len(layout),)),
            pltpu.SemaphoreType.DMA((11,)),
        ],
        input_output_aliases={first_kept + i: 2 + i for i in range(len(kept))},
        compiler_params=pltpu.CompilerParams(vmem_limit_bytes=VMEM_LIMIT),
        cost_estimate=pl.CostEstimate(flops=flops, bytes_accessed=20_000_000, transcendentals=0),
        name="forward_save" if save else "forward_only",
    )(flag, vrow, vcol, lines, offs, x, *packs, *kept)
    return result[0], result[1], tuple(result[2:])


def backward_kernel(layout, pack_count, crop, kept_count, *refs):
    flag, vcol, lines, g_hbm = refs[:4]
    packs = refs[4 : 4 + pack_count]
    saved = refs[4 + pack_count : 14 + pack_count]
    refs = refs[14 + pack_count + kept_count :]
    vec_out, offs_out, dx_low = refs[:3]
    dx_out, branch_out, upward_out, output_out, mixture_out = refs[3:8]
    (
        g_buf, w_proj, w_out, w_expand, w_contract, mix, probs, hat1, hat2, rstd1, rstd2, slope,
        dbranch, dupward, doutput, datt, dmix, wide, total, w_sems, in_sems, out_sems,
    ) = refs[8:]
    rows, features = g_buf.shape
    groups = w_expand.shape[2] // features
    buffers = {"proj": w_proj, "out": w_out, "expand": w_expand, "contract": w_contract}

    @pl.when(flag[0] == 1)
    def _():
        copies = weight_copies(layout, packs, buffers, w_sems)
        fetches = {}
        for at, (name, source, place) in enumerate(
            (
                ("g", g_hbm.at[crop] if len(g_hbm.shape) == 3 else g_hbm, g_buf),
                ("hat2", saved[8], hat2),
                ("rstd2", saved[9], rstd2),
                ("slope", saved[7], slope),
                ("hat1", saved[4], hat1),
                ("rstd1", saved[5], rstd1),
                ("mix", saved[0], mix),
                ("probs", saved[1], probs),
            )
        ):
            fetches[name] = [pltpu.make_async_copy(source, place, in_sems.at[at])]
        fetches.update(copies)
        for name in (
            "g", "hat2", "rstd2", "contract", "slope", "expand", "hat1", "rstd1", "out", "mix",
            "probs", "proj",
        ):
            for copy in fetches[name]:
                copy.start()

        def arrive(*names):
            for name in names:
                for copy in fetches[name]:
                    copy.wait()

        sends = []

        def send(index, source, place):
            copy = pltpu.make_async_copy(source, place, out_sems.at[index])
            copy.start()
            sends.append(copy)

        zero = jnp.zeros((8, features), jnp.float32)

        def norm_back(gradient, hat, scale, gain):
            weighted = gradient * gain
            mean = jnp.mean(weighted, axis=-1, keepdims=True)
            slant = jnp.mean(weighted * hat, axis=-1, keepdims=True)
            return scale * (weighted - mean - hat * slant)

        arrive("g", "hat2", "rstd2")

        def second_norm(at, held):
            gradient = g_buf[at, :].astype(jnp.float32)
            if len(g_hbm.shape) == 3:
                gradient = gradient * vcol[0, crop, at, :]
            hat = hat2[at, :].astype(jnp.float32)
            moved = norm_back(gradient, hat, rstd2[at, 0:1], lines[1:2, :])
            total[at, :] = moved
            rounded = moved.astype(jnp.bfloat16)
            dbranch[at, :] = rounded
            return (
                held[0] + by_eights(gradient * hat),
                held[1] + by_eights(gradient),
                held[2] + by_eights(rounded.astype(jnp.float32)),
            )

        sums = each_strip(rows, second_norm, (zero, zero, zero))
        for line, partial in zip((1, 7, 6), sums):
            vec_out[line : line + 1, :] = jnp.sum(partial, axis=0, keepdims=True)
        send(0, dbranch, branch_out)
        arrive("contract", "slope")
        stack = w_contract.shape[0] // groups
        for group in range(groups):
            columns = pl.ds(group * features, features)
            wide[...] = dot_nt(
                dbranch[...], flat(w_contract[group * stack : (group + 1) * stack])
            )

            def through(at, held):
                rounded = (wide[at, :] * slope[at, columns].astype(jnp.float32)).astype(jnp.bfloat16)
                dupward[at, columns] = rounded
                return held + by_eights(rounded.astype(jnp.float32))

            partial = each_strip(rows, through, zero)
            offs_out[:, columns] = jnp.sum(partial, axis=0, keepdims=True)
            if group == 0:
                arrive("expand")
            total[...] += dot_nt(dupward[:, columns], flat(w_expand[:, :, columns]))
        send(1, dupward, upward_out)
        arrive("hat1", "rstd1")

        def first_norm(at, held):
            gradient = total[at, :]
            hat = hat1[at, :].astype(jnp.float32)
            moved = norm_back(gradient, hat, rstd1[at, 0:1], lines[0:1, :])
            total[at, :] = moved
            rounded = moved.astype(jnp.bfloat16)
            doutput[at, :] = rounded
            return (
                held[0] + by_eights(gradient * hat),
                held[1] + by_eights(gradient),
                held[2] + by_eights(rounded.astype(jnp.float32)),
            )

        sums = each_strip(rows, first_norm, (zero, zero, zero))
        for line, partial in zip((0, 5, 4), sums):
            vec_out[line : line + 1, :] = jnp.sum(partial, axis=0, keepdims=True)
        send(2, doutput, output_out)
        arrive("out")
        datt[...] = dot_nt(doutput[...], flat(w_out[...])).astype(jnp.bfloat16)
        arrive("mix", "probs")
        head_low = lax.broadcasted_iota(jnp.int32, (rows, 2 * HD), 1) < HD

        def pair_step(pair, _):
            at = pl.multiple_of(pair * 2 * HD, 2 * HD)
            q = mix[:, pl.ds(at, 2 * HD)]
            k = mix[:, pl.ds(at + features, 2 * HD)]
            v = mix[:, pl.ds(at + 2 * features, 2 * HD)]
            pull = datt[:, pl.ds(at, 2 * HD)]
            parts = []
            for side in range(2):
                lanes = head_low if side == 0 else jnp.logical_not(head_low)
                own = jnp.where(lanes, pull, jnp.zeros_like(pull))
                weights = probs[2 * pair + side]
                dweights = dot_nt(own, v)
                wide_weights = weights.astype(jnp.float32)
                product = dweights * wide_weights
                inner = jnp.sum(product, axis=-1, keepdims=True)
                dscores = (product - wide_weights * inner).astype(jnp.bfloat16)
                parts.append((dot_nn(dscores, k), dot_tn(dscores, q), dot_tn(weights, pull)))
            for place, (first, second) in enumerate(zip(*parts)):
                merged = jnp.where(head_low, first, second)
                if place < 2:
                    merged = merged * SCALE
                dmix[:, pl.ds(at + place * features, 2 * HD)] = merged.astype(jnp.bfloat16)

        lax.fori_loop(0, features // (2 * HD), pair_step, None)
        send(3, dmix, mixture_out)

        def mixture_sums(at, held):
            return (
                held[0] + by_eights(dmix[at, 0:features].astype(jnp.float32)),
                held[1] + by_eights(dmix[at, 2 * features : 3 * features].astype(jnp.float32)),
            )

        sums = each_strip(rows, mixture_sums, (zero, zero))
        for line, partial in zip((2, 3), sums):
            vec_out[line : line + 1, :] = jnp.sum(partial, axis=0, keepdims=True)
        arrive("proj")
        for third in range(3):
            columns = pl.ds(third * features, features)
            total[...] += dot_nt(dmix[:, columns], flat(w_proj[:, :, columns]))
        dx_low[...] = total[...].astype(jnp.bfloat16)
        send(4, total, dx_out)
        for copy in sends:
            copy.wait()


def backward_block(flag, gradient, vcol, lines, packs, layout, saved, crop, kept=()):
    rows, features = gradient.shape[-2:]
    hidden_size = saved[6].shape[-1]
    heads = features // HD
    blocks = features // BLOCK
    bf16, f32 = jnp.bfloat16, jnp.float32
    kept = tuple(kept)
    out_shape = [
        jax.ShapeDtypeStruct((8, features), f32),
        jax.ShapeDtypeStruct((1, hidden_size), f32),
        jax.ShapeDtypeStruct((rows, features), bf16),
        jax.ShapeDtypeStruct((rows, features), f32),
        jax.ShapeDtypeStruct((rows, features), bf16),
        jax.ShapeDtypeStruct((rows, hidden_size), bf16),
        jax.ShapeDtypeStruct((rows, features), bf16),
        jax.ShapeDtypeStruct((rows, 3 * features), bf16),
    ]
    flops = 2 * rows * (4 * features * features + 2 * features * hidden_size)
    first_kept = 4 + len(packs) + 10
    result = pl.pallas_call(
        functools.partial(backward_kernel, layout, len(packs), crop, len(kept)),
        out_shape=out_shape,
        in_specs=[SMEM] + [VMEM] * 2 + [ANY] * (1 + len(packs) + 10 + len(kept)),
        out_specs=[VMEM] * 3 + [ANY] * 5,
        scratch_shapes=[
            pltpu.VMEM((rows, features), bf16),
            pltpu.VMEM((blocks, BLOCK, 3 * features), bf16),
            pltpu.VMEM((blocks, BLOCK, features), bf16),
            pltpu.VMEM((blocks, BLOCK, hidden_size), bf16),
            pltpu.VMEM((blocks, hidden_size // features, BLOCK, features), bf16),
            pltpu.VMEM((rows, 3 * features), bf16),
            pltpu.VMEM((heads, rows, rows), bf16),
            pltpu.VMEM((rows, features), bf16),
            pltpu.VMEM((rows, features), bf16),
            pltpu.VMEM((rows, 128), f32),
            pltpu.VMEM((rows, 128), f32),
            pltpu.VMEM((rows, hidden_size), bf16),
            pltpu.VMEM((rows, features), bf16),
            pltpu.VMEM((rows, hidden_size), bf16),
            pltpu.VMEM((rows, features), bf16),
            pltpu.VMEM((rows, features), bf16),
            pltpu.VMEM((rows, 3 * features), bf16),
            pltpu.VMEM((rows, features), f32),
            pltpu.VMEM((rows, features), f32),
            pltpu.SemaphoreType.DMA((len(layout),)),
            pltpu.SemaphoreType.DMA((8,)),
            pltpu.SemaphoreType.DMA((5,)),
        ],
        input_output_aliases={first_kept + i: 3 + i for i in range(len(kept))},
        compiler_params=pltpu.CompilerParams(vmem_limit_bytes=VMEM_LIMIT),
        cost_estimate=pl.CostEstimate(flops=flops, bytes_accessed=25_000_000, transcendentals=0),
        name="backward_data",
    )(flag, vcol, lines, gradient, *packs, *saved, *kept)
    return result[:3], tuple(result[3:])


def contract_kernel(core, act0, act1, grad0, grad1, *refs):
    outs, (piece,) = refs[:4], refs[4:]
    features = grad0.shape[1]
    groups = act0.shape[1] // features
    span = outs[0].shape[2] // features
    stack = 2 * outs[0].shape[0] // groups
    for part in range(groups):
        columns = pl.ds(part * features, features)
        piece[...] = (
            dot_tn(act0[:, columns], grad0[...]) + dot_tn(act1[:, columns], grad1[...])
        ).astype(jnp.bfloat16)
        for block in range(stack):
            place = (part * stack + block) // 2
            for group in range(groups):
                rows = pl.ds((block * groups + group) * BLOCK, BLOCK)
                at = pl.ds((group % span) * features, features)
                keep, send = outs[2 * (group // span)], outs[2 * (group // span) + 1]

                @pl.when(core[0] == block % 2)
                def _():
                    keep[place, :, at] = piece[rows, :]

                @pl.when(core[0] != block % 2)
                def _():
                    send[place, :, at] = piece[rows, :]


def row_kernel(plan, core, *refs):
    count = len({source for entry in plan for source in entry[:2]})
    sources, outs, (piece,) = refs[: 2 * count], refs[2 * count : -1], refs[-1:]
    features = piece.shape[0]
    width = piece.shape[1]
    for left, right, column, target, to in plan:
        columns = pl.ds(column, width)
        piece[...] = (
            dot_tn(sources[2 * left][...], sources[2 * right][:, columns])
            + dot_tn(sources[2 * left + 1][...], sources[2 * right + 1][:, columns])
        ).astype(jnp.bfloat16)
        keep, send = outs[2 * target], outs[2 * target + 1]
        for block in range(features // BLOCK):
            rows = pl.ds(block * BLOCK, BLOCK)

            @pl.when(core[0] == block % 2)
            def _():
                keep[block // 2, :, pl.ds(to, width)] = piece[rows, :]

            @pl.when(core[0] != block % 2)
            def _():
                send[block // 2, :, pl.ds(to, width)] = piece[rows, :]


def weight_gradient(kernel, core, operands, targets, features, width, name):
    blocks = features // BLOCK // 2
    shape = jax.ShapeDtypeStruct((blocks, BLOCK, 2 * features), jnp.bfloat16)
    return pl.pallas_call(
        kernel,
        out_shape=[shape] * (2 * targets),
        in_specs=[SMEM] + [VMEM] * len(operands),
        out_specs=[VMEM] * (2 * targets),
        scratch_shapes=[pltpu.VMEM((features, width), jnp.bfloat16)],
        compiler_params=pltpu.CompilerParams(vmem_limit_bytes=VMEM_LIMIT),
        cost_estimate=pl.CostEstimate(
            flops=4 * targets * features * features * 512, bytes_accessed=9_000_000, transcendentals=0
        ),
        name=name,
    )(core, *operands)


def pack_kernel(plan, *refs):
    sems = refs[-1]
    target = refs[-2]
    copies = []
    for at, (source, row, column, width, place) in enumerate(plan):
        block = refs[source].at[0, pl.ds(row, target.shape[0]), pl.ds(column, width)]
        copy = pltpu.make_async_copy(block, target.at[:, pl.ds(place, width)], sems.at[at])
        copy.start()
        copies.append(copy)
    for copy in copies:
        copy.wait()


def packed(arrays, pieces, rows):
    width = sum(piece[3] for piece in pieces)
    if rows % 16:
        return jnp.concatenate(
            [arrays[i][0, r : r + rows, c : c + w] for i, r, c, w in pieces], axis=1
        )
    plan, place = [], 0
    for piece in pieces:
        plan.append(piece + (place,))
        place += piece[3]
    return pl.pallas_call(
        functools.partial(pack_kernel, tuple(plan)),
        out_shape=jax.ShapeDtypeStruct((rows, width), jnp.bfloat16),
        in_specs=[ANY] * len(arrays),
        out_specs=ANY,
        scratch_shapes=[pltpu.SemaphoreType.DMA((len(plan),))],
        name="pack",
    )(*arrays)


def refold(columns, shards_of, features):
    rows = features // shards_of
    if rows == BLOCK:
        return columns
    natural = jnp.moveaxis(columns.reshape(shards_of, rows, -1, features), 2, 1)
    natural = natural.reshape(features // BLOCK, -1, BLOCK, features)
    return jnp.moveaxis(natural, 1, 2).reshape(features, -1)


def unfold(blocks, shards_of, features):
    rows = features // shards_of
    if rows == BLOCK:
        return blocks
    natural = jnp.moveaxis(blocks.reshape(features // BLOCK, BLOCK, -1, features), 2, 1)
    natural = natural.reshape(shards_of, -1, rows, features)
    return jnp.moveaxis(natural, 1, 2).reshape(shards_of, rows, -1)


def swapped(block, level):
    route = [(i, i ^ (1 << level)) for i in range(lax.axis_size("dp"))]
    return lax.ppermute(block, "dp", route)


def added(first, second):
    return (first.astype(jnp.float32) + second.astype(jnp.float32)).astype(jnp.bfloat16)


def tied(value, *others):
    return lax.optimization_barrier((value,) + others)[0]


def split(block, level):
    levels = lax.axis_size("dp").bit_length() - 1
    mine = (lax.axis_index("dp") >> level) & 1
    axis = levels - 1 - level
    keep = lax.dynamic_index_in_dim(block, mine, axis, keepdims=False)
    return keep, lax.dynamic_index_in_dim(block, 1 - mine, axis, keepdims=False)


def by_bits(block, levels):
    return block.reshape((2,) * levels + block.shape[1:])


def halved(pair, level):
    keep, send = pair
    total = added(keep, swapped(send, level))
    if level + 1 == lax.axis_size("dp").bit_length() - 1:
        return total
    return split(total, level + 1)


def first_pair(keep, send, shards_of, features, contracted):
    levels = shards_of.bit_length() - 1
    if features == BLOCK * shards_of:
        return by_bits(keep, levels - 1), by_bits(send, levels - 1)
    blocks = jnp.stack([keep, send], axis=1).reshape(-1, BLOCK, keep.shape[-1])
    if contracted:
        blocks = unfold(blocks, shards_of, features)
    else:
        blocks = blocks.reshape(shards_of, features // shards_of, -1)
    return split(by_bits(blocks, levels), 0)


def doubled(block):
    here = lax.axis_index("dp")
    for level in range(lax.axis_size("dp").bit_length() - 1):
        other = swapped(block, level)
        upper = ((here >> level) & 1) == 1
        block = jnp.concatenate(
            [jnp.where(upper, other, block), jnp.where(upper, block, other)], axis=0
        )
    return block


def shards(
    inputs,
    keep_mask,
    lengths,
    slot_order,
    cotangent,
    query_projection,
    query_output,
    query_expand,
    query_contract,
    query_gains,
    query_biases,
    query_offsets,
    momentum_projection,
    momentum_output,
    momentum_expand,
    momentum_contract,
    momentum_gains,
    momentum_biases,
    momentum_offsets,
):
    first_section = lax.axis_index("section") == 0
    shards_of = lax.axis_size("dp")
    crop_count, crop_len, features = inputs.shape[1:]
    rows = features // shards_of
    hidden_size = query_expand.shape[2]
    groups = hidden_size // features
    blocks = features // BLOCK

    def folded(which):
        return [(which, i * rows, 0, features) for i in range(groups)]

    late_from, late_to = 2 * features // 3, 2 * features
    own = packed(
        (query_projection, query_output, query_expand, query_contract)
        + (momentum_output, momentum_projection),
        [(0, 0, 0, 3 * features), (1, 0, 0, features), (2, 0, 0, hidden_size)]
        + folded(3)
        + [(4, 0, 0, features), (5, 0, late_from, late_to - late_from)],
        rows,
    )
    gathered = lax.all_gather(own, "dp", axis=0, tiled=True)
    rest = packed(
        (tied(momentum_projection, own), momentum_expand, momentum_contract),
        [(0, 0, 0, late_from), (0, 0, late_to, 3 * features - late_to), (1, 0, 0, hidden_size)]
        + folded(2),
        rows,
    )
    late = lax.all_gather(rest, "dp", axis=0, tiled=True)

    sizes = (2 * rows, 6 * rows, groups * rows)
    vectors = doubled(
        jnp.concatenate(
            [
                array[0].reshape(-1)
                for array in (
                    query_gains,
                    query_biases,
                    query_offsets,
                    momentum_gains,
                    momentum_biases,
                    momentum_offsets,
                )
            ]
        )[None]
    ).astype(jnp.float32)

    def vector_rows(start):
        lines = vectors[:, start : start + 8 * rows].reshape(shards_of, 8, rows)
        marks = vectors[:, start + 8 * rows : start + sum(sizes)]
        return jnp.moveaxis(lines, 1, 0).reshape(8, features), marks.reshape(1, hidden_size)

    query_lines, query_offs = vector_rows(0)
    momentum_lines, momentum_offs = vector_rows(sum(sizes))

    inner = 4 * features + hidden_size
    vectors_at = inner + groups * features
    if rows != BLOCK:
        gathered = jnp.concatenate(
            [
                gathered[:, :inner],
                refold(gathered[:, inner:vectors_at], shards_of, features),
                gathered[:, vectors_at:],
            ],
            axis=1,
        )
        late_end = late.shape[1] - groups * features
        late = jnp.concatenate(
            [late[:, :late_end], refold(late[:, late_end:], shards_of, features)], axis=1
        )
    gathered = gathered.reshape(blocks, BLOCK, -1)
    late = late.reshape(blocks, BLOCK, -1)
    query_layout = (
        ("proj", 0, 0, 3 * features, 0),
        ("out", 0, 3 * features, features, 0),
        ("expand", 0, 4 * features, hidden_size, 0),
    ) + tuple(("contract", 0, inner + i * features, features, i) for i in range(groups))
    late_expand = 3 * features - (late_to - late_from)
    momentum_layout = (
        ("proj", 0, vectors_at + features, late_to - late_from, late_from),
        ("proj", 1, 0, late_from, 0),
        ("proj", 1, late_from, 3 * features - late_to, late_to),
        ("out", 0, vectors_at, features, 0),
        ("expand", 1, late_expand, hidden_size, 0),
    ) + tuple(
        ("contract", 1, late_expand + hidden_size + i * features, features, i)
        for i in range(groups)
    )

    positions = lax.broadcasted_iota(jnp.int32, keep_mask.shape, 2)
    validity = ((positions < lengths[:, :, None]) & ((keep_mask > 0) | (positions == 0))).astype(
        jnp.float32
    )
    across = validity[:, :, None, :]
    down = validity[:, :, :, None]
    in_first = first_section.astype(jnp.int32).reshape(1)
    in_second = 1 - in_first

    def query_forward(flag, block_in, crop, kept=()):
        return forward_block(
            flag,
            block_in,
            across,
            down,
            query_lines,
            query_offs,
            (gathered,),
            query_layout,
            True,
            0,
            crop,
            1,
            kept,
        )

    def query_backward(flag, gradient, crop, saved, kept=()):
        return backward_block(
            flag, gradient, down, query_lines, (gathered,), query_layout, saved, crop, kept
        )

    def momentum_forward(flag, block_in):
        return forward_block(
            flag,
            block_in,
            across,
            down,
            momentum_lines,
            momentum_offs,
            (gathered, late),
            momentum_layout,
            False,
            1,
            0,
            crop_count,
        )[:2]

    crops = range(crop_count)
    started = [query_forward(in_first, inputs, c) for c in crops]
    passed = [lax.ppermute(started[c][0], "section", [(0, 1)]) for c in crops]
    pools, saved, pulled, returned = [], [], [], []
    for c in crops:
        _, pool, kept = query_forward(in_second, passed[c], c, started[c][2])
        pools.append(jnp.where(first_section, started[c][1], pool))
        saved.append(kept)
        pulled.append(query_backward(in_second, cotangent, c, kept))
        returned.append(lax.ppermute(pulled[c][0][2], "section", [(1, 0)]))
    vectors, marks, terms = 0.0, 0.0, []
    for c in crops:
        ends, kept = query_backward(in_first, returned[c], c, saved[c], pulled[c][1])
        terms.append(kept)
        vectors = vectors + jnp.where(first_section, ends[0], pulled[c][0][0])
        marks = marks + jnp.where(first_section, ends[1], pulled[c][0][1])
    grad_input = jnp.stack([term[0] for term in terms])[None]

    core = lax.axis_index("dp") & 1 if rows == BLOCK else jnp.int32(0)
    core = jnp.asarray(core, jnp.int32).reshape(1)
    block_ins = [jnp.where(first_section, inputs[0, c], passed[c][0]) for c in crops]

    def pairs(sums, contracted=False):
        return [
            first_pair(sums[2 * i], sums[2 * i + 1], shards_of, features, contracted)
            for i in range(len(sums) // 2)
        ]

    contract_pairs = pairs(
        weight_gradient(
            contract_kernel,
            core,
            [kept[6] for kept in saved] + [term[1] for term in terms],
            groups // 2,
            features,
            features,
            "grad_contract",
        ),
        True,
    )
    expand_pairs = pairs(
        weight_gradient(
            functools.partial(
                row_kernel,
                tuple((0, 1, i * features, i // 2, i % 2 * features) for i in range(groups)),
            ),
            core,
            [kept[3] for kept in saved] + [term[2] for term in terms],
            groups // 2,
            features,
            features,
            "grad_expand",
        )
    )
    contract_pairs = [halved(pair, 0) for pair in contract_pairs]
    project_pairs = pairs(
        weight_gradient(
            functools.partial(
                row_kernel,
                (
                    (0, 1, 0, 0, 0),
                    (2, 3, 0, 0, features),
                    (2, 3, features, 1, 0),
                    (2, 3, 2 * features, 1, features),
                ),
            ),
            tied(core, *[pair[1] for pair in contract_pairs]),
            [kept[2] for kept in saved]
            + [term[3] for term in terms]
            + block_ins
            + [term[4] for term in terms],
            2,
            features,
            features,
            "grad_projection",
        )
    )
    columns = jnp.concatenate(
        [
            vectors.T.reshape(shards_of, rows, 8),
            jnp.moveaxis(marks.reshape(shards_of, groups, rows), 1, 2),
        ],
        axis=2,
    )
    coarse = columns.astype(jnp.bfloat16)
    fine = (columns - coarse.astype(jnp.float32)).astype(jnp.bfloat16)
    both = jnp.concatenate([coarse, fine], axis=2)
    both = jnp.pad(both, ((0, 0), (0, 0), (0, 128 - both.shape[2])))
    levels = shards_of.bit_length() - 1
    small = split(by_bits(both, levels), 0)
    chunks = contract_pairs + [halved(pair, 0) for pair in expand_pairs + project_pairs]
    small = halved(small, 0)

    key_out, key_pool = momentum_forward(tied(in_first, *[pair[1] for pair in chunks]), inputs)
    key_in = lax.ppermute(key_out, "section", [(0, 1)])
    chunks = [halved((tied(keep, key_pool), send), 1) for keep, send in chunks]
    small = halved(small, 1)
    for level in range(2, levels):
        chunks = [halved(pair, level) for pair in chunks]
        small = halved(small, level)
    small = small.astype(jnp.float32)
    small = (small[:, :12] + small[:, 12:24]).T

    key_pool_second = momentum_forward(in_second, key_in)[1]
    key_pool = jnp.where(first_section, key_pool, key_pool_second)
    pooled = jnp.concatenate([jnp.concatenate(pools, axis=0)[:, None], key_pool[:, None]], axis=1)
    order = (slot_order[:, None] == jnp.arange(crop_count, dtype=jnp.int32)[None, :])[..., None]
    pooled = pooled.reshape(crop_count, -1)
    pooled = jnp.sum(jnp.where(order, pooled[None], 0.0), axis=1)
    pooled = doubled(pooled).reshape(-1, 2, features)
    pooled = jnp.moveaxis(pooled, 1, 0)[None]

    def wide(parts):
        return jnp.concatenate(parts, axis=1).astype(jnp.float32)

    half = groups // 2
    contract_sum = jnp.moveaxis(wide(chunks[:half]).reshape(rows, groups, features), 1, 0)
    expand_sum = wide(chunks[half : 2 * half])
    project_sum = wide(chunks[2 * half :])
    return (
        pooled,
        grad_input,
        project_sum[None, :, features:],
        project_sum[None, :, :features],
        expand_sum[None],
        contract_sum.reshape(1, groups * rows, features),
        small[None, :2],
        small[None, 2:8],
        small[8:].reshape(1, groups * rows),
    )


def solution(mesh):
    in_specs = (
        P(None, "dp", None, None),
        P(None, "dp", None),
        P(None, "dp"),
        P("dp"),
        P("dp", None, None),
        P("section", "dp", None),
        P("section", "dp", None),
        P("section", "dp", None),
        P("section", "dp", None),
        P("section", None, "dp"),
        P("section", None, "dp"),
        P("section", "dp"),
        P("section", "dp", None),
        P("section", "dp", None),
        P("section", "dp", None),
        P("section", "dp", None),
        P("section", None, "dp"),
        P("section", None, "dp"),
        P("section", "dp"),
    )
    out_specs = (
        P("section", None, None, None),
        P("section", "dp", None, None),
        P("section", "dp", None),
        P("section", "dp", None),
        P("section", "dp", None),
        P("section", "dp", None),
        P("section", None, "dp"),
        P("section", None, "dp"),
        P("section", "dp"),
    )
    return jax.shard_map(shards, mesh=mesh, in_specs=in_specs, out_specs=out_specs, check_vma=False)
```

```python
import functools

import jax
import jax.numpy as jnp
from jax import lax
from jax.experimental import pallas as pl
from jax.experimental.pallas import tpu as pltpu
from jax.sharding import PartitionSpec as P

HD = 64
BLOCK = 48
VMEM_LIMIT = 40 * 1024 * 1024

epsilon = 1e-12
SCALE = HD ** (-0.5)

ANY = pl.BlockSpec(memory_space=pl.ANY)
VMEM = pl.BlockSpec(memory_space=pltpu.VMEM)
SMEM = pl.BlockSpec(memory_space=pltpu.SMEM)
HBM = pl.BlockSpec(memory_space=pltpu.HBM)


def dot_nn(a, b):
    return jnp.dot(a, b, preferred_element_type=jnp.float32)


def dot_nt(a, b):
    return lax.dot_general(a, b, (((1,), (1,)), ((), ())), preferred_element_type=jnp.float32)


def dot_tn(a, b):
    return lax.dot_general(a, b, (((0,), (0,)), ((), ())), preferred_element_type=jnp.float32)


def gelu_parts(values):
    size = jnp.abs(values)
    inverse = 1.0 / (1.0 + (0.3275911 * 0.5**0.5) * size)
    series = 0.5 * 1.061405429
    for factor in (-1.453152027, 1.421413741, -0.284496736, 0.254829592):
        series = series * inverse + 0.5 * factor
    bell = jnp.exp(-0.5 * (values * values))
    tail = series * inverse * bell
    phi = jnp.where(values >= 0, 1.0 - tail, tail)
    return values * phi, phi + values * bell * 0.3989422804014327


def normalised(values):
    centred = values - jnp.mean(values, axis=-1, keepdims=True)
    variance = jnp.mean(centred * centred, axis=-1, keepdims=True)
    scale = lax.rsqrt(variance + epsilon)
    return centred * scale, scale


def weight_copies(layout, packs, weights, sems):
    copies = {}
    for at, (name, pack, source, width, target) in enumerate(layout):
        block = packs[pack].at[:, :, pl.ds(source, width)]
        if name == "contract":
            place = weights[name].at[:, target]
        else:
            place = weights[name].at[:, :, pl.ds(target, width)]
        copies.setdefault(name, []).append(pltpu.make_async_copy(block, place, sems.at[at]))
    return copies


NAMES = ("proj", "out", "expand", "contract")


def weight_shapes(features, hidden_size):
    blocks = features // BLOCK
    return (
        (blocks, BLOCK, 3 * features),
        (blocks, BLOCK, features),
        (blocks, BLOCK, hidden_size),
        (blocks, hidden_size // features, BLOCK, features),
    )


def in_vmem(arrays):
    return [pltpu.with_memory_space_constraint(array, pltpu.VMEM) for array in arrays]


def in_hbm(arrays):
    return [pltpu.with_memory_space_constraint(array, pltpu.HBM) for array in arrays]


def flat(block):
    return block.reshape(-1, block.shape[-1])


def two_heads(pair, head_low):
    zero = jnp.zeros_like(pair)
    return jnp.concatenate(
        [jnp.where(head_low, pair, zero), jnp.where(head_low, zero, pair)], axis=0
    )


def merged_heads(stacked, head_low):
    rows = stacked.shape[0] // 2
    return jnp.where(head_low, stacked[:rows], stacked[rows:])


def forward_kernel(layout, pack_count, view, first, crops, saved_count, kept_count, *refs):
    flag, vrow, vcol, lines, offs, x_hbm = refs[:6]
    sources = refs[6 : 6 + (pack_count or 4)]
    refs = refs[6 + (pack_count or 4) + kept_count :]
    y_out, pooled_out = refs[:2]
    refs = refs[2:]
    if pack_count:
        weights, refs = refs[:4], refs[4:]
    else:
        weights = sources
    weights = dict(zip(NAMES, weights))
    saved = refs[:saved_count]
    x_buf, mix, probs, att, low, hat1, hat2, stats, act, slope, w_sems, io_sems = refs[saved_count:]
    rows, features = x_buf.shape[1:]
    copies = {}
    if pack_count:
        copies = weight_copies(layout, sources, weights, w_sems)
        for name in NAMES:
            for copy in copies[name]:
                copy.start()

    def arrive(name):
        for copy in copies.get(name, ()):
            copy.wait()

    @pl.when(flag[0] == 1)
    def _():
        sends = []

        def keep(index, source):
            if saved_count:
                copy = pltpu.make_async_copy(source, saved[index], io_sems.at[crops + index])
                copy.start()
                sends.append(copy)

        fetches = []
        for crop in range(crops):
            source = x_hbm.at[view, first + crop] if len(x_hbm.shape) == 4 else x_hbm.at[crop]
            fetches.append(pltpu.make_async_copy(source, x_buf.at[crop], io_sems.at[crop]))
            fetches[-1].start()
        for crop in range(crops):
            fetches[crop].wait()
            x = x_buf[crop]
            if crop == 0:
                arrive("proj")
            for start, stop, line in ((0, 1, 2), (1, 2, None), (2, 3, 3)):
                columns = pl.ds(start * features, (stop - start) * features)
                part = dot_nn(x, flat(weights["proj"][:, :, columns]))
                if line is not None:
                    part = part + lines[line : line + 1, :]
                mix[:, columns] = part.astype(jnp.bfloat16)
            head_low = lax.broadcasted_iota(jnp.int32, (rows, 2 * HD), 1) < HD
            valid = jnp.broadcast_to(vrow[view, first + crop] > 0, (2 * rows, rows))
            for pair in range(features // (2 * HD)):
                at = pair * 2 * HD
                q = mix[:, at : at + 2 * HD] * jnp.asarray(SCALE, jnp.bfloat16)
                k = mix[:, features + at : features + at + 2 * HD]
                v = mix[:, 2 * features + at : 2 * features + at + 2 * HD]
                scores = jnp.where(valid, dot_nt(two_heads(q, head_low), k), -1e30)
                top = jnp.max(scores, axis=-1, keepdims=True)
                weight = jnp.exp(scores - top)
                share = 1.0 / jnp.sum(weight, axis=-1, keepdims=True)
                weight = weight.astype(jnp.bfloat16)
                if saved_count:
                    probs[2 * pair] = weight[:rows]
                    probs[2 * pair + 1] = weight[rows:]
                    stats[:, 2 + 2 * pair : 3 + 2 * pair] = share[:rows]
                    stats[:, 3 + 2 * pair : 4 + 2 * pair] = share[rows:]
                mixed = merged_heads(dot_nn(weight, v) * share, head_low)
                att[:, at : at + 2 * HD] = mixed.astype(jnp.bfloat16)
            keep(0, mix)
            keep(1, probs)
            keep(2, att)
            if crop == 0:
                arrive("out")
            total = x.astype(jnp.float32) + dot_nn(att[...], flat(weights["out"][...]))
            hat, scale = normalised(total + lines[4:5, :])
            hidden = hat * lines[0:1, :] + lines[5:6, :]
            low[...] = hidden.astype(jnp.bfloat16)
            if saved_count:
                hat1[...] = hat.astype(jnp.bfloat16)
                stats[:, 0:1] = scale
            keep(3, low)
            keep(4, hat1)
            if crop == 0:
                arrive("expand")
            groups = offs.shape[1] // features
            stack = weights["contract"].shape[0] // groups
            total = hidden + lines[6:7, :]
            for group in range(groups):
                columns = pl.ds(group * features, features)
                upward = dot_nn(low[...], flat(weights["expand"][:, :, columns]))
                value, gradient = gelu_parts(upward + offs[:, columns])
                value = value.astype(jnp.bfloat16)
                if saved_count:
                    act[:, columns] = value
                    slope[:, columns] = gradient.astype(jnp.bfloat16)
                if crop == 0 and group == 0:
                    arrive("contract")
                block = weights["contract"][group * stack : (group + 1) * stack]
                total = total + dot_nn(value, flat(block))
            keep(6, act)
            keep(7, slope)
            hat, scale = normalised(total)
            value = hat * lines[1:2, :] + lines[7:8, :]
            y_out[crop] = value.astype(jnp.bfloat16)
            if saved_count:
                hat2[...] = hat.astype(jnp.bfloat16)
                stats[:, 1:2] = scale
            count = jnp.sum(vrow[view, first + crop], axis=-1, keepdims=True)
            total = jnp.sum(value * vcol[view, first + crop], axis=0, keepdims=True)
            pooled_out[crop] = total / count
            keep(5, hat2)
            keep(8, stats)
        for copy in sends:
            copy.wait()

    if pack_count:

        @pl.when(flag[0] != 1)
        def _():
            for name in NAMES:
                arrive(name)


def forward_block(
    flag, x, vrow, vcol, lines, offs, packs, layout, save, view, first, crops, kept=()
):
    rows, features = x.shape[-2:]
    hidden_size = offs.shape[-1]
    heads = features // HD
    bf16, f32 = jnp.bfloat16, jnp.float32
    staged = bool(layout)
    shapes = []
    if staged:
        shapes = [(shape, bf16) for shape in weight_shapes(features, hidden_size)]
    first_saved = 2 + len(shapes)
    if save:
        shapes += [
            ((rows, 3 * features), bf16),
            ((heads, rows, rows), bf16),
            ((rows, features), bf16),
            ((rows, features), bf16),
            ((rows, features), bf16),
            ((rows, features), bf16),
            ((rows, hidden_size), bf16),
            ((rows, hidden_size), bf16),
            ((rows, 128), f32),
        ]
    saved_count = 9 if save else 0
    kept = tuple(kept)
    out_shape = [
        jax.ShapeDtypeStruct((crops, rows, features), bf16),
        jax.ShapeDtypeStruct((crops, 1, features), f32),
    ]
    out_shape += [pltpu.VMEM(*shape) for shape in shapes[: first_saved - 2]]
    out_shape += [pltpu.HBM(*shape) for shape in shapes[first_saved - 2 :]]
    flops = 2 * crops * rows * (4 * features * features + 2 * features * hidden_size)
    first_kept = 6 + len(packs)
    unused = (8, 128)
    result = pl.pallas_call(
        functools.partial(
            forward_kernel,
            layout,
            len(packs) if staged else 0,
            view,
            first,
            crops,
            saved_count,
            len(kept),
        ),
        out_shape=out_shape,
        in_specs=[SMEM]
        + [VMEM] * 4
        + [ANY]
        + [ANY if staged else VMEM] * len(packs)
        + [HBM] * len(kept),
        out_specs=[VMEM] * first_saved + [HBM] * saved_count,
        scratch_shapes=[
            pltpu.VMEM((crops, rows, features), bf16),
            pltpu.VMEM((rows, 3 * features), bf16),
            pltpu.VMEM((heads, rows, rows) if save else unused, bf16),
            pltpu.VMEM((rows, features), bf16),
            pltpu.VMEM((rows, features), bf16),
            pltpu.VMEM((rows, features) if save else unused, bf16),
            pltpu.VMEM((rows, features) if save else unused, bf16),
            pltpu.VMEM((rows, 128), f32),
            pltpu.VMEM((rows, hidden_size) if save else unused, bf16),
            pltpu.VMEM((rows, hidden_size) if save else unused, bf16),
            pltpu.SemaphoreType.DMA((max(1, len(layout)),)),
            pltpu.SemaphoreType.DMA((crops + 9,)),
        ],
        input_output_aliases={first_kept + i: first_saved + i for i in range(len(kept))},
        compiler_params=pltpu.CompilerParams(vmem_limit_bytes=VMEM_LIMIT),
        cost_estimate=pl.CostEstimate(flops=flops, bytes_accessed=20_000_000, transcendentals=0),
        name="forward_save" if save else "forward_only",
    )(flag, vrow, vcol, lines, offs, x, *(packs if staged else in_vmem(packs)), *in_hbm(kept))
    return result[0], result[1], tuple(result[2:first_saved]), tuple(result[first_saved:])


def backward_kernel(crop, kept_count, *refs):
    flag, vcol, lines, g_hbm = refs[:4]
    weights = dict(zip(NAMES, refs[4:8]))
    saved = refs[8:17]
    refs = refs[17 + kept_count :]
    vec_out, offs_out, dx_low = refs[:3]
    dx_out, branch_out, upward_out, output_out, mixture_out = refs[3:8]
    (
        g_buf, mix, probs, hat1, hat2, stats, slope, dbranch, dupward, doutput, datt, dmix, total,
        in_sems, out_sems,
    ) = refs[8:]
    rows, features = g_buf.shape
    hidden_size = dupward.shape[1]

    @pl.when(flag[0] == 1)
    def _():
        fetches = {}
        for at, (name, source, place) in enumerate(
            (
                ("g", g_hbm.at[crop] if len(g_hbm.shape) == 3 else g_hbm, g_buf),
                ("hat2", saved[5], hat2),
                ("stats", saved[8], stats),
                ("slope", saved[7], slope),
                ("hat1", saved[4], hat1),
                ("mix", saved[0], mix),
                ("probs", saved[1], probs),
            )
        ):
            fetches[name] = pltpu.make_async_copy(source, place, in_sems.at[at])
            fetches[name].start()

        def arrive(*names):
            for name in names:
                fetches[name].wait()

        sends = []

        def send(index, source, place):
            copy = pltpu.make_async_copy(source, place, out_sems.at[index])
            copy.start()
            sends.append(copy)

        def norm_back(gradient, hat, scale, gain):
            weighted = gradient * gain
            mean = jnp.mean(weighted, axis=-1, keepdims=True)
            slant = jnp.mean(weighted * hat, axis=-1, keepdims=True)
            return scale * (weighted - mean - hat * slant)

        def column_sum(line, values):
            vec_out[line : line + 1, :] = jnp.sum(values, axis=0, keepdims=True)

        arrive("g", "hat2", "stats")
        gradient = g_buf[...].astype(jnp.float32)
        if len(g_hbm.shape) == 3:
            gradient = gradient * vcol[0, crop]
        hat = hat2[...].astype(jnp.float32)
        column_sum(1, gradient * hat)
        column_sum(7, gradient)
        moved = norm_back(gradient, hat, stats[:, 1:2], lines[1:2, :])
        total[...] = moved
        rounded = moved.astype(jnp.bfloat16)
        dbranch[...] = rounded
        column_sum(6, rounded.astype(jnp.float32))
        send(0, dbranch, branch_out)
        arrive("slope")
        groups = hidden_size // features
        stack = weights["contract"].shape[0] // groups
        for group in range(groups):
            columns = pl.ds(group * features, features)
            block = weights["contract"][group * stack : (group + 1) * stack]
            dactive = dot_nt(rounded, flat(block))
            dup = (dactive * slope[:, columns].astype(jnp.float32)).astype(jnp.bfloat16)
            dupward[:, columns] = dup
            offs_out[:, columns] = jnp.sum(dup.astype(jnp.float32), axis=0, keepdims=True)
        send(1, dupward, upward_out)
        arrive("hat1")
        gradient = total[...] + dot_nt(dupward[...], flat(weights["expand"][...]))
        hat = hat1[...].astype(jnp.float32)
        column_sum(0, gradient * hat)
        column_sum(5, gradient)
        moved = norm_back(gradient, hat, stats[:, 0:1], lines[0:1, :])
        total[...] = moved
        rounded = moved.astype(jnp.bfloat16)
        doutput[...] = rounded
        column_sum(4, rounded.astype(jnp.float32))
        send(2, doutput, output_out)
        datt[...] = dot_nt(rounded, flat(weights["out"][...])).astype(jnp.bfloat16)
        arrive("mix", "probs")
        head_low = lax.broadcasted_iota(jnp.int32, (rows, 2 * HD), 1) < HD
        for pair in range(features // (2 * HD)):
            at = pair * 2 * HD
            q = mix[:, at : at + 2 * HD]
            k = mix[:, features + at : features + at + 2 * HD]
            v = mix[:, 2 * features + at : 2 * features + at + 2 * HD]
            share = jnp.concatenate(
                [stats[:, 2 + 2 * pair : 3 + 2 * pair], stats[:, 3 + 2 * pair : 4 + 2 * pair]], axis=0
            )
            pull = two_heads(datt[:, at : at + 2 * HD], head_low).astype(jnp.float32)
            pull = (pull * share).astype(jnp.bfloat16)
            weight = flat(probs[2 * pair : 2 * pair + 2])
            wide = weight.astype(jnp.float32)
            product = dot_nt(pull, v) * wide
            inner = jnp.sum(product, axis=-1, keepdims=True) * share
            dscores = (product - wide * inner).astype(jnp.bfloat16)
            dq = merged_heads(dot_nn(dscores, k), head_low)
            dmix[:, at : at + 2 * HD] = (dq * SCALE).astype(jnp.bfloat16)
            q_turned = q.T
            pull_turned = merged_heads(pull, head_low).T
            dk, dv = [], []
            for side in range(2):
                lanes = slice(side * HD, (side + 1) * HD)
                part = slice(side * rows, (side + 1) * rows)
                dk.append(dot_nn(q_turned[lanes], dscores[part]))
                dv.append(dot_nn(pull_turned[lanes], weight[part]))
            dk = (jnp.concatenate(dk, axis=0) * SCALE).astype(jnp.bfloat16).T
            dv = jnp.concatenate(dv, axis=0).astype(jnp.bfloat16).T
            dmix[:, features + at : features + at + 2 * HD] = dk
            dmix[:, 2 * features + at : 2 * features + at + 2 * HD] = dv
        send(3, dmix, mixture_out)
        column_sum(2, dmix[:, 0:features].astype(jnp.float32))
        column_sum(3, dmix[:, 2 * features : 3 * features].astype(jnp.float32))
        moved = total[...] + dot_nt(dmix[...], flat(weights["proj"][...]))
        total[...] = moved
        dx_low[...] = moved.astype(jnp.bfloat16)
        send(4, total, dx_out)
        for copy in sends:
            copy.wait()


def backward_block(flag, gradient, vcol, lines, weights, saved, crop, kept=()):
    rows, features = gradient.shape[-2:]
    hidden_size = saved[6].shape[-1]
    heads = features // HD
    bf16, f32 = jnp.bfloat16, jnp.float32
    kept = tuple(kept)
    out_shape = [
        jax.ShapeDtypeStruct((8, features), f32),
        jax.ShapeDtypeStruct((1, hidden_size), f32),
        jax.ShapeDtypeStruct((rows, features), bf16),
        pltpu.HBM((rows, features), f32),
        pltpu.HBM((rows, features), bf16),
        pltpu.HBM((rows, hidden_size), bf16),
        pltpu.HBM((rows, features), bf16),
        pltpu.HBM((rows, 3 * features), bf16),
    ]
    flops = 2 * rows * (4 * features * features + 2 * features * hidden_size)
    first_kept = 8 + 9
    result = pl.pallas_call(
        functools.partial(backward_kernel, crop, len(kept)),
        out_shape=out_shape,
        in_specs=[SMEM] + [VMEM] * 2 + [ANY] + [VMEM] * 4 + [HBM] * (9 + len(kept)),
        out_specs=[VMEM] * 3 + [HBM] * 5,
        scratch_shapes=[
            pltpu.VMEM((rows, features), bf16),
            pltpu.VMEM((rows, 3 * features), bf16),
            pltpu.VMEM((heads, rows, rows), bf16),
            pltpu.VMEM((rows, features), bf16),
            pltpu.VMEM((rows, features), bf16),
            pltpu.VMEM((rows, 128), f32),
            pltpu.VMEM((rows, hidden_size), bf16),
            pltpu.VMEM((rows, features), bf16),
            pltpu.VMEM((rows, hidden_size), bf16),
            pltpu.VMEM((rows, features), bf16),
            pltpu.VMEM((rows, features), bf16),
            pltpu.VMEM((rows, 3 * features), bf16),
            pltpu.VMEM((rows, features), f32),
            pltpu.SemaphoreType.DMA((7,)),
            pltpu.SemaphoreType.DMA((5,)),
        ],
        input_output_aliases={first_kept + i: 3 + i for i in range(len(kept))},
        compiler_params=pltpu.CompilerParams(vmem_limit_bytes=VMEM_LIMIT),
        cost_estimate=pl.CostEstimate(flops=flops, bytes_accessed=25_000_000, transcendentals=0),
        name="backward_data",
    )(flag, vcol, lines, gradient, *in_vmem(weights), *in_hbm(saved), *in_hbm(kept))
    return result[:3], tuple(result[3:])


def load_pairs(sources, buffers, width, sems):
    copies = {}
    for i, buffer in enumerate(buffers):
        rows = buffer.shape[0] // 2
        for column in range(0, buffer.shape[1], width):
            columns = pl.ds(column, width)
            for half in range(2):
                copies.setdefault((i, column), []).append(
                    pltpu.make_async_copy(
                        sources[2 * i + half].at[:, columns],
                        buffer.at[pl.ds(half * rows, rows), columns],
                        sems.at[2 * i + half, column // width],
                    )
                )
    waited = set()

    def arrive(which, column):
        if (which, column) not in waited:
            waited.add((which, column))
            for copy in copies[which, column]:
                copy.wait()

    return copies, arrive


def contract_kernel(core, act0, act1, grad0, grad1, *refs):
    outs, (act, grad, pieces, in_sems, out_sems) = refs[:-5], refs[-5:]
    features = grad.shape[1]
    groups = act.shape[1] // features
    span = outs[0].shape[2] // features
    copies, arrive = load_pairs((act0, act1, grad0, grad1), (act, grad), features, in_sems)
    for which in [(1, 0)] + [(0, part * features) for part in range(groups)]:
        for copy in copies[which]:
            copy.start()
    arrive(1, 0)
    sends = []
    for part in range(groups):
        columns = pl.ds(part * features, features)
        arrive(0, part * features)
        piece = dot_tn(act[:, columns], grad[...]).astype(jnp.bfloat16)
        pieces[part] = piece.reshape(pieces.shape[1:])
        count = pieces.shape[1]
        for group in range(groups):
            for side in range(2):
                source = pieces.at[part, :, core[0] ^ side, group]
                place = outs[2 * (group // span) + side].at[
                    pl.ds(part * count, count), :, pl.ds((group % span) * features, features)
                ]
                copy = pltpu.make_async_copy(source, place, out_sems.at[part, group, side])
                copy.start()
                sends.append(copy)
    for copy in sends:
        copy.wait()


def row_kernel(plan, core, *refs):
    count = 1 + max(max(entry[:2]) for entry in plan)
    sources, refs = refs[: 2 * count], refs[2 * count :]
    buffers, (pieces, in_sems, out_sems) = refs[-3 - count : -3], refs[-3:]
    outs = refs[: -3 - count]
    width = pieces.shape[-1]
    copies, arrive = load_pairs(sources, buffers, width, in_sems)
    needs = [need for entry in plan for need in ((entry[0], 0), (entry[1], entry[2]))]
    for need in dict.fromkeys(needs):
        for copy in copies[need]:
            copy.start()
    sends = []
    for part, (left, right, column, target, to) in enumerate(plan):
        arrive(left, 0)
        arrive(right, column)
        piece = dot_tn(buffers[left][...], buffers[right][:, column : column + width])
        pieces[part] = piece.astype(jnp.bfloat16).reshape(pieces.shape[1:])
        for side in range(2):
            source = pieces.at[part, :, core[0] ^ side]
            place = outs[2 * target + side].at[:, :, pl.ds(to, width)]
            copy = pltpu.make_async_copy(source, place, out_sems.at[part, side])
            copy.start()
            sends.append(copy)
    for copy in sends:
        copy.wait()


def weight_gradient(kernel, core, operands, targets, contracted, features, name):
    pairs = features // BLOCK // 2
    bf16 = jnp.bfloat16
    shape = pltpu.HBM((pairs, BLOCK, 2 * features), bf16)
    parts = 2 * targets
    buffers = [
        pltpu.VMEM((2 * operand.shape[0], operand.shape[1]), bf16) for operand in operands[::2]
    ]
    if contracted:
        pieces = pltpu.VMEM((parts, pairs // parts, 2, parts, BLOCK, features), bf16)
        out_sems = pltpu.SemaphoreType.DMA((parts, parts, 2))
    else:
        pieces = pltpu.VMEM((parts, pairs, 2, BLOCK, features), bf16)
        out_sems = pltpu.SemaphoreType.DMA((parts, 2))
    return pl.pallas_call(
        kernel,
        out_shape=[shape] * (2 * targets),
        in_specs=[SMEM] + [HBM] * len(operands),
        out_specs=[HBM] * (2 * targets),
        scratch_shapes=buffers
        + [pieces, pltpu.SemaphoreType.DMA((len(operands), parts)), out_sems],
        compiler_params=pltpu.CompilerParams(vmem_limit_bytes=VMEM_LIMIT),
        cost_estimate=pl.CostEstimate(
            flops=4 * targets * features * features * 512, bytes_accessed=9_000_000, transcendentals=0
        ),
        name=name,
    )(core, *in_hbm(operands))


def pack_kernel(plan, *refs):
    target = refs[-1]
    for source, row, column, width, place in plan:
        block = refs[source][0, row : row + target.shape[0], column : column + width]
        target[:, place : place + width] = block


def packed(arrays, pieces, rows):
    width = sum(piece[3] for piece in pieces)
    if rows % 16:
        return jnp.concatenate(
            [arrays[i][0, r : r + rows, c : c + w] for i, r, c, w in pieces], axis=1
        )
    plan, place = [], 0
    for piece in pieces:
        plan.append(piece + (place,))
        place += piece[3]
    return pl.pallas_call(
        functools.partial(pack_kernel, tuple(plan)),
        out_shape=jax.ShapeDtypeStruct((rows, width), jnp.bfloat16),
        in_specs=[VMEM] * len(arrays),
        out_specs=VMEM,
        name="pack",
    )(*arrays)


def refold(columns, shards_of, features):
    rows = features // shards_of
    if rows == BLOCK:
        return columns
    natural = jnp.moveaxis(columns.reshape(shards_of, rows, -1, features), 2, 1)
    natural = natural.reshape(features // BLOCK, -1, BLOCK, features)
    return jnp.moveaxis(natural, 1, 2).reshape(features, -1)


def unfold(blocks, shards_of, features):
    rows = features // shards_of
    if rows == BLOCK:
        return blocks
    natural = jnp.moveaxis(blocks.reshape(features // BLOCK, BLOCK, -1, features), 2, 1)
    natural = natural.reshape(shards_of, -1, rows, features)
    return jnp.moveaxis(natural, 1, 2).reshape(shards_of, rows, -1)


def swapped(block, level):
    route = [(i, i ^ (1 << level)) for i in range(lax.axis_size("dp"))]
    return lax.ppermute(block, "dp", route)


def added(first, second):
    return (first.astype(jnp.float32) + second.astype(jnp.float32)).astype(jnp.bfloat16)


def tied(value, *others):
    return lax.optimization_barrier((value,) + others)[0]


def split(block, level):
    levels = lax.axis_size("dp").bit_length() - 1
    mine = (lax.axis_index("dp") >> level) & 1
    axis = levels - 1 - level
    keep = lax.dynamic_index_in_dim(block, mine, axis, keepdims=False)
    return keep, lax.dynamic_index_in_dim(block, 1 - mine, axis, keepdims=False)


def by_bits(block, levels):
    return block.reshape((2,) * levels + block.shape[1:])


def halved(pair, level):
    keep, send = pair
    total = added(keep, swapped(send, level))
    if level + 1 == lax.axis_size("dp").bit_length() - 1:
        return total
    return split(total, level + 1)


def first_pair(keep, send, shards_of, features, contracted):
    levels = shards_of.bit_length() - 1
    if features == BLOCK * shards_of:
        return by_bits(keep, levels - 1), by_bits(send, levels - 1)
    blocks = jnp.stack([keep, send], axis=1).reshape(-1, BLOCK, keep.shape[-1])
    if contracted:
        blocks = unfold(blocks, shards_of, features)
    else:
        blocks = blocks.reshape(shards_of, features // shards_of, -1)
    return split(by_bits(blocks, levels), 0)


def doubled(block):
    here = lax.axis_index("dp")
    for level in range(lax.axis_size("dp").bit_length() - 1):
        other = swapped(block, level)
        upper = ((here >> level) & 1) == 1
        block = jnp.concatenate(
            [jnp.where(upper, other, block), jnp.where(upper, block, other)], axis=0
        )
    return block


def shards(
    inputs,
    keep_mask,
    lengths,
    slot_order,
    cotangent,
    query_projection,
    query_output,
    query_expand,
    query_contract,
    query_gains,
    query_biases,
    query_offsets,
    momentum_projection,
    momentum_output,
    momentum_expand,
    momentum_contract,
    momentum_gains,
    momentum_biases,
    momentum_offsets,
):
    first_section = lax.axis_index("section") == 0
    shards_of = lax.axis_size("dp")
    crop_count, crop_len, features = inputs.shape[1:]
    rows = features // shards_of
    hidden_size = query_expand.shape[2]
    groups = hidden_size // features
    blocks = features // BLOCK

    def folded(which):
        return [(which, i * rows, 0, features) for i in range(groups)]

    late_from, late_to = 2 * features // 3, 2 * features
    own = packed(
        (query_projection, query_output, query_expand, query_contract)
        + (momentum_output, momentum_projection),
        [(0, 0, 0, 3 * features), (1, 0, 0, features), (2, 0, 0, hidden_size)]
        + folded(3)
        + [(4, 0, 0, features), (5, 0, late_from, late_to - late_from)],
        rows,
    )
    gathered = lax.all_gather(own, "dp", axis=0, tiled=True)
    rest = packed(
        (tied(momentum_projection, own), momentum_expand, momentum_contract),
        [(0, 0, 0, late_from), (0, 0, late_to, 3 * features - late_to), (1, 0, 0, hidden_size)]
        + folded(2),
        rows,
    )
    late = lax.all_gather(rest, "dp", axis=0, tiled=True)

    sizes = (2 * rows, 6 * rows, groups * rows)
    vectors = doubled(
        jnp.concatenate(
            [
                array[0].reshape(-1)
                for array in (
                    query_gains,
                    query_biases,
                    query_offsets,
                    momentum_gains,
                    momentum_biases,
                    momentum_offsets,
                )
            ]
        )[None]
    ).astype(jnp.float32)

    def vector_rows(start):
        lines = vectors[:, start : start + 8 * rows].reshape(shards_of, 8, rows)
        marks = vectors[:, start + 8 * rows : start + sum(sizes)]
        return jnp.moveaxis(lines, 1, 0).reshape(8, features), marks.reshape(1, hidden_size)

    query_lines, query_offs = vector_rows(0)
    momentum_lines, momentum_offs = vector_rows(sum(sizes))

    inner = 4 * features + hidden_size
    vectors_at = inner + groups * features
    if rows != BLOCK:
        gathered = jnp.concatenate(
            [
                gathered[:, :inner],
                refold(gathered[:, inner:vectors_at], shards_of, features),
                gathered[:, vectors_at:],
            ],
            axis=1,
        )
        late_end = late.shape[1] - groups * features
        late = jnp.concatenate(
            [late[:, :late_end], refold(late[:, late_end:], shards_of, features)], axis=1
        )
    gathered = gathered.reshape(blocks, BLOCK, -1)
    late = late.reshape(blocks, BLOCK, -1)
    query_layout = (
        ("proj", 0, 0, 3 * features, 0),
        ("out", 0, 3 * features, features, 0),
        ("expand", 0, 4 * features, hidden_size, 0),
    ) + tuple(("contract", 0, inner + i * features, features, i) for i in range(groups))
    late_expand = 3 * features - (late_to - late_from)
    momentum_layout = (
        ("proj", 0, vectors_at + features, late_to - late_from, late_from),
        ("proj", 1, 0, late_from, 0),
        ("proj", 1, late_from, 3 * features - late_to, late_to),
        ("out", 0, vectors_at, features, 0),
        ("expand", 1, late_expand, hidden_size, 0),
    ) + tuple(
        ("contract", 1, late_expand + hidden_size + i * features, features, i)
        for i in range(groups)
    )

    positions = lax.broadcasted_iota(jnp.int32, keep_mask.shape, 2)
    validity = ((positions < lengths[:, :, None]) & ((keep_mask > 0) | (positions == 0))).astype(
        jnp.float32
    )
    across = validity[:, :, None, :]
    down = validity[:, :, :, None]
    in_first = first_section.astype(jnp.int32).reshape(1)
    in_second = 1 - in_first

    def query_forward(flag, block_in, crop, weights, layout=(), kept=()):
        return forward_block(
            flag,
            block_in,
            across,
            down,
            query_lines,
            query_offs,
            weights,
            layout,
            True,
            0,
            crop,
            1,
            kept,
        )

    def momentum_forward(flag, block_in, weights, layout=()):
        return forward_block(
            flag,
            block_in,
            across,
            down,
            momentum_lines,
            momentum_offs,
            weights,
            layout,
            False,
            1,
            0,
            crop_count,
        )[:3]

    crops = range(crop_count)
    started = [query_forward(in_first, inputs, 0, (gathered,), query_layout)]
    weights = started[0][2]
    started += [query_forward(in_first, inputs, c, weights) for c in crops[1:]]
    passed = [lax.ppermute(started[c][0], "section", [(0, 1)]) for c in crops]
    pools, saved, pulled, returned = [], [], [], []
    for c in crops:
        _, pool, _, kept = query_forward(
            in_second, passed[c], c, weights, (), started[c][3]
        )
        pools.append(jnp.where(first_section, started[c][1], pool))
        saved.append(kept)
        pulled.append(backward_block(in_second, cotangent, down, query_lines, weights, kept, c))
        returned.append(lax.ppermute(pulled[c][0][2], "section", [(1, 0)]))
    vectors, marks, terms = 0.0, 0.0, []
    for c in crops:
        ends, kept = backward_block(
            in_first, returned[c], down, query_lines, weights, saved[c], c, pulled[c][1]
        )
        terms.append(kept)
        vectors = vectors + jnp.where(first_section, ends[0], pulled[c][0][0])
        marks = marks + jnp.where(first_section, ends[1], pulled[c][0][1])
    grad_input = jnp.stack([term[0] for term in terms])[None]

    core = lax.axis_index("dp") & 1 if rows == BLOCK else jnp.int32(0)
    core = jnp.asarray(core, jnp.int32).reshape(1)
    block_ins = [jnp.where(first_section, inputs[0, c], passed[c][0]) for c in crops]

    def pairs(sums, contracted=False):
        return [
            first_pair(sums[2 * i], sums[2 * i + 1], shards_of, features, contracted)
            for i in range(len(sums) // 2)
        ]

    contract_pairs = pairs(
        weight_gradient(
            contract_kernel,
            core,
            [kept[6] for kept in saved] + [term[1] for term in terms],
            groups // 2,
            True,
            features,
            "grad_contract",
        ),
        True,
    )
    expand_pairs = pairs(
        weight_gradient(
            functools.partial(
                row_kernel,
                tuple((0, 1, i * features, i // 2, i % 2 * features) for i in range(groups)),
            ),
            core,
            [kept[3] for kept in saved] + [term[2] for term in terms],
            groups // 2,
            False,
            features,
            "grad_expand",
        )
    )
    contract_pairs = [halved(pair, 0) for pair in contract_pairs]
    project_pairs = pairs(
        weight_gradient(
            functools.partial(
                row_kernel,
                (
                    (0, 1, 0, 0, 0),
                    (2, 3, 0, 0, features),
                    (2, 3, features, 1, 0),
                    (2, 3, 2 * features, 1, features),
                ),
            ),
            tied(core, *[pair[1] for pair in contract_pairs]),
            [kept[2] for kept in saved]
            + [term[3] for term in terms]
            + block_ins
            + [term[4] for term in terms],
            2,
            False,
            features,
            "grad_projection",
        )
    )
    columns = jnp.concatenate(
        [
            vectors.T.reshape(shards_of, rows, 8),
            jnp.moveaxis(marks.reshape(shards_of, groups, rows), 1, 2),
        ],
        axis=2,
    )
    coarse = columns.astype(jnp.bfloat16)
    fine = (columns - coarse.astype(jnp.float32)).astype(jnp.bfloat16)
    both = jnp.concatenate([coarse, fine], axis=2)
    both = jnp.pad(both, ((0, 0), (0, 0), (0, 128 - both.shape[2])))
    levels = shards_of.bit_length() - 1
    small = split(by_bits(both, levels), 0)
    chunks = contract_pairs + [halved(pair, 0) for pair in expand_pairs + project_pairs]
    small = halved(small, 0)

    key_out, key_pool, key_weights = momentum_forward(
        tied(in_first, *[pair[1] for pair in chunks]), inputs, (gathered, late), momentum_layout
    )
    key_in = lax.ppermute(key_out, "section", [(0, 1)])
    chunks = [halved((tied(keep, key_pool), send), 1) for keep, send in chunks]
    small = halved(small, 1)
    for level in range(2, levels):
        chunks = [halved(pair, level) for pair in chunks]
        small = halved(small, level)
    small = small.astype(jnp.float32)
    small = (small[:, :12] + small[:, 12:24]).T

    key_pool_second = momentum_forward(in_second, key_in, key_weights)[1]
    key_pool = jnp.where(first_section, key_pool, key_pool_second)
    pooled = jnp.concatenate([jnp.concatenate(pools, axis=0)[:, None], key_pool[:, None]], axis=1)
    order = (slot_order[:, None] == jnp.arange(crop_count, dtype=jnp.int32)[None, :])[..., None]
    pooled = pooled.reshape(crop_count, -1)
    pooled = jnp.sum(jnp.where(order, pooled[None], 0.0), axis=1)
    pooled = doubled(pooled).reshape(-1, 2, features)
    pooled = jnp.moveaxis(pooled, 1, 0)[None]

    def wide(parts):
        return jnp.concatenate(parts, axis=1).astype(jnp.float32)

    half = groups // 2
    contract_sum = jnp.moveaxis(wide(chunks[:half]).reshape(rows, groups, features), 1, 0)
    expand_sum = wide(chunks[half : 2 * half])
    project_sum = wide(chunks[2 * half :])
    return (
        pooled,
        grad_input,
        project_sum[None, :, features:],
        project_sum[None, :, :features],
        expand_sum[None],
        contract_sum.reshape(1, groups * rows, features),
        small[None, :2],
        small[None, 2:8],
        small[8:].reshape(1, groups * rows),
    )


def solution(mesh):
    in_specs = (
        P(None, "dp", None, None),
        P(None, "dp", None),
        P(None, "dp"),
        P("dp"),
        P("dp", None, None),
        P("section", "dp", None),
        P("section", "dp", None),
        P("section", "dp", None),
        P("section", "dp", None),
        P("section", None, "dp"),
        P("section", None, "dp"),
        P("section", "dp"),
        P("section", "dp", None),
        P("section", "dp", None),
        P("section", "dp", None),
        P("section", "dp", None),
        P("section", None, "dp"),
        P("section", None, "dp"),
        P("section", "dp"),
    )
    out_specs = (
        P("section", None, None, None),
        P("section", "dp", None, None),
        P("section", "dp", None),
        P("section", "dp", None),
        P("section", "dp", None),
        P("section", "dp", None),
        P("section", None, "dp"),
        P("section", None, "dp"),
        P("section", "dp"),
    )
    return jax.shard_map(shards, mesh=mesh, in_specs=in_specs, out_specs=out_specs, check_vma=False)
```

```python
import functools

import jax
import jax.numpy as jnp
from jax import lax
from jax.experimental import pallas as pl
from jax.experimental.pallas import tpu as pltpu
from jax.sharding import PartitionSpec as P

DP, SECTION = "dp", "section"
HD = 64
BLOCK = 48
VMEM_LIMIT = 56 * 1024 * 1024

epsilon = 1e-12
SCALE = HD ** (-0.5)

ANY = pl.BlockSpec(memory_space=pl.ANY)
VMEM = pl.BlockSpec(memory_space=pltpu.VMEM)
SMEM = pl.BlockSpec(memory_space=pltpu.SMEM)


def dot_nn(a, b):
    return jnp.dot(a, b, preferred_element_type=jnp.float32)


def dot_nt(a, b):
    return lax.dot_general(a, b, (((1,), (1,)), ((), ())), preferred_element_type=jnp.float32)


def dot_tn(a, b):
    return lax.dot_general(a, b, (((0,), (0,)), ((), ())), preferred_element_type=jnp.float32)


def gelu_parts(values):
    size = jnp.abs(values)
    inverse = 1.0 / (1.0 + (0.3275911 * 0.5**0.5) * size)
    series = 0.5 * 1.061405429
    for factor in (-1.453152027, 1.421413741, -0.284496736, 0.254829592):
        series = series * inverse + 0.5 * factor
    bell = jnp.exp(-0.5 * (values * values))
    tail = series * inverse * bell
    phi = jnp.where(values >= 0, 1.0 - tail, tail)
    return values * phi, phi + values * bell * 0.3989422804014327


def normalised(values):
    centred = values - jnp.mean(values, axis=-1, keepdims=True)
    variance = jnp.mean(centred * centred, axis=-1, keepdims=True)
    scale = lax.rsqrt(variance + epsilon)
    return centred * scale, scale


(
    PROJ,
    OUT,
    EXPAND,
    CONTRACT,
    MIX,
    PROBS,
    HAT1,
    HAT2,
    SLOPE,
    STATS,
    ATT,
    LOW,
    ACT,
    TOTAL,
    DBRANCH,
    DUPWARD,
    DOUTPUT,
    DMIX,
    DATT,
    X_IN,
    G_IN,
) = range(21)
NAMES = (PROJ, OUT, EXPAND, CONTRACT)
SAVED = (MIX, PROBS, HAT1, HAT2, SLOPE, STATS, ATT, LOW, ACT)
UNROLL = 3
TERMS = (TOTAL, DBRANCH, DUPWARD, DOUTPUT, DMIX)


def flat(block):
    return block.reshape(-1, block.shape[-1])


def shape_of(name, rows, features, hidden_size):
    blocks = features // BLOCK
    bf16, f32 = jnp.bfloat16, jnp.float32
    return {
        PROJ: ((blocks, BLOCK, 3 * features), bf16),
        OUT: ((blocks, BLOCK, features), bf16),
        EXPAND: ((blocks, BLOCK, hidden_size), bf16),
        CONTRACT: ((blocks, hidden_size // features, BLOCK, features), bf16),
        MIX: ((rows, 3 * features), bf16),
        PROBS: ((features // HD, rows, rows), bf16),
        STATS: ((rows, 128), f32),
        ACT: ((rows, hidden_size), bf16),
        SLOPE: ((rows, hidden_size), bf16),
        DUPWARD: ((rows, hidden_size), bf16),
        DMIX: ((rows, 3 * features), bf16),
        TOTAL: ((rows, features), f32),
    }.get(name, ((rows, features), bf16))


def scratch_of(names, *sizes):
    return [pltpu.VMEM(*shape_of(name, *sizes)) for name in names]


def outputs_of(names, *sizes):
    return [jax.ShapeDtypeStruct(*shape_of(name, *sizes)) for name in names]


class Copier:
    def __init__(self, sems):
        self.sems, self.count, self.open = sems, 0, []

    def fetch(self, source, place):
        copy = pltpu.make_async_copy(source, place, self.sems.at[self.count])
        self.count += 1
        copy.start()
        return copy

    def send(self, source, place):
        self.open.append(self.fetch(source, place))

    def finish(self):
        for copy in self.open:
            copy.wait()


class Held:
    def __init__(self, names, buffers, copier):
        self.buffers, self.pending, self.copier = dict(zip(names, buffers)), {}, copier

    def fill(self, name, source):
        self.pending[name] = [self.copier.fetch(source, self.buffers[name])]

    def fill_weight(self, wanted, layout, packs):
        buffer = self.buffers[wanted]
        for name, pack, source, width, target in layout:
            if name == wanted:
                block = packs[pack].at[:, :, pl.ds(source, width)]
                if name == CONTRACT:
                    place = buffer.at[:, target]
                else:
                    place = buffer.at[:, :, pl.ds(target, width)]
                self.pending.setdefault(name, []).append(self.copier.fetch(block, place))

    def __contains__(self, name):
        return name in self.buffers

    def __getitem__(self, name):
        for copy in self.pending.pop(name, ()):
            copy.wait()
        return self.buffers[name]


def two_heads(pair, head_low):
    zero = jnp.zeros_like(pair)
    return jnp.concatenate(
        [jnp.where(head_low, pair, zero), jnp.where(head_low, zero, pair)], axis=0
    )


def merged_heads(stacked, head_low):
    rows = stacked.shape[0] // 2
    return jnp.where(head_low, stacked[:rows], stacked[rows:])


def low_lanes(rows):
    return lax.broadcasted_iota(jnp.int32, (rows, 2 * HD), 1) < HD


def forward_rows(x, validity, lines, offs, held, done):
    rows, features = x.shape
    saving = PROBS in held
    mix, att, low = held[MIX], held[ATT], held[LOW]
    for third, line in enumerate((2, None, 3)):
        columns = pl.ds(third * features, features)
        part = dot_nn(x, flat(held[PROJ][:, :, columns]))
        if line is not None:
            part = part + lines[line : line + 1, :]
        mix[:, columns] = part.astype(jnp.bfloat16)
    done(MIX)
    head_low = low_lanes(rows)
    valid = jnp.broadcast_to(validity > 0, (2 * rows, rows))

    def pair_step(pair, _):
        at = pl.multiple_of(pair * 2 * HD, 2 * HD)
        q = mix[:, pl.ds(at, 2 * HD)] * jnp.asarray(SCALE, jnp.bfloat16)
        k = mix[:, pl.ds(features + at, 2 * HD)]
        v = mix[:, pl.ds(2 * features + at, 2 * HD)]
        scores = jnp.where(valid, dot_nt(two_heads(q, head_low), k), -1e30)
        top = jnp.max(scores, axis=-1, keepdims=True)
        weight = jnp.exp(scores - top)
        share = 1.0 / jnp.sum(weight, axis=-1, keepdims=True)
        if saving:
            weight = (weight * share).astype(jnp.bfloat16)
            held[PROBS][pl.ds(2 * pair, 2)] = weight.reshape(2, rows, rows)
            mixed = dot_nn(weight, v)
        else:
            mixed = dot_nn(weight.astype(jnp.bfloat16), v) * share
        att[:, pl.ds(at, 2 * HD)] = merged_heads(mixed, head_low).astype(jnp.bfloat16)

    lax.fori_loop(0, features // (2 * HD), pair_step, None, unroll=UNROLL)
    done(PROBS)
    done(ATT)
    total = x.astype(jnp.float32) + dot_nn(att[...], flat(held[OUT][...]))
    hat, scale = normalised(total + lines[4:5, :])
    hidden = hat * lines[0:1, :] + lines[5:6, :]
    low[...] = hidden.astype(jnp.bfloat16)
    if saving:
        held[HAT1][...] = hat.astype(jnp.bfloat16)
        held[STATS][:, 0:1] = scale
    done(LOW)
    done(HAT1)
    groups = offs.shape[1] // features
    total = hidden + lines[6:7, :]
    for group in range(groups):
        columns = pl.ds(group * features, features)
        upward = dot_nn(low[...], flat(held[EXPAND][:, :, columns]))
        value, gradient = gelu_parts(upward + offs[:, columns])
        value = value.astype(jnp.bfloat16)
        if saving:
            held[ACT][:, columns] = value
            held[SLOPE][:, columns] = gradient.astype(jnp.bfloat16)
        contract = held[CONTRACT]
        stack = contract.shape[0] // groups
        total = total + dot_nn(value, flat(contract[group * stack : (group + 1) * stack]))
    done(ACT)
    done(SLOPE)
    hat, scale = normalised(total)
    if saving:
        held[HAT2][...] = hat.astype(jnp.bfloat16)
        held[STATS][:, 1:2] = scale
    done(HAT2)
    done(STATS)
    return hat * lines[1:2, :] + lines[7:8, :]


def pooled_rows(value, across, down):
    total = jnp.sum(value * down, axis=0, keepdims=True)
    return total / jnp.sum(across, axis=-1, keepdims=True)


def norm_back(gradient, hat, scale, gain):
    weighted = gradient * gain
    mean = jnp.mean(weighted, axis=-1, keepdims=True)
    slant = jnp.mean(weighted * hat, axis=-1, keepdims=True)
    return scale * (weighted - mean - hat * slant)


def column_sum(vec_out, line, values):
    vec_out[line : line + 1, :] = jnp.sum(values, axis=0, keepdims=True)


def backward_feed(gradient, lines, held, vec_out, offs_out, done):
    features = gradient.shape[1]
    hat = held[HAT2][...].astype(jnp.float32)
    column_sum(vec_out, 1, gradient * hat)
    column_sum(vec_out, 7, gradient)
    moved = norm_back(gradient, hat, held[STATS][:, 1:2], lines[1:2, :])
    held[TOTAL][...] = moved
    rounded = moved.astype(jnp.bfloat16)
    held[DBRANCH][...] = rounded
    column_sum(vec_out, 6, rounded.astype(jnp.float32))
    done(DBRANCH)
    groups = offs_out.shape[1] // features
    contract = held[CONTRACT]
    stack = contract.shape[0] // groups
    for group in range(groups):
        columns = pl.ds(group * features, features)
        dactive = dot_nt(rounded, flat(contract[group * stack : (group + 1) * stack]))
        slope = held[SLOPE][:, columns].astype(jnp.float32)
        dup = (dactive * slope).astype(jnp.bfloat16)
        held[DUPWARD][:, columns] = dup
        offs_out[:, columns] = jnp.sum(dup.astype(jnp.float32), axis=0, keepdims=True)
    done(DUPWARD)


def backward_rest(lines, held, vec_out, done):
    rows, features = held[TOTAL].shape
    gradient = held[TOTAL][...] + dot_nt(held[DUPWARD][...], flat(held[EXPAND][...]))
    hat = held[HAT1][...].astype(jnp.float32)
    column_sum(vec_out, 0, gradient * hat)
    column_sum(vec_out, 5, gradient)
    stats, datt, dmix = held[STATS], held[DATT], held[DMIX]
    moved = norm_back(gradient, hat, stats[:, 0:1], lines[0:1, :])
    held[TOTAL][...] = moved
    rounded = moved.astype(jnp.bfloat16)
    held[DOUTPUT][...] = rounded
    column_sum(vec_out, 4, rounded.astype(jnp.float32))
    done(DOUTPUT)
    datt[...] = dot_nt(rounded, flat(held[OUT][...])).astype(jnp.bfloat16)
    head_low = low_lanes(rows)
    mix, probs = held[MIX], held[PROBS]

    def pair_step(pair, _):
        at = pl.multiple_of(pair * 2 * HD, 2 * HD)
        q = mix[:, pl.ds(at, 2 * HD)]
        k = mix[:, pl.ds(features + at, 2 * HD)]
        v = mix[:, pl.ds(2 * features + at, 2 * HD)]
        pull = datt[:, pl.ds(at, 2 * HD)]
        weight = flat(probs[pl.ds(2 * pair, 2)])
        wide = weight.astype(jnp.float32)
        product = dot_nt(two_heads(pull, head_low), v) * wide
        inner = jnp.sum(product, axis=-1, keepdims=True)
        dscores = (product - wide * inner).astype(jnp.bfloat16)
        dq = merged_heads(dot_nn(dscores, k), head_low)
        dmix[:, pl.ds(at, 2 * HD)] = (dq * SCALE).astype(jnp.bfloat16)
        q_turned, pull_turned = q.T, pull.T
        dk, dv = [], []
        for side in range(2):
            lanes = slice(side * HD, (side + 1) * HD)
            part = slice(side * rows, (side + 1) * rows)
            dk.append(dot_nn(q_turned[lanes], dscores[part]))
            dv.append(dot_nn(pull_turned[lanes], weight[part]))
        dk = (jnp.concatenate(dk, axis=0) * SCALE).astype(jnp.bfloat16).T
        dv = jnp.concatenate(dv, axis=0).astype(jnp.bfloat16).T
        dmix[:, pl.ds(features + at, 2 * HD)] = dk
        dmix[:, pl.ds(2 * features + at, 2 * HD)] = dv

    lax.fori_loop(0, features // (2 * HD), pair_step, None, unroll=UNROLL)
    done(DMIX)
    column_sum(vec_out, 2, dmix[:, 0:features].astype(jnp.float32))
    column_sum(vec_out, 3, dmix[:, 2 * features : 3 * features].astype(jnp.float32))
    moved = held[TOTAL][...] + dot_nt(dmix[...], flat(held[PROJ][...]))
    held[TOTAL][...] = moved
    done(TOTAL)
    return moved


def taken(refs, *counts):
    parts, at = [], 0
    for count in counts:
        parts.append(refs[at : at + count])
        at += count
    return parts + [refs[at:]]


FORWARD_HELD = (MIX, ATT, LOW)


def forward_kernel(layout, pack_count, view, first, crops, save, *refs):
    names = SAVED if save else FORWARD_HELD
    (flag, vrow, vcol, lines, offs, x_hbm), packs, (y_out, pooled_out), saved, refs = taken(
        refs, 6, pack_count, 2, len(SAVED) + 1 if save else 0
    )
    buffers, (x_buf, sems) = taken(refs, len(NAMES + names))
    saved = dict(zip(SAVED, saved[1:])) | {X_IN: saved[:1]}

    @pl.when(flag[0] == 1)
    def _():
        copier = Copier(sems)
        held = Held(NAMES + names, buffers, copier)
        fetches = []
        for crop in range(crops):
            at = (view, first + crop) if len(x_hbm.shape) == 4 else (first + crop,)
            source = x_hbm.at[at]
            fetches.append(copier.fetch(source, x_buf.at[crop]))
        for name in NAMES:
            held.fill_weight(name, layout, packs)

        def done(name):
            if save:
                copier.send(held[name], saved[name])

        for crop in range(crops):
            fetches[crop].wait()
            if save:
                copier.send(x_buf.at[crop], saved[X_IN][0])
            across = vrow[view, first + crop]
            value = forward_rows(x_buf[crop], across, lines, offs, held, done)
            y_out[crop] = value.astype(jnp.bfloat16)
            pooled_out[crop] = pooled_rows(value, across, vcol[view, first + crop])
        copier.finish()


def cost_of(flops):
    return pl.CostEstimate(flops=3 * flops, bytes_accessed=0, transcendentals=0)


def params(kept, first_in, first_out, flops):
    return dict(
        input_output_aliases={first_in + i: first_out + i for i in range(kept)},
        compiler_params=pltpu.CompilerParams(vmem_limit_bytes=VMEM_LIMIT),
        cost_estimate=cost_of(flops),
    )


def block_flops(rows, features, hidden_size):
    return 2 * rows * (4 * features * features + 2 * features * hidden_size)


def forward_block(flag, x, vrow, vcol, lines, offs, packs, layout, save, view, first, crops):
    rows, features = x.shape[-2:]
    sizes = rows, features, offs.shape[-1]
    names = (X_IN,) + SAVED if save else ()
    result = pl.pallas_call(
        functools.partial(forward_kernel, layout, len(packs), view, first, crops, save),
        out_shape=[
            jax.ShapeDtypeStruct((crops, rows, features), jnp.bfloat16),
            jax.ShapeDtypeStruct((crops, 1, features), jnp.float32),
        ]
        + outputs_of(names, *sizes),
        in_specs=[SMEM] + [VMEM] * 4 + [ANY] * (1 + len(packs)),
        out_specs=[VMEM] * 2 + [ANY] * len(names),
        scratch_shapes=scratch_of(NAMES + (SAVED if save else FORWARD_HELD), *sizes)
        + [
            pltpu.VMEM((crops, rows, features), jnp.bfloat16),
            pltpu.SemaphoreType.DMA((crops + len(layout) + len(names),)),
        ],
        **params(0, 0, 0, crops * block_flops(*sizes)),
    )(flag, vrow, vcol, lines, offs, x, *packs)
    return result[0], result[1], dict(zip(names, result[2:]))


ENDS = (ATT, LOW, ACT, X_IN)
BACK_HELD = (DBRANCH, DUPWARD, DOUTPUT, DATT, DMIX, TOTAL)


def turn_kernel(layout, pack_count, crop, *refs):
    head, packs, _, outs, ends, terms, refs = taken(
        refs, 7, pack_count, len(ENDS), 4, len(ENDS), len(TERMS)
    )
    flag, vrow, vcol, lines, offs, x_hbm, g_hbm = head
    pooled_out, vec_out, offs_out, dx_low = outs
    names = NAMES + SAVED + BACK_HELD + (X_IN, G_IN)
    buffers, (sems,) = taken(refs, len(names))
    places = dict(zip(ENDS + TERMS, ends + terms))

    @pl.when(flag[0] == 1)
    def _():
        copier = Copier(sems)
        held = Held(names, buffers, copier)
        held.fill(X_IN, x_hbm.at[0])
        for name in NAMES:
            held.fill_weight(name, layout, packs)
        held.fill(G_IN, g_hbm.at[crop])

        def done(name):
            if name in places:
                copier.send(held[name], places[name])

        done(X_IN)
        value = forward_rows(held[X_IN][...], vrow[0, crop], lines, offs, held, done)
        pooled_out[0] = pooled_rows(value, vrow[0, crop], vcol[0, crop])
        gradient = held[G_IN][...].astype(jnp.float32) * vcol[0, crop]
        backward_feed(gradient, lines, held, vec_out, offs_out, done)
        dx_low[...] = backward_rest(lines, held, vec_out, done).astype(jnp.bfloat16)
        copier.finish()


def turn_block(flag, x, gradient, vrow, vcol, lines, offs, packs, layout, crop, saved):
    rows, features = x.shape[-2:]
    sizes = rows, features, offs.shape[-1]
    result = pl.pallas_call(
        functools.partial(turn_kernel, layout, len(packs), crop),
        out_shape=[
            jax.ShapeDtypeStruct((1, 1, features), jnp.float32),
            jax.ShapeDtypeStruct((8, features), jnp.float32),
            jax.ShapeDtypeStruct(offs.shape, jnp.float32),
            jax.ShapeDtypeStruct((rows, features), jnp.bfloat16),
        ]
        + outputs_of(ENDS + TERMS, *sizes),
        in_specs=[SMEM] + [VMEM] * 4 + [ANY] * (2 + len(packs) + len(ENDS)),
        out_specs=[VMEM] * 4 + [ANY] * len(ENDS + TERMS),
        scratch_shapes=scratch_of(NAMES + SAVED + BACK_HELD + (X_IN, G_IN), *sizes)
        + [pltpu.SemaphoreType.DMA((2 + len(layout) + len(ENDS + TERMS),))],
        **params(len(ENDS), 7 + len(packs), 4, 2 * block_flops(*sizes)),
    )(flag, vrow, vcol, lines, offs, x, gradient, *packs, *[saved[name] for name in ENDS])
    return result[:4], dict(zip(ENDS + TERMS, result[4:]))


BACK_SAVED = (HAT2, STATS, SLOPE, HAT1, MIX, PROBS)
BACK_ORDER = (G_IN, HAT2, STATS, CONTRACT, SLOPE, EXPAND, HAT1, OUT, MIX, PROBS, PROJ)


def backward_kernel(layout, pack_count, *refs):
    (flag, lines, g_hbm), packs, saved, _, outs, terms, refs = taken(
        refs, 3, pack_count, len(BACK_SAVED), len(TERMS), 2, len(TERMS)
    )
    vec_out, offs_out = outs
    names = NAMES + BACK_SAVED + BACK_HELD + (G_IN,)
    buffers, (sems,) = taken(refs, len(names))
    places = dict(zip(TERMS, terms))
    saved = dict(zip(BACK_SAVED, saved)) | {G_IN: g_hbm}

    @pl.when(flag[0] == 1)
    def _():
        copier = Copier(sems)
        held = Held(names, buffers, copier)
        for name in BACK_ORDER:
            if name in NAMES:
                held.fill_weight(name, layout, packs)
            else:
                held.fill(name, saved[name])

        def done(name):
            copier.send(held[name], places[name])

        gradient = held[G_IN][...].astype(jnp.float32)
        backward_feed(gradient, lines, held, vec_out, offs_out, done)
        backward_rest(lines, held, vec_out, done)
        copier.finish()


def backward_block(flag, gradient, lines, packs, layout, saved, terms):
    rows, features = gradient.shape
    hidden_size = saved[SLOPE].shape[-1]
    sizes = rows, features, hidden_size
    result = pl.pallas_call(
        functools.partial(backward_kernel, layout, len(packs)),
        out_shape=[
            jax.ShapeDtypeStruct((8, features), jnp.float32),
            jax.ShapeDtypeStruct((1, hidden_size), jnp.float32),
        ]
        + outputs_of(TERMS, *sizes),
        in_specs=[SMEM, VMEM] + [ANY] * (1 + len(packs) + len(BACK_SAVED) + len(TERMS)),
        out_specs=[VMEM] * 2 + [ANY] * len(TERMS),
        scratch_shapes=scratch_of(NAMES + BACK_SAVED + BACK_HELD + (G_IN,), *sizes)
        + [pltpu.SemaphoreType.DMA((1 + len(layout) + len(BACK_SAVED) + len(TERMS),))],
        **params(
            len(TERMS), 3 + len(packs) + len(BACK_SAVED), 2, block_flops(*sizes)
        ),
    )(
        flag,
        lines,
        gradient,
        *packs,
        *[saved[name] for name in BACK_SAVED],
        *[terms[name] for name in TERMS],
    )
    return result[:2], dict(zip(TERMS, result[2:]))


FEED_SAVED = (HAT2, STATS, SLOPE)
FEED_TERMS = (DBRANCH, DUPWARD)


def feed_kernel(layout, pack_count, *refs):
    (flag, lines, g_hbm), packs, saved, _, outs, refs = taken(
        refs, 3, pack_count, len(FEED_SAVED), len(FEED_TERMS), 5
    )
    vec_out, offs_out, total_out, branch_out, upward_out = outs
    names = (CONTRACT,) + FEED_SAVED + FEED_TERMS + (TOTAL, G_IN)
    buffers, (sems,) = taken(refs, len(names))
    places = {DBRANCH: branch_out, DUPWARD: upward_out}

    @pl.when(flag[0] == 1)
    def _():
        copier = Copier(sems)
        held = Held(names, buffers, copier)
        held.fill(G_IN, g_hbm)
        held.fill(HAT2, saved[0])
        held.fill(STATS, saved[1])
        held.fill_weight(CONTRACT, layout, packs)
        held.fill(SLOPE, saved[2])

        def done(name):
            copier.send(held[name], places[name])

        vec_out[...] = jnp.zeros_like(vec_out)
        gradient = held[G_IN][...].astype(jnp.float32)
        backward_feed(gradient, lines, held, vec_out, offs_out, done)
        copier.send(held[TOTAL], total_out)
        copier.finish()


def feed_block(flag, gradient, lines, packs, layout, saved, terms):
    rows, features = gradient.shape
    hidden_size = saved[SLOPE].shape[-1]
    sizes = rows, features, hidden_size
    names = (TOTAL,) + FEED_TERMS
    result = pl.pallas_call(
        functools.partial(feed_kernel, layout, len(packs)),
        out_shape=[
            jax.ShapeDtypeStruct((8, features), jnp.float32),
            jax.ShapeDtypeStruct((1, hidden_size), jnp.float32),
        ]
        + outputs_of(names, *sizes),
        in_specs=[SMEM, VMEM] + [ANY] * (1 + len(packs) + len(FEED_SAVED) + len(FEED_TERMS)),
        out_specs=[VMEM] * 2 + [ANY] * len(names),
        scratch_shapes=scratch_of(
            (CONTRACT,) + FEED_SAVED + FEED_TERMS + (TOTAL, G_IN), *sizes
        )
        + [pltpu.SemaphoreType.DMA((1 + len(layout) + len(FEED_SAVED) + len(names),))],
        **params(
            len(FEED_TERMS),
            3 + len(packs) + len(FEED_SAVED),
            3,
            block_flops(*sizes) // 3,
        ),
    )(
        flag,
        lines,
        gradient,
        *packs,
        *[saved[name] for name in FEED_SAVED],
        *[terms[name] for name in FEED_TERMS],
    )
    return result[:2], dict(zip(names, result[2:]))


REST_IN = (DUPWARD, TOTAL, HAT1, STATS, MIX, PROBS)
REST_ORDER = (DUPWARD, EXPAND, TOTAL, HAT1, STATS, OUT, MIX, PROBS, PROJ)
REST_TERMS = (TOTAL, DOUTPUT, DMIX)


REST_WEIGHTS = (PROJ, OUT, EXPAND)


def closing_kernel(plan, layout, pack_count, *refs):
    (flag, core, lines), parts, packs, sources, _, operands, terms, outs, refs = taken(
        refs, 3, 8, pack_count, len(REST_IN), len(REST_TERMS), 6, len(REST_TERMS), 4
    )
    names = REST_WEIGHTS + REST_IN + (DOUTPUT, DMIX, DATT)
    held_buffers, buffers, (vec, sems, *scratch) = taken(refs, len(names), 4)
    places = dict(zip(REST_TERMS, terms))
    sources = dict(zip(REST_IN, sources))

    @pl.when(flag[0] == 1)
    def _():
        copier = Copier(sems)
        held = Held(names, held_buffers, copier)
        for name in REST_ORDER:
            if name in NAMES:
                held.fill_weight(name, layout, packs)
            else:
                held.fill(name, sources[name])

        def done(name):
            copier.send(held[name], places[name])

        vec[...] = jnp.zeros_like(vec)
        backward_rest(lines, held, vec, done)
        copier.finish()

    att0, att1, dout0, x0, x1, dmix0 = operands
    pairs = (att0, att1, dout0, places[DOUTPUT], x0, x1, dmix0, places[DMIX])
    own = (parts[4], parts[5], vec, parts[6], parts[7])
    row_products(plan, core, (flag, tuple(parts[:4]) + own), pairs, outs, buffers, *scratch)


def closing_block(plan, flag, core, lines, parts, packs, layout, saved, feed, terms, operands):
    rows, features = feed[TOTAL].shape
    sizes = rows, features, feed[DUPWARD].shape[-1]
    sources = dict(saved) | {DUPWARD: feed[DUPWARD], TOTAL: feed[TOTAL]}
    names = REST_WEIGHTS + REST_IN + (DOUTPUT, DMIX, DATT)
    pairs = [
        pltpu.VMEM((2 * rows, operand.shape[1]), jnp.bfloat16)
        for operand in (operands[0], operands[2], operands[3], operands[5])
    ]
    result = pl.pallas_call(
        functools.partial(closing_kernel, plan, layout, len(packs)),
        out_shape=outputs_of(REST_TERMS, *sizes) + sum_shapes(4, features, 128),
        in_specs=[SMEM] * 2
        + [VMEM] * (1 + len(parts))
        + [ANY] * (len(packs) + len(REST_IN) + len(REST_TERMS) + len(operands)),
        out_specs=[ANY] * (len(REST_TERMS) + 4),
        scratch_shapes=scratch_of(names, *sizes)
        + pairs
        + [
            pltpu.VMEM((8, features), jnp.float32),
            pltpu.SemaphoreType.DMA((len(layout) + len(REST_IN) + len(REST_TERMS),)),
        ]
        + row_scratch(4, 4, features),
        **params(
            len(REST_TERMS),
            3 + len(parts) + len(packs) + len(REST_IN),
            0,
            block_flops(*sizes) * 3 // 2,
        ),
    )(
        flag,
        core,
        lines,
        *parts,
        *packs,
        *[sources[name] for name in REST_IN],
        *[terms[name] for name in REST_TERMS],
        *operands,
    )
    return dict(zip(REST_TERMS, result)), result[len(REST_TERMS) :]


def load_pairs(sources, buffers, width, sems):
    copies = {}
    for i, buffer in enumerate(buffers):
        rows = buffer.shape[0] // 2
        for column in range(0, buffer.shape[1], width):
            columns = pl.ds(column, width)
            for half in range(2):
                copies.setdefault((i, column), []).append(
                    pltpu.make_async_copy(
                        sources[2 * i + half].at[:, columns],
                        buffer.at[pl.ds(half * rows, rows), columns],
                        sems.at[2 * i + half, column // width],
                    )
                )
    waited = set()

    def arrive(which, column):
        if (which, column) not in waited:
            waited.add((which, column))
            for copy in copies[which, column]:
                copy.wait()

    return copies, arrive


def contract_kernel(core, act0, act1, grad0, grad1, *refs):
    outs, (act, grad, pieces, in_sems, out_sems) = refs[:-5], refs[-5:]
    features = grad.shape[1]
    groups = act.shape[1] // features
    span = outs[0].shape[-1] // features
    copies, arrive = load_pairs((act0, act1, grad0, grad1), (act, grad), features, in_sems)
    for which in [(1, 0)] + [(0, part * features) for part in range(groups)]:
        for copy in copies[which]:
            copy.start()
    arrive(1, 0)
    sends = []
    for part in range(groups):
        columns = pl.ds(part * features, features)
        arrive(0, part * features)
        piece = dot_tn(act[:, columns], grad[...]).astype(jnp.bfloat16)
        pieces[part] = piece.reshape(pieces.shape[1:])
        for group in range(groups):
            for side in range(2):
                source = pieces.at[part, :, core[0] ^ side, group]
                place = outs[2 * (group // span) + side].at[
                    :, part % 2, part // 2, :, pl.ds((group % span) * features, features)
                ]
                copy = pltpu.make_async_copy(source, place, out_sems.at[part, group, side])
                copy.start()
                sends.append(copy)
    for copy in sends:
        copy.wait()


def vector_columns(flag, parts, target):
    turned, own, _ = taken(parts, 4, 5)
    chosen = flag[0] == 1
    vec = jnp.where(chosen, own[0][...] + own[1][...] + own[2][...], turned[0][...] + turned[1][...])
    marks = jnp.where(chosen, own[3][...] + own[4][...], turned[2][...] + turned[3][...])
    features = vec.shape[1]
    lane = lax.broadcasted_iota(jnp.int32, (features, 128), 1)
    column = jnp.concatenate([vec.T, jnp.zeros((features, 120), jnp.float32)], axis=1)
    marks = jnp.broadcast_to(marks, (8, marks.shape[1])).T.reshape(features // BLOCK, -1, BLOCK, 8)
    for group in range(marks.shape[1]):
        part = jnp.broadcast_to(marks[:, group].reshape(features, 8)[:, 0:1], column.shape)
        column = jnp.where(lane == 8 + group, part, column)
    coarse = column.astype(jnp.bfloat16)
    fine = pltpu.roll(column - coarse.astype(jnp.float32), 12, 1)
    both = jnp.where(lane < 12, column, jnp.where(lane < 24, fine, 0.0)).astype(jnp.bfloat16)
    for block in range(features // BLOCK):
        place = tuple((block >> level) & 1 for level in range(4))
        target[place] = both[block * BLOCK : (block + 1) * BLOCK]


def row_products(plan, core, vectors, sources, outs, buffers, pieces, small, in_sems, out_sems):
    width = pieces.shape[-1]
    copies, arrive = load_pairs(sources, buffers, width, in_sems)
    needs = [need for entry in plan for need in ((entry[0], 0), (entry[1], entry[2]))]
    for need in dict.fromkeys(needs):
        for copy in copies[need]:
            copy.start()
    sends = []

    def send(source, place, sem):
        copy = pltpu.make_async_copy(source, place, sem)
        copy.start()
        sends.append(copy)

    if vectors:
        vector_columns(*vectors, small)
        for side in range(2):
            place = outs[side].at[:, :, :, :, pl.ds(outs[side].shape[-1] - 128, 128)]
            send(small.at[core[0] ^ side], place, out_sems.at[len(plan), side, 0, 0])
    for part, (left, right, column, target, to) in enumerate(plan):
        arrive(left, 0)
        arrive(right, column)
        piece = dot_tn(buffers[left][...], buffers[right][:, column : column + width])
        pieces[part] = piece.astype(jnp.bfloat16).reshape(pieces.shape[1:])
        for side in range(2):
            for low, high in ((0, 0), (0, 1), (1, 0), (1, 1)):
                source = pieces.at[part, :, high, low, core[0] ^ side]
                place = outs[2 * target + side].at[low, high, :, :, pl.ds(to, width)]
                send(source, place, out_sems.at[part, side, low, high])
    for copy in sends:
        copy.wait()


def row_kernel(plan, core, *refs):
    sources, outs, buffers, refs = taken(refs, 4, len(refs) - 10, 2)
    row_products(plan, core, (), sources, outs, buffers, *refs)


def row_scratch(parts, pairs, features):
    return [
        pltpu.VMEM((parts, 2, 2, 2, 2, BLOCK, features), jnp.bfloat16),
        pltpu.VMEM((2, 2, 2, 2, BLOCK, 128), jnp.bfloat16),
        pltpu.SemaphoreType.DMA((2 * pairs, parts)),
        pltpu.SemaphoreType.DMA((parts + 1, 2, 2, 2)),
    ]


def sum_shapes(count, features, extra):
    widths = [2 * features + (extra if i < 2 else 0) for i in range(count)]
    return [jax.ShapeDtypeStruct((2, 2, 2, BLOCK, width), jnp.bfloat16) for width in widths]


def weight_gradient(kernel, core, operands, targets, contracted, features):
    pairs = features // BLOCK // 2
    bf16 = jnp.bfloat16
    parts = 2 * targets
    buffers = [
        pltpu.VMEM((2 * operand.shape[0], operand.shape[1]), bf16) for operand in operands[::2]
    ]
    if contracted:
        scratch = [
            pltpu.VMEM((parts, pairs // parts, 2, parts, BLOCK, features), bf16),
            pltpu.SemaphoreType.DMA((len(operands), parts)),
            pltpu.SemaphoreType.DMA((parts, parts, 2)),
        ]
    else:
        scratch = row_scratch(parts, len(operands) // 2, features)
    return pl.pallas_call(
        kernel,
        out_shape=sum_shapes(2 * targets, features, 0),
        in_specs=[SMEM] + [ANY] * len(operands),
        out_specs=[ANY] * (2 * targets),
        scratch_shapes=buffers + scratch,
        **params(0, 0, 0, 8 * targets * features * features * 512),
    )(core, *operands)


def pack_kernel(plan, *refs):
    target = refs[-1]
    for source, row, column, width, place in plan:
        block = refs[source][0, row : row + target.shape[0], column : column + width]
        target[:, place : place + width] = block


def packed(arrays, pieces, rows):
    width = sum(piece[3] for piece in pieces)
    if rows % 16:
        return jnp.concatenate(
            [arrays[i][0, r : r + rows, c : c + w] for i, r, c, w in pieces], axis=1
        )
    plan, place = [], 0
    for piece in pieces:
        plan.append(piece + (place,))
        place += piece[3]
    return pl.pallas_call(
        functools.partial(pack_kernel, tuple(plan)),
        out_shape=jax.ShapeDtypeStruct((rows, width), jnp.bfloat16),
        in_specs=[VMEM] * len(arrays),
        out_specs=VMEM,
    )(*arrays)


def refold(columns, shards_of, features):
    rows = features // shards_of
    if rows == BLOCK:
        return columns
    natural = jnp.moveaxis(columns.reshape(shards_of, rows, -1, features), 2, 1)
    natural = natural.reshape(features // BLOCK, -1, BLOCK, features)
    return jnp.moveaxis(natural, 1, 2).reshape(features, -1)


def unfold(blocks, shards_of, features):
    rows = features // shards_of
    if rows == BLOCK:
        return blocks
    natural = jnp.moveaxis(blocks.reshape(features // BLOCK, BLOCK, -1, features), 2, 1)
    natural = natural.reshape(shards_of, -1, rows, features)
    return jnp.moveaxis(natural, 1, 2).reshape(shards_of, rows, -1)


def swapped(block, level):
    route = [(i, i ^ (1 << level)) for i in range(lax.axis_size(DP))]
    return lax.ppermute(block, DP, route)


def added(first, second):
    return (first.astype(jnp.float32) + second.astype(jnp.float32)).astype(jnp.bfloat16)


def tied(value, *others):
    return lax.optimization_barrier((value,) + others)[0]


def bit(level):
    return (lax.axis_index(DP) >> level) & 1


def by_bits(block, levels):
    block = block.reshape((2,) * levels + block.shape[1:])
    return jnp.transpose(block, tuple(range(levels))[::-1] + tuple(range(levels, block.ndim)))


def outgoing(block, level):
    return lax.dynamic_index_in_dim(block, 1 - bit(level), 0, keepdims=False)


def joined(state, got, level):
    block = state[0]
    if isinstance(block, tuple):
        keep = block[0]
    else:
        keep = lax.dynamic_index_in_dim(block, bit(level), 0, keepdims=False)
    total = added(keep, got)
    if level + 1 == lax.axis_size(DP).bit_length() - 1:
        return total, total
    return total, outgoing(total, level + 1)


def halved(state, level):
    return joined(state, swapped(state[1], level), level)


def first_state(keep, send, shards_of, features, contracted, small):
    levels = shards_of.bit_length() - 1
    if features == BLOCK * shards_of:
        return (keep,), send
    blocks = jnp.transpose(jnp.stack([keep, send]), (3, 2, 1, 0, 4, 5))
    blocks = blocks.reshape((-1,) + blocks.shape[4:])
    if contracted:
        blocks = unfold(blocks, shards_of, features)
    else:
        blocks = blocks.reshape(shards_of, features // shards_of, -1)
    if small:
        lines = blocks[:, :, 2 * features :].reshape(features, 128)
        marks = jnp.stack([lines[:, 8:12], lines[:, 20:24]]).reshape(2, -1, BLOCK, 4)
        marks = jnp.moveaxis(marks, 3, 2).reshape(2, shards_of, 4, -1)
        marks = jnp.moveaxis(marks, 2, 3).reshape(2, features, 4)
        lines = jnp.concatenate([lines[:, :8], marks[0], lines[:, 12:20], marks[1]], axis=1)
        lines = jnp.pad(lines, ((0, 0), (0, 104))).reshape(shards_of, -1, 128)
        blocks = jnp.concatenate([blocks[:, :, : 2 * features], lines], axis=2)
    blocks = by_bits(blocks, levels)
    return blocks, outgoing(blocks, 0)


def doubled(block, level, other):
    upper = bit(level) == 1
    return jnp.concatenate(
        [jnp.where(upper, other, block), jnp.where(upper, block, other)], axis=0
    )


def shards(
    inputs,
    keep_mask,
    lengths,
    slot_order,
    cotangent,
    query_projection,
    query_output,
    query_expand,
    query_contract,
    query_gains,
    query_biases,
    query_offsets,
    momentum_projection,
    momentum_output,
    momentum_expand,
    momentum_contract,
    momentum_gains,
    momentum_biases,
    momentum_offsets,
):
    first_section = lax.axis_index(SECTION) == 0
    shards_of = lax.axis_size(DP)
    crop_count, crop_len, features = inputs.shape[1:]
    rows = features // shards_of
    hidden_size = query_expand.shape[2]
    groups = hidden_size // features
    blocks = features // BLOCK

    def folded(which):
        return [(which, i * rows, 0, features) for i in range(groups)]

    late_from, late_to = 2 * features // 3, 2 * features
    own = packed(
        (query_projection, query_output, query_expand, query_contract)
        + (momentum_output, momentum_projection),
        [(0, 0, 0, 3 * features), (1, 0, 0, features), (2, 0, 0, hidden_size)]
        + folded(3)
        + [(4, 0, 0, features), (5, 0, late_from, late_to - late_from)],
        rows,
    )
    gathered = lax.all_gather(own, DP, axis=0, tiled=True)
    rest = packed(
        (tied(momentum_projection, own), momentum_expand, momentum_contract),
        [(0, 0, 0, late_from), (0, 0, late_to, 3 * features - late_to), (1, 0, 0, hidden_size)]
        + folded(2),
        rows,
    )
    late = lax.all_gather(rest, DP, axis=0, tiled=True)

    sizes = (2 * rows, 6 * rows, groups * rows)
    vectors = jnp.concatenate(
        [
            array[0].reshape(-1)
            for array in (
                query_gains,
                query_biases,
                query_offsets,
                momentum_gains,
                momentum_biases,
                momentum_offsets,
            )
        ]
    )[None]
    levels = shards_of.bit_length() - 1
    for level in range(levels):
        vectors = doubled(vectors, level, swapped(vectors, level))
    vectors = vectors.astype(jnp.float32)

    def vector_rows(start):
        lines = vectors[:, start : start + 8 * rows].reshape(shards_of, 8, rows)
        marks = vectors[:, start + 8 * rows : start + sum(sizes)]
        return jnp.moveaxis(lines, 1, 0).reshape(8, features), marks.reshape(1, hidden_size)

    query_lines, query_offs = vector_rows(0)
    momentum_lines, momentum_offs = vector_rows(sum(sizes))

    inner = 4 * features + hidden_size
    vectors_at = inner + groups * features
    if rows != BLOCK:
        gathered = jnp.concatenate(
            [
                gathered[:, :inner],
                refold(gathered[:, inner:vectors_at], shards_of, features),
                gathered[:, vectors_at:],
            ],
            axis=1,
        )
        late_end = late.shape[1] - groups * features
        late = jnp.concatenate(
            [late[:, :late_end], refold(late[:, late_end:], shards_of, features)], axis=1
        )
    gathered = gathered.reshape(blocks, BLOCK, -1)
    late = late.reshape(blocks, BLOCK, -1)
    query_layout = (
        (PROJ, 0, 0, 3 * features, 0),
        (OUT, 0, 3 * features, features, 0),
        (EXPAND, 0, 4 * features, hidden_size, 0),
    ) + tuple((CONTRACT, 0, inner + i * features, features, i) for i in range(groups))
    late_expand = 3 * features - (late_to - late_from)
    momentum_layout = (
        (PROJ, 0, vectors_at + features, late_to - late_from, late_from),
        (PROJ, 1, 0, late_from, 0),
        (PROJ, 1, late_from, 3 * features - late_to, late_to),
        (OUT, 0, vectors_at, features, 0),
        (EXPAND, 1, late_expand, hidden_size, 0),
    ) + tuple(
        (CONTRACT, 1, late_expand + hidden_size + i * features, features, i)
        for i in range(groups)
    )

    positions = lax.broadcasted_iota(jnp.int32, keep_mask.shape, 2)
    validity = ((positions < lengths[:, :, None]) & ((keep_mask > 0) | (positions == 0))).astype(
        jnp.float32
    )
    across = validity[:, :, None, :]
    down = validity[:, :, :, None]
    in_first = first_section.astype(jnp.int32).reshape(1)
    in_second = 1 - in_first

    def momentum_forward(flag, block_in, crop, count):
        return forward_block(
            flag,
            block_in,
            across,
            down,
            momentum_lines,
            momentum_offs,
            (gathered, late),
            momentum_layout,
            False,
            1,
            crop,
            count,
        )[:2]

    crops = range(crop_count)
    last = crop_count - 1
    started, turned, before = [], [], [momentum_lines, momentum_offs]
    for c in crops:
        started.append(
            forward_block(
                tied(in_first, *before),
                inputs,
                across,
                down,
                query_lines,
                query_offs,
                (gathered,),
                query_layout,
                True,
                0,
                c,
                1,
            )
        )
        before = [started[c][1]]
    passed = [lax.ppermute(started[c][0], SECTION, [(0, 1)]) for c in crops]
    for c in crops:
        turned.append(
            turn_block(
                tied(in_second, *before),
                passed[c],
                cotangent,
                across,
                down,
                query_lines,
                query_offs,
                (gathered,),
                query_layout,
                c,
                started[c][2],
            )
        )
        before = [turned[c][0][0]]
    returned = [lax.ppermute(turned[c][0][3], SECTION, [(1, 0)]) for c in crops]
    ended = [
        backward_block(
            in_first,
            returned[c],
            query_lines,
            (gathered,),
            query_layout,
            started[c][2],
            turned[c][1],
        )
        for c in crops[:last]
    ]
    feed_ends, feed_terms = feed_block(
        tied(in_first, *[end[0][0] for end in ended]),
        returned[last],
        query_lines,
        (gathered,),
        query_layout,
        started[last][2],
        turned[last][1],
    )
    ends = [turned[c][1] | ended[c][1] for c in crops[:last]] + [turned[last][1] | feed_terms]

    core = lax.axis_index(DP) & 1 if rows == BLOCK else jnp.int32(0)
    core = jnp.asarray(core, jnp.int32).reshape(1)
    def pairs(sums, contracted=False, small=False):
        return [
            first_state(
                sums[2 * i], sums[2 * i + 1], shards_of, features, contracted, small and not i
            )
            for i in range(len(sums) // 2)
        ]

    def operands(*names):
        return [ends[c][name] for name in names for c in crops]

    chunks = pairs(
        weight_gradient(
            contract_kernel,
            core,
            operands(ACT, DBRANCH),
            groups // 2,
            True,
            features,
        ),
        True,
    )
    half = len(chunks)
    level_of = [0] * 6

    key_pools, key_seconds, key_ways, key_ins = [], [], [], []

    def advance(i, got):
        chunks[i] = joined(chunks[i], got, level_of[i])
        level_of[i] += 1

    def step(moving, kernel):
        gots = [swapped(chunks[i][1], level_of[i]) for i in moving]
        passing, key_ways[:] = list(key_ways), []
        done = kernel(*[chunks[i][1] for i in moving])
        done, *gots = lax.optimization_barrier((done, *gots, *passing))
        key_ins.extend(gots[len(moving) :])
        for i, got in zip(moving, gots):
            advance(i, got)
        return done

    def expand_gradient(*before):
        sums = weight_gradient(
            functools.partial(
                row_kernel,
                tuple((0, 1, i * features, i // 2, i % 2 * features) for i in range(groups)),
            ),
            tied(core, *before),
            operands(LOW, DUPWARD),
            groups // 2,
            False,
            features,
        )
        chunks.extend(pairs(sums))
        return sums[0]

    def closing(*before):
        turned_parts = [turned[c][0][1] for c in crops] + [turned[c][0][2] for c in crops]
        own_parts = [ended[0][0][0], feed_ends[0], ended[0][0][1], feed_ends[1]]
        terms, sums = closing_block(
            (
                (0, 1, 0, 0, 0),
                (2, 3, 0, 0, features),
                (2, 3, features, 1, 0),
                (2, 3, 2 * features, 1, features),
            ),
            tied(in_first, *before),
            core,
            query_lines,
            turned_parts + own_parts,
            (gathered,),
            query_layout,
            started[last][2],
            feed_terms,
            turned[last][1],
            operands(ATT) + [ends[0][DOUTPUT]] + operands(X_IN) + [ends[0][DMIX]],
        )
        ends[last] = ends[last] | terms
        chunks.extend(pairs(sums, False, True))
        return sums[2]

    def key_first(*before):
        key_out, pool = momentum_forward(tied(in_first, *before), inputs, 0, crop_count)
        key_ways.append(lax.ppermute(key_out, SECTION, [(0, 1)]))
        key_pools.append(pool)
        return pool

    def key_second(c, *before):
        return momentum_forward(tied(in_second, *before), key_ins[0], c, 1)[1]

    def unfinished(*second):
        return [
            i
            for i in range(len(chunks))
            if level_of[i] < levels and (level_of[i] != 1 or i in second)
        ]

    step([0, 1], expand_gradient)
    step(unfinished(0, 1), key_first)
    step(unfinished(2, 3), closing)
    for i in (4, 5):
        advance(i, swapped(chunks[i][1], 0))
    key_seconds.append(step(unfinished(4), functools.partial(key_second, 0)))
    chunks[5] = chunks[5][0], tied(chunks[5][1], key_seconds[0])
    done = step(unfinished(5), functools.partial(key_second, 1))
    key_seconds.append(done)

    key_pool = jnp.where(first_section, key_pools[0], jnp.concatenate(key_seconds, axis=0))
    pools = [jnp.where(first_section, started[c][1], turned[c][0][0]) for c in crops]
    pooled = jnp.concatenate([jnp.concatenate(pools, axis=0)[:, None], key_pool[:, None]], axis=1)
    order = (slot_order[:, None] == jnp.arange(crop_count, dtype=jnp.int32)[None, :])[..., None]
    pooled = jnp.sum(jnp.where(order, pooled.reshape(crop_count, -1)[None], 0.0), axis=1)
    for level in range(levels):
        moving = unfinished(*range(6))
        gots = [swapped(chunks[i][1], level_of[i]) for i in moving]
        other, *gots = lax.optimization_barrier((swapped(pooled, level), *gots))
        pooled = doubled(pooled, level, other)
        for i, got in zip(moving, gots):
            advance(i, got)
    pooled = jnp.moveaxis(pooled.reshape(-1, 2, features), 1, 0)[None]
    chunks[:4] = [(tied(chunk[0], done),) for chunk in chunks[:4]]
    small = chunks[4][0][:, half * features :]
    chunks[4] = (chunks[4][0][:, : half * features],)
    grad_input = jnp.stack([tied(end[TOTAL], done) for end in ends])[None]
    chunks = [chunk[0] for chunk in chunks]
    small = small.astype(jnp.float32)
    small = (small[:, :12] + small[:, 12:24]).T

    def wide(parts):
        return jnp.concatenate(parts, axis=1).astype(jnp.float32)

    contract_sum = jnp.moveaxis(wide(chunks[:half]).reshape(rows, groups, features), 1, 0)
    expand_sum = wide(chunks[half : 2 * half])
    project_sum = wide(chunks[2 * half :])
    return (
        pooled,
        grad_input,
        project_sum[None, :, features:],
        project_sum[None, :, :features],
        expand_sum[None],
        contract_sum.reshape(1, groups * rows, features),
        small[None, :2],
        small[None, 2:8],
        small[8:].reshape(1, groups * rows),
    )


def solution(mesh):
    in_specs = (
        P(None, DP, None, None),
        P(None, DP, None),
        P(None, DP),
        P(DP),
        P(DP, None, None),
        P(SECTION, DP, None),
        P(SECTION, DP, None),
        P(SECTION, DP, None),
        P(SECTION, DP, None),
        P(SECTION, None, DP),
        P(SECTION, None, DP),
        P(SECTION, DP),
        P(SECTION, DP, None),
        P(SECTION, DP, None),
        P(SECTION, DP, None),
        P(SECTION, DP, None),
        P(SECTION, None, DP),
        P(SECTION, None, DP),
        P(SECTION, DP),
    )
    out_specs = (
        P(SECTION, None, None, None),
        P(SECTION, DP, None, None),
        P(SECTION, DP, None),
        P(SECTION, DP, None),
        P(SECTION, DP, None),
        P(SECTION, DP, None),
        P(SECTION, None, DP),
        P(SECTION, None, DP),
        P(SECTION, DP),
    )
    return jax.shard_map(shards, mesh=mesh, in_specs=in_specs, out_specs=out_specs, check_vma=False)
```

```python
import functools

import jax
import jax.numpy as jnp
from jax import lax
from jax.experimental import pallas as pl
from jax.experimental.pallas import tpu as pltpu
from jax.sharding import PartitionSpec as P

DP, SECTION = "dp", "section"
HD = 64
BLOCK = 48
VMEM_LIMIT = 56 * 1024 * 1024

epsilon = 1e-12
SCALE = HD ** (-0.5)

ANY = pl.BlockSpec(memory_space=pl.ANY)
VMEM = pl.BlockSpec(memory_space=pltpu.VMEM)
SMEM = pl.BlockSpec(memory_space=pltpu.SMEM)


def dot_nn(a, b):
    return jnp.dot(a, b, preferred_element_type=jnp.float32)


def dot_nt(a, b):
    return lax.dot_general(a, b, (((1,), (1,)), ((), ())), preferred_element_type=jnp.float32)


def dot_tn(a, b):
    return lax.dot_general(a, b, (((0,), (0,)), ((), ())), preferred_element_type=jnp.float32)


def gelu_parts(values):
    size = jnp.abs(values)
    inverse = 1.0 / (1.0 + (0.3275911 * 0.5**0.5) * size)
    series = 0.5 * 1.061405429
    for factor in (-1.453152027, 1.421413741, -0.284496736, 0.254829592):
        series = series * inverse + 0.5 * factor
    bell = jnp.exp(-0.5 * (values * values))
    tail = series * inverse * bell
    phi = jnp.where(values >= 0, 1.0 - tail, tail)
    return values * phi, phi + values * bell * 0.3989422804014327


def normalised(values):
    centred = values - jnp.mean(values, axis=-1, keepdims=True)
    variance = jnp.mean(centred * centred, axis=-1, keepdims=True)
    scale = lax.rsqrt(variance + epsilon)
    return centred * scale, scale


(
    PROJ,
    OUT,
    EXPAND,
    CONTRACT,
    MIX,
    PROBS,
    HAT1,
    HAT2,
    SLOPE,
    STATS,
    ATT,
    LOW,
    ACT,
    TOTAL,
    DBRANCH,
    DUPWARD,
    DOUTPUT,
    DMIX,
    DATT,
    X_IN,
    G_IN,
    SUMS,
) = range(22)
NAMES = (PROJ, OUT, EXPAND, CONTRACT)
SAVED = (MIX, PROBS, HAT1, HAT2, SLOPE, STATS, ATT, LOW, ACT)
UNROLL = 3
TERMS = (TOTAL, DBRANCH, DUPWARD, DOUTPUT, DMIX)


def flat(block):
    return block.reshape(-1, block.shape[-1])


def shape_of(name, rows, features, hidden_size):
    blocks = features // BLOCK
    bf16, f32 = jnp.bfloat16, jnp.float32
    return {
        PROJ: ((blocks, BLOCK, 3 * features), bf16),
        OUT: ((blocks, BLOCK, features), bf16),
        EXPAND: ((blocks, BLOCK, hidden_size), bf16),
        CONTRACT: ((blocks, hidden_size // features, BLOCK, features), bf16),
        MIX: ((rows, 3 * features), bf16),
        PROBS: ((features // HD, rows, rows), bf16),
        STATS: ((rows, 128), f32),
        ACT: ((rows, hidden_size), bf16),
        SLOPE: ((rows, hidden_size), bf16),
        DUPWARD: ((rows, hidden_size), bf16),
        DMIX: ((rows, 3 * features), bf16),
        TOTAL: ((rows, features), f32),
        SUMS: ((rows, features), f32),
    }.get(name, ((rows, features), bf16))


def scratch_of(names, *sizes):
    return [pltpu.VMEM(*shape_of(name, *sizes)) for name in names]


def outputs_of(names, *sizes):
    return [jax.ShapeDtypeStruct(*shape_of(name, *sizes)) for name in names]


class Copier:
    def __init__(self, sems):
        self.sems, self.count, self.open = sems, 0, []

    def fetch(self, source, place):
        copy = pltpu.make_async_copy(source, place, self.sems.at[self.count])
        self.count += 1
        copy.start()
        return copy

    def send(self, source, place):
        self.open.append(self.fetch(source, place))

    def finish(self):
        for copy in self.open:
            copy.wait()


class Held:
    def __init__(self, names, buffers, copier, once=None):
        self.buffers, self.pending, self.copier = dict(zip(names, buffers)), {}, copier
        self.once = once

    def fill(self, name, source):
        self.pending[name] = [self.copier.fetch(source, self.buffers[name])]

    def fill_weight(self, wanted, layout, packs):
        buffer = self.buffers[wanted]
        for name, pack, source, width, target in layout:
            if name == wanted:
                block = packs[pack].at[:, :, pl.ds(source, width)]
                if name == CONTRACT:
                    place = buffer.at[:, target]
                else:
                    place = buffer.at[:, :, pl.ds(target, width)]
                self.pending.setdefault(name, []).append(self.copier.fetch(block, place))

    def __contains__(self, name):
        return name in self.buffers

    def __getitem__(self, name):
        copies = self.pending.pop(name, ())

        def wait():
            for copy in copies:
                copy.wait()

        if copies and self.once is not None:
            pl.when(self.once)(wait)
        else:
            wait()
        return self.buffers[name]


def two_heads(pair, head_low):
    zero = jnp.zeros_like(pair)
    return jnp.concatenate(
        [jnp.where(head_low, pair, zero), jnp.where(head_low, zero, pair)], axis=0
    )


def merged_heads(stacked, head_low):
    rows = stacked.shape[0] // 2
    return jnp.where(head_low, stacked[:rows], stacked[rows:])


def low_lanes(rows):
    return lax.broadcasted_iota(jnp.int32, (rows, 2 * HD), 1) < HD


def forward_rows(x, validity, lines, offs, held, done):
    rows, features = x.shape
    saving = PROBS in held
    mix, att, low = held[MIX], held[ATT], held[LOW]
    for third, line in enumerate((2, None, 3)):
        columns = pl.ds(third * features, features)
        part = dot_nn(x, flat(held[PROJ][:, :, columns]))
        if line is not None:
            part = part + lines[line : line + 1, :]
        mix[:, columns] = part.astype(jnp.bfloat16)
    done(MIX)
    head_low = low_lanes(rows)
    valid = jnp.broadcast_to(validity > 0, (2 * rows, rows))

    def pair_step(pair, _):
        at = pl.multiple_of(pair * 2 * HD, 2 * HD)
        q = mix[:, pl.ds(at, 2 * HD)] * jnp.asarray(SCALE, jnp.bfloat16)
        k = mix[:, pl.ds(features + at, 2 * HD)]
        v = mix[:, pl.ds(2 * features + at, 2 * HD)]
        scores = jnp.where(valid, dot_nt(two_heads(q, head_low), k), -1e30)
        top = jnp.max(scores, axis=-1, keepdims=True)
        weight = jnp.exp(scores - top)
        share = 1.0 / jnp.sum(weight, axis=-1, keepdims=True)
        if saving:
            weight = (weight * share).astype(jnp.bfloat16)
            held[PROBS][pl.ds(2 * pair, 2)] = weight.reshape(2, rows, rows)
            mixed = dot_nn(weight, v)
        else:
            mixed = dot_nn(weight.astype(jnp.bfloat16), v) * share
        att[:, pl.ds(at, 2 * HD)] = merged_heads(mixed, head_low).astype(jnp.bfloat16)

    lax.fori_loop(0, features // (2 * HD), pair_step, None, unroll=UNROLL)
    done(PROBS)
    done(ATT)
    total = x.astype(jnp.float32) + dot_nn(att[...], flat(held[OUT][...]))
    hat, scale = normalised(total + lines[4:5, :])
    hidden = hat * lines[0:1, :] + lines[5:6, :]
    low[...] = hidden.astype(jnp.bfloat16)
    if saving:
        held[HAT1][...] = hat.astype(jnp.bfloat16)
        held[STATS][:, 0:1] = scale
    done(LOW)
    done(HAT1)
    halves = 2
    span = offs.shape[1] // halves
    expand, contract = held[EXPAND], held[CONTRACT]
    stack = contract.shape[0] // halves
    sums = held[SUMS]
    sums[...] = hidden + lines[6:7, :]

    def feed_step(half, _):
        columns = pl.ds(pl.multiple_of(half * span, span), span)
        upward = dot_nn(low[...], flat(expand[:, :, columns]))
        value, gradient = gelu_parts(upward + offs[:, columns])
        value = value.astype(jnp.bfloat16)
        if saving:
            held[ACT][:, columns] = value
            held[SLOPE][:, columns] = gradient.astype(jnp.bfloat16)
        sums[...] += dot_nn(value, flat(contract[pl.ds(half * stack, stack)]))

    lax.fori_loop(0, halves, feed_step, None)
    total = sums[...]
    done(ACT)
    done(SLOPE)
    hat, scale = normalised(total)
    if saving:
        held[HAT2][...] = hat.astype(jnp.bfloat16)
        held[STATS][:, 1:2] = scale
    done(HAT2)
    done(STATS)
    return hat * lines[1:2, :] + lines[7:8, :]


def pooled_rows(value, across, down):
    total = jnp.sum(value * down, axis=0, keepdims=True)
    return total / jnp.sum(across, axis=-1, keepdims=True)


def norm_back(gradient, hat, scale, gain):
    weighted = gradient * gain
    mean = jnp.mean(weighted, axis=-1, keepdims=True)
    slant = jnp.mean(weighted * hat, axis=-1, keepdims=True)
    return scale * (weighted - mean - hat * slant)


def column_sum(vec_out, line, values):
    vec_out[line : line + 1, :] = jnp.sum(values, axis=0, keepdims=True)


def backward_feed(gradient, lines, held, vec_out, offs_out, done):
    features = gradient.shape[1]
    hat = held[HAT2][...].astype(jnp.float32)
    column_sum(vec_out, 1, gradient * hat)
    column_sum(vec_out, 7, gradient)
    moved = norm_back(gradient, hat, held[STATS][:, 1:2], lines[1:2, :])
    held[TOTAL][...] = moved
    rounded = moved.astype(jnp.bfloat16)
    held[DBRANCH][...] = rounded
    column_sum(vec_out, 6, rounded.astype(jnp.float32))
    done(DBRANCH)
    groups = offs_out.shape[1] // features
    contract = held[CONTRACT]
    stack = contract.shape[0] // groups
    for group in range(groups):
        columns = pl.ds(group * features, features)
        dactive = dot_nt(rounded, flat(contract[group * stack : (group + 1) * stack]))
        slope = held[SLOPE][:, columns].astype(jnp.float32)
        dup = (dactive * slope).astype(jnp.bfloat16)
        held[DUPWARD][:, columns] = dup
        offs_out[:, columns] = jnp.sum(dup.astype(jnp.float32), axis=0, keepdims=True)
    done(DUPWARD)


def backward_rest(lines, held, vec_out, done):
    rows, features = held[TOTAL].shape
    gradient = held[TOTAL][...] + dot_nt(held[DUPWARD][...], flat(held[EXPAND][...]))
    hat = held[HAT1][...].astype(jnp.float32)
    column_sum(vec_out, 0, gradient * hat)
    column_sum(vec_out, 5, gradient)
    stats, datt, dmix = held[STATS], held[DATT], held[DMIX]
    moved = norm_back(gradient, hat, stats[:, 0:1], lines[0:1, :])
    held[TOTAL][...] = moved
    rounded = moved.astype(jnp.bfloat16)
    held[DOUTPUT][...] = rounded
    column_sum(vec_out, 4, rounded.astype(jnp.float32))
    done(DOUTPUT)
    datt[...] = dot_nt(rounded, flat(held[OUT][...])).astype(jnp.bfloat16)
    head_low = low_lanes(rows)
    mix, probs = held[MIX], held[PROBS]

    def pair_step(pair, _):
        at = pl.multiple_of(pair * 2 * HD, 2 * HD)
        q = mix[:, pl.ds(at, 2 * HD)]
        k = mix[:, pl.ds(features + at, 2 * HD)]
        v = mix[:, pl.ds(2 * features + at, 2 * HD)]
        pull = datt[:, pl.ds(at, 2 * HD)]
        weight = flat(probs[pl.ds(2 * pair, 2)])
        wide = weight.astype(jnp.float32)
        product = dot_nt(two_heads(pull, head_low), v) * wide
        inner = jnp.sum(product, axis=-1, keepdims=True)
        dscores = (product - wide * inner).astype(jnp.bfloat16)
        dq = merged_heads(dot_nn(dscores, k), head_low)
        dmix[:, pl.ds(at, 2 * HD)] = (dq * SCALE).astype(jnp.bfloat16)
        q_turned, pull_turned = q.T, pull.T
        dk, dv = [], []
        for side in range(2):
            lanes = slice(side * HD, (side + 1) * HD)
            part = slice(side * rows, (side + 1) * rows)
            dk.append(dot_nn(q_turned[lanes], dscores[part]))
            dv.append(dot_nn(pull_turned[lanes], weight[part]))
        dk = (jnp.concatenate(dk, axis=0) * SCALE).astype(jnp.bfloat16).T
        dv = jnp.concatenate(dv, axis=0).astype(jnp.bfloat16).T
        dmix[:, pl.ds(features + at, 2 * HD)] = dk
        dmix[:, pl.ds(2 * features + at, 2 * HD)] = dv

    lax.fori_loop(0, features // (2 * HD), pair_step, None, unroll=UNROLL)
    done(DMIX)
    column_sum(vec_out, 2, dmix[:, 0:features].astype(jnp.float32))
    column_sum(vec_out, 3, dmix[:, 2 * features : 3 * features].astype(jnp.float32))
    moved = held[TOTAL][...] + dot_nt(dmix[...], flat(held[PROJ][...]))
    held[TOTAL][...] = moved
    done(TOTAL)
    return moved


def taken(refs, *counts):
    parts, at = [], 0
    for count in counts:
        parts.append(refs[at : at + count])
        at += count
    return parts + [refs[at:]]


FORWARD_HELD = (MIX, ATT, LOW, SUMS)


def forward_kernel(layout, pack_count, view, first, crops, save, *refs):
    names = SAVED + (SUMS,) if save else FORWARD_HELD
    (flag, vrow, vcol, lines, offs, x_hbm), packs, (y_out, pooled_out), saved, refs = taken(
        refs, 6, pack_count, 2, len(SAVED) + 1 if save else 0
    )
    buffers, (x_buf, sems) = taken(refs, len(NAMES + names))
    saved = dict(zip(SAVED, saved[1:])) | {X_IN: saved[:1]}

    @pl.when(flag[0] == 1)
    def _():
        copier = Copier(sems)
        held = Held(NAMES + names, buffers, copier)
        fetches = []
        for crop in range(crops):
            at = (view, first + crop) if len(x_hbm.shape) == 4 else (crop,)
            source = x_hbm.at[at]
            fetches.append(copier.fetch(source, x_buf.at[crop]))
        for name in NAMES:
            held.fill_weight(name, layout, packs)

        def done(name):
            if save:
                copier.send(held[name], saved[name])

        def one(crop, _):
            for at, fetch in enumerate(fetches):
                if crops == 1:
                    fetch.wait()
                else:
                    pl.when(crop == at)(fetch.wait)
            if save:
                copier.send(x_buf.at[crop], saved[X_IN][0])
            across = vrow[view, first + crop]
            value = forward_rows(x_buf[crop], across, lines, offs, held, done)
            y_out[crop] = value.astype(jnp.bfloat16)
            pooled_out[crop] = pooled_rows(value, across, vcol[view, first + crop])

        if crops == 1:
            one(0, None)
        else:

            def looped(crop, _):
                held.once = crop == 0
                one(crop, None)

            lax.fori_loop(0, crops, looped, None)
        copier.finish()


def cost_of(flops):
    return pl.CostEstimate(flops=3 * flops, bytes_accessed=0, transcendentals=0)


def params(kept, first_in, first_out, flops):
    return dict(
        input_output_aliases={first_in + i: first_out + i for i in range(kept)},
        compiler_params=pltpu.CompilerParams(vmem_limit_bytes=VMEM_LIMIT),
        cost_estimate=cost_of(flops),
    )


def block_flops(rows, features, hidden_size):
    return 2 * rows * (4 * features * features + 2 * features * hidden_size)


def forward_block(flag, x, vrow, vcol, lines, offs, packs, layout, save, view, first, crops):
    rows, features = x.shape[-2:]
    sizes = rows, features, offs.shape[-1]
    names = (X_IN,) + SAVED if save else ()
    result = pl.pallas_call(
        functools.partial(forward_kernel, layout, len(packs), view, first, crops, save),
        out_shape=[
            jax.ShapeDtypeStruct((crops, rows, features), jnp.bfloat16),
            jax.ShapeDtypeStruct((crops, 1, features), jnp.float32),
        ]
        + outputs_of(names, *sizes),
        in_specs=[SMEM] + [VMEM] * 4 + [ANY] * (1 + len(packs)),
        out_specs=[VMEM] * 2 + [ANY] * len(names),
        scratch_shapes=scratch_of(NAMES + (SAVED + (SUMS,) if save else FORWARD_HELD), *sizes)
        + [
            pltpu.VMEM((crops, rows, features), jnp.bfloat16),
            pltpu.SemaphoreType.DMA((crops + len(layout) + len(names),)),
        ],
        **params(0, 0, 0, crops * block_flops(*sizes)),
    )(flag, vrow, vcol, lines, offs, x, *packs)
    return result[0], result[1], dict(zip(names, result[2:]))


ENDS = (ATT, LOW, ACT, X_IN)
BACK_HELD = (DBRANCH, DUPWARD, DOUTPUT, DATT, DMIX, TOTAL)


def turn_kernel(layout, pack_count, crop, *refs):
    head, packs, _, outs, ends, terms, refs = taken(
        refs, 7, pack_count, len(ENDS), 4, len(ENDS), len(TERMS)
    )
    flag, vrow, vcol, lines, offs, x_hbm, g_hbm = head
    pooled_out, vec_out, offs_out, dx_low = outs
    names = NAMES + SAVED + BACK_HELD + (SUMS, X_IN, G_IN)
    buffers, (sems,) = taken(refs, len(names))
    places = dict(zip(ENDS + TERMS, ends + terms))

    @pl.when(flag[0] == 1)
    def _():
        copier = Copier(sems)
        held = Held(names, buffers, copier)
        held.fill(X_IN, x_hbm.at[0])
        for name in NAMES:
            held.fill_weight(name, layout, packs)
        held.fill(G_IN, g_hbm.at[crop])

        def done(name):
            if name in places:
                copier.send(held[name], places[name])

        done(X_IN)
        value = forward_rows(held[X_IN][...], vrow[0, crop], lines, offs, held, done)
        pooled_out[0] = pooled_rows(value, vrow[0, crop], vcol[0, crop])
        gradient = held[G_IN][...].astype(jnp.float32) * vcol[0, crop]
        backward_feed(gradient, lines, held, vec_out, offs_out, done)
        dx_low[...] = backward_rest(lines, held, vec_out, done).astype(jnp.bfloat16)
        copier.finish()


def turn_block(flag, x, gradient, vrow, vcol, lines, offs, packs, layout, crop, saved):
    rows, features = x.shape[-2:]
    sizes = rows, features, offs.shape[-1]
    result = pl.pallas_call(
        functools.partial(turn_kernel, layout, len(packs), crop),
        out_shape=[
            jax.ShapeDtypeStruct((1, 1, features), jnp.float32),
            jax.ShapeDtypeStruct((8, features), jnp.float32),
            jax.ShapeDtypeStruct(offs.shape, jnp.float32),
            jax.ShapeDtypeStruct((rows, features), jnp.bfloat16),
        ]
        + outputs_of(ENDS + TERMS, *sizes),
        in_specs=[SMEM] + [VMEM] * 4 + [ANY] * (2 + len(packs) + len(ENDS)),
        out_specs=[VMEM] * 4 + [ANY] * len(ENDS + TERMS),
        scratch_shapes=scratch_of(NAMES + SAVED + BACK_HELD + (SUMS, X_IN, G_IN), *sizes)
        + [pltpu.SemaphoreType.DMA((2 + len(layout) + len(ENDS + TERMS),))],
        **params(len(ENDS), 7 + len(packs), 4, 2 * block_flops(*sizes)),
    )(flag, vrow, vcol, lines, offs, x, gradient, *packs, *[saved[name] for name in ENDS])
    return result[:4], dict(zip(ENDS + TERMS, result[4:]))


BACK_SAVED = (HAT2, STATS, SLOPE, HAT1, MIX, PROBS)
BACK_ORDER = (G_IN, HAT2, STATS, CONTRACT, SLOPE, EXPAND, HAT1, OUT, MIX, PROBS, PROJ)


def backward_kernel(layout, pack_count, *refs):
    (flag, lines, g_hbm), packs, saved, _, outs, terms, refs = taken(
        refs, 3, pack_count, len(BACK_SAVED), len(TERMS), 2, len(TERMS)
    )
    vec_out, offs_out = outs
    names = NAMES + BACK_SAVED + BACK_HELD + (G_IN,)
    buffers, (sems,) = taken(refs, len(names))
    places = dict(zip(TERMS, terms))
    saved = dict(zip(BACK_SAVED, saved)) | {G_IN: g_hbm}

    @pl.when(flag[0] == 1)
    def _():
        copier = Copier(sems)
        held = Held(names, buffers, copier)
        for name in BACK_ORDER:
            if name in NAMES:
                held.fill_weight(name, layout, packs)
            else:
                held.fill(name, saved[name])

        def done(name):
            copier.send(held[name], places[name])

        gradient = held[G_IN][...].astype(jnp.float32)
        backward_feed(gradient, lines, held, vec_out, offs_out, done)
        backward_rest(lines, held, vec_out, done)
        copier.finish()


def backward_block(flag, gradient, lines, packs, layout, saved, terms):
    rows, features = gradient.shape
    hidden_size = saved[SLOPE].shape[-1]
    sizes = rows, features, hidden_size
    result = pl.pallas_call(
        functools.partial(backward_kernel, layout, len(packs)),
        out_shape=[
            jax.ShapeDtypeStruct((8, features), jnp.float32),
            jax.ShapeDtypeStruct((1, hidden_size), jnp.float32),
        ]
        + outputs_of(TERMS, *sizes),
        in_specs=[SMEM, VMEM] + [ANY] * (1 + len(packs) + len(BACK_SAVED) + len(TERMS)),
        out_specs=[VMEM] * 2 + [ANY] * len(TERMS),
        scratch_shapes=scratch_of(NAMES + BACK_SAVED + BACK_HELD + (G_IN,), *sizes)
        + [pltpu.SemaphoreType.DMA((1 + len(layout) + len(BACK_SAVED) + len(TERMS),))],
        **params(
            len(TERMS), 3 + len(packs) + len(BACK_SAVED), 2, block_flops(*sizes)
        ),
    )(
        flag,
        lines,
        gradient,
        *packs,
        *[saved[name] for name in BACK_SAVED],
        *[terms[name] for name in TERMS],
    )
    return result[:2], dict(zip(TERMS, result[2:]))


FEED_SAVED = (HAT2, STATS, SLOPE)
FEED_TERMS = (DBRANCH, DUPWARD)


def feed_kernel(plan, layout, pack_count, *refs):
    (flag, core, lines, g_hbm), packs, saved, _, operands, outs, sums, refs = taken(
        refs, 4, pack_count, len(FEED_SAVED), len(FEED_TERMS), 6, 5, 8
    )
    act0, act1, branch0, low0, low1, upward0 = operands
    vec_out, offs_out, total_out, branch_out, upward_out = outs
    names = (CONTRACT,) + FEED_SAVED + FEED_TERMS + (TOTAL, G_IN)
    buffers, (act, branch, low, upward, pieces, sems, in_sems, out_sems, *scratch) = taken(
        refs, len(names)
    )
    places = {DBRANCH: branch_out, DUPWARD: upward_out}
    first_copies, first_arrive = load_pairs(
        (act0, act1, branch0, branch_out), (act, branch), branch.shape[1], in_sems
    )

    @pl.when(flag[0] == 1)
    def _():
        copier = Copier(sems)
        held = Held(names, buffers, copier)
        held.fill(G_IN, g_hbm)
        held.fill(HAT2, saved[0])
        held.fill(STATS, saved[1])
        held.fill_weight(CONTRACT, layout, packs)
        held.fill(SLOPE, saved[2])

        def done(name):
            copier.send(held[name], places[name])

        vec_out[...] = jnp.zeros_like(vec_out)
        gradient = held[G_IN][...].astype(jnp.float32)
        backward_feed(gradient, lines, held, vec_out, offs_out, done)
        copier.send(held[TOTAL], total_out)
        copier.finish()

    contract_products(core, sums[:4], act, branch, pieces, first_copies, first_arrive, out_sems)
    row_products(
        plan, core, (), (low0, low1, upward0, upward_out), sums[4:], (low, upward), *scratch
    )


def feed_block(plan, flag, core, gradient, lines, packs, layout, saved, terms, operands):
    rows, features = gradient.shape
    hidden_size = saved[SLOPE].shape[-1]
    sizes = rows, features, hidden_size
    names = (TOTAL,) + FEED_TERMS
    groups = hidden_size // features
    blocks = features // BLOCK
    bf16 = jnp.bfloat16
    result = pl.pallas_call(
        functools.partial(feed_kernel, plan, layout, len(packs)),
        out_shape=[
            jax.ShapeDtypeStruct((8, features), jnp.float32),
            jax.ShapeDtypeStruct((1, hidden_size), jnp.float32),
        ]
        + outputs_of(names, *sizes)
        + sum_shapes(8, features, 0),
        in_specs=[SMEM] * 2
        + [VMEM]
        + [ANY] * (1 + len(packs) + len(FEED_SAVED) + len(FEED_TERMS) + len(operands)),
        out_specs=[VMEM] * 2 + [ANY] * (len(names) + 8),
        scratch_shapes=scratch_of(
            (CONTRACT,) + FEED_SAVED + FEED_TERMS + (TOTAL, G_IN), *sizes
        )
        + [
            pltpu.VMEM((2 * rows, width), bf16)
            for width in (hidden_size, features, features, hidden_size)
        ]
        + [
            pltpu.VMEM((groups, blocks // 2 // groups, 2, groups, BLOCK, features), bf16),
            pltpu.SemaphoreType.DMA((1 + len(layout) + len(FEED_SAVED) + len(names),)),
            pltpu.SemaphoreType.DMA((4, groups)),
            pltpu.SemaphoreType.DMA((groups, groups, 2)),
        ]
        + row_scratch(groups, 2, features),
        **params(
            len(FEED_TERMS),
            4 + len(packs) + len(FEED_SAVED),
            3,
            2 * block_flops(*sizes),
        ),
    )(
        flag,
        core,
        lines,
        gradient,
        *packs,
        *[saved[name] for name in FEED_SAVED],
        *[terms[name] for name in FEED_TERMS],
        *operands,
    )
    return result[:2], dict(zip(names, result[2:])), result[5:]


REST_IN = (DUPWARD, TOTAL, HAT1, STATS, MIX, PROBS)
REST_ORDER = (DUPWARD, EXPAND, TOTAL, HAT1, STATS, OUT, MIX, PROBS, PROJ)
REST_TERMS = (TOTAL, DOUTPUT, DMIX)


REST_WEIGHTS = (PROJ, OUT, EXPAND)


def closing_kernel(plan, layout, pack_count, *refs):
    (flag, core, lines), parts, packs, sources, _, operands, terms, outs, refs = taken(
        refs, 3, 8, pack_count, len(REST_IN), len(REST_TERMS), 6, len(REST_TERMS), 4
    )
    names = REST_WEIGHTS + REST_IN + (DOUTPUT, DMIX, DATT)
    held_buffers, buffers, (vec, sems, *scratch) = taken(refs, len(names), 4)
    places = dict(zip(REST_TERMS, terms))
    sources = dict(zip(REST_IN, sources))

    @pl.when(flag[0] == 1)
    def _():
        copier = Copier(sems)
        held = Held(names, held_buffers, copier)
        for name in REST_ORDER:
            if name in NAMES:
                held.fill_weight(name, layout, packs)
            else:
                held.fill(name, sources[name])

        def done(name):
            copier.send(held[name], places[name])

        vec[...] = jnp.zeros_like(vec)
        backward_rest(lines, held, vec, done)
        copier.finish()

    att0, att1, dout0, x0, x1, dmix0 = operands
    pairs = (att0, att1, dout0, places[DOUTPUT], x0, x1, dmix0, places[DMIX])
    own = (parts[4], parts[5], vec, parts[6], parts[7])
    row_products(plan, core, (flag, tuple(parts[:4]) + own), pairs, outs, buffers, *scratch)


def closing_block(plan, flag, core, lines, parts, packs, layout, saved, feed, terms, operands):
    rows, features = feed[TOTAL].shape
    sizes = rows, features, feed[DUPWARD].shape[-1]
    sources = dict(saved) | {DUPWARD: feed[DUPWARD], TOTAL: feed[TOTAL]}
    names = REST_WEIGHTS + REST_IN + (DOUTPUT, DMIX, DATT)
    pairs = [
        pltpu.VMEM((2 * rows, operand.shape[1]), jnp.bfloat16)
        for operand in (operands[0], operands[2], operands[3], operands[5])
    ]
    result = pl.pallas_call(
        functools.partial(closing_kernel, plan, layout, len(packs)),
        out_shape=outputs_of(REST_TERMS, *sizes) + sum_shapes(4, features, 128),
        in_specs=[SMEM] * 2
        + [VMEM] * (1 + len(parts))
        + [ANY] * (len(packs) + len(REST_IN) + len(REST_TERMS) + len(operands)),
        out_specs=[ANY] * (len(REST_TERMS) + 4),
        scratch_shapes=scratch_of(names, *sizes)
        + pairs
        + [
            pltpu.VMEM((8, features), jnp.float32),
            pltpu.SemaphoreType.DMA((len(layout) + len(REST_IN) + len(REST_TERMS),)),
        ]
        + row_scratch(4, 4, features),
        **params(
            len(REST_TERMS),
            3 + len(parts) + len(packs) + len(REST_IN),
            0,
            block_flops(*sizes) * 3 // 2,
        ),
    )(
        flag,
        core,
        lines,
        *parts,
        *packs,
        *[sources[name] for name in REST_IN],
        *[terms[name] for name in REST_TERMS],
        *operands,
    )
    return dict(zip(REST_TERMS, result)), result[len(REST_TERMS) :]


def load_pairs(sources, buffers, width, sems):
    copies = {}
    for i, buffer in enumerate(buffers):
        rows = buffer.shape[0] // 2
        for column in range(0, buffer.shape[1], width):
            columns = pl.ds(column, width)
            for half in range(2):
                copies.setdefault((i, column), []).append(
                    pltpu.make_async_copy(
                        sources[2 * i + half].at[:, columns],
                        buffer.at[pl.ds(half * rows, rows), columns],
                        sems.at[2 * i + half, column // width],
                    )
                )
    waited = set()

    def arrive(which, column):
        if (which, column) not in waited:
            waited.add((which, column))
            for copy in copies[which, column]:
                copy.wait()

    return copies, arrive


def contract_products(core, outs, act, grad, pieces, copies, arrive, out_sems):
    features = grad.shape[1]
    groups = act.shape[1] // features
    span = outs[0].shape[-1] // features
    for which in [(1, 0)] + [(0, part * features) for part in range(groups)]:
        for copy in copies[which]:
            copy.start()
    arrive(1, 0)
    sends = []
    for part in range(groups):
        columns = pl.ds(part * features, features)
        arrive(0, part * features)
        piece = dot_tn(act[:, columns], grad[...]).astype(jnp.bfloat16)
        pieces[part] = piece.reshape(pieces.shape[1:])
        for group in range(groups):
            for side in range(2):
                source = pieces.at[part, :, core[0] ^ side, group]
                place = outs[2 * (group // span) + side].at[
                    :, part % 2, part // 2, :, pl.ds((group % span) * features, features)
                ]
                copy = pltpu.make_async_copy(source, place, out_sems.at[part, group, side])
                copy.start()
                sends.append(copy)
    for copy in sends:
        copy.wait()


def vector_columns(flag, parts, target):
    turned, own, _ = taken(parts, 4, 5)
    chosen = flag[0] == 1
    vec = jnp.where(chosen, own[0][...] + own[1][...] + own[2][...], turned[0][...] + turned[1][...])
    marks = jnp.where(chosen, own[3][...] + own[4][...], turned[2][...] + turned[3][...])
    features = vec.shape[1]
    lane = lax.broadcasted_iota(jnp.int32, (features, 128), 1)
    column = jnp.concatenate([vec.T, jnp.zeros((features, 120), jnp.float32)], axis=1)
    marks = jnp.broadcast_to(marks, (8, marks.shape[1])).T.reshape(features // BLOCK, -1, BLOCK, 8)
    for group in range(marks.shape[1]):
        part = jnp.broadcast_to(marks[:, group].reshape(features, 8)[:, 0:1], column.shape)
        column = jnp.where(lane == 8 + group, part, column)
    coarse = column.astype(jnp.bfloat16)
    fine = pltpu.roll(column - coarse.astype(jnp.float32), 12, 1)
    both = jnp.where(lane < 12, column, jnp.where(lane < 24, fine, 0.0)).astype(jnp.bfloat16)
    for block in range(features // BLOCK):
        place = tuple((block >> level) & 1 for level in range(4))
        target[place] = both[block * BLOCK : (block + 1) * BLOCK]


def row_products(plan, core, vectors, sources, outs, buffers, pieces, small, in_sems, out_sems):
    width = pieces.shape[-1]
    copies, arrive = load_pairs(sources, buffers, width, in_sems)
    needs = [need for entry in plan for need in ((entry[0], 0), (entry[1], entry[2]))]
    for need in dict.fromkeys(needs):
        for copy in copies[need]:
            copy.start()
    sends = []

    def send(source, place, sem):
        copy = pltpu.make_async_copy(source, place, sem)
        copy.start()
        sends.append(copy)

    if vectors:
        vector_columns(*vectors, small)
        for side in range(2):
            place = outs[side].at[:, :, :, :, pl.ds(outs[side].shape[-1] - 128, 128)]
            send(small.at[core[0] ^ side], place, out_sems.at[len(plan), side, 0, 0])
    for part, (left, right, column, target, to) in enumerate(plan):
        arrive(left, 0)
        arrive(right, column)
        piece = dot_tn(buffers[left][...], buffers[right][:, column : column + width])
        pieces[part] = piece.astype(jnp.bfloat16).reshape(pieces.shape[1:])
        for side in range(2):
            for low, high in ((0, 0), (0, 1), (1, 0), (1, 1)):
                source = pieces.at[part, :, high, low, core[0] ^ side]
                place = outs[2 * target + side].at[low, high, :, :, pl.ds(to, width)]
                send(source, place, out_sems.at[part, side, low, high])
    for copy in sends:
        copy.wait()


def row_scratch(parts, pairs, features):
    return [
        pltpu.VMEM((parts, 2, 2, 2, 2, BLOCK, features), jnp.bfloat16),
        pltpu.VMEM((2, 2, 2, 2, BLOCK, 128), jnp.bfloat16),
        pltpu.SemaphoreType.DMA((2 * pairs, parts)),
        pltpu.SemaphoreType.DMA((parts + 1, 2, 2, 2)),
    ]


def sum_shapes(count, features, extra):
    widths = [2 * features + (extra if i < 2 else 0) for i in range(count)]
    return [jax.ShapeDtypeStruct((2, 2, 2, BLOCK, width), jnp.bfloat16) for width in widths]


def pack_kernel(plan, *refs):
    target = refs[-1]
    for source, row, column, width, place in plan:
        block = refs[source][0, row : row + target.shape[0], column : column + width]
        target[:, place : place + width] = block


def packed(arrays, pieces, rows):
    width = sum(piece[3] for piece in pieces)
    if rows % 16:
        return jnp.concatenate(
            [arrays[i][0, r : r + rows, c : c + w] for i, r, c, w in pieces], axis=1
        )
    plan, place = [], 0
    for piece in pieces:
        plan.append(piece + (place,))
        place += piece[3]
    return pl.pallas_call(
        functools.partial(pack_kernel, tuple(plan)),
        out_shape=jax.ShapeDtypeStruct((rows, width), jnp.bfloat16),
        in_specs=[VMEM] * len(arrays),
        out_specs=VMEM,
    )(*arrays)


def refold(columns, shards_of, features):
    rows = features // shards_of
    if rows == BLOCK:
        return columns
    natural = jnp.moveaxis(columns.reshape(shards_of, rows, -1, features), 2, 1)
    natural = natural.reshape(features // BLOCK, -1, BLOCK, features)
    return jnp.moveaxis(natural, 1, 2).reshape(features, -1)


def unfold(blocks, shards_of, features):
    rows = features // shards_of
    if rows == BLOCK:
        return blocks
    natural = jnp.moveaxis(blocks.reshape(features // BLOCK, BLOCK, -1, features), 2, 1)
    natural = natural.reshape(shards_of, -1, rows, features)
    return jnp.moveaxis(natural, 1, 2).reshape(shards_of, rows, -1)


def swapped(block, level):
    route = [(i, i ^ (1 << level)) for i in range(lax.axis_size(DP))]
    return lax.ppermute(block, DP, route)


def added(first, second):
    return (first.astype(jnp.float32) + second.astype(jnp.float32)).astype(jnp.bfloat16)


def tied(value, *others):
    return lax.optimization_barrier((value,) + others)[0]


def bit(level):
    return (lax.axis_index(DP) >> level) & 1


def by_bits(block, levels):
    block = block.reshape((2,) * levels + block.shape[1:])
    return jnp.transpose(block, tuple(range(levels))[::-1] + tuple(range(levels, block.ndim)))


def outgoing(block, level):
    return lax.dynamic_index_in_dim(block, 1 - bit(level), 0, keepdims=False)


def joined(state, got, level):
    block = state[0]
    if isinstance(block, tuple):
        keep = block[0]
    else:
        keep = lax.dynamic_index_in_dim(block, bit(level), 0, keepdims=False)
    total = added(keep, got)
    if level + 1 == lax.axis_size(DP).bit_length() - 1:
        return total, total
    return total, outgoing(total, level + 1)


def halved(state, level):
    return joined(state, swapped(state[1], level), level)


def first_state(keep, send, shards_of, features, contracted, small):
    levels = shards_of.bit_length() - 1
    if features == BLOCK * shards_of:
        return (keep,), send
    blocks = jnp.transpose(jnp.stack([keep, send]), (3, 2, 1, 0, 4, 5))
    blocks = blocks.reshape((-1,) + blocks.shape[4:])
    if contracted:
        blocks = unfold(blocks, shards_of, features)
    else:
        blocks = blocks.reshape(shards_of, features // shards_of, -1)
    if small:
        lines = blocks[:, :, 2 * features :].reshape(features, 128)
        marks = jnp.stack([lines[:, 8:12], lines[:, 20:24]]).reshape(2, -1, BLOCK, 4)
        marks = jnp.moveaxis(marks, 3, 2).reshape(2, shards_of, 4, -1)
        marks = jnp.moveaxis(marks, 2, 3).reshape(2, features, 4)
        lines = jnp.concatenate([lines[:, :8], marks[0], lines[:, 12:20], marks[1]], axis=1)
        lines = jnp.pad(lines, ((0, 0), (0, 104))).reshape(shards_of, -1, 128)
        blocks = jnp.concatenate([blocks[:, :, : 2 * features], lines], axis=2)
    blocks = by_bits(blocks, levels)
    return blocks, outgoing(blocks, 0)


def doubled(block, level, other):
    upper = bit(level) == 1
    return jnp.concatenate(
        [jnp.where(upper, other, block), jnp.where(upper, block, other)], axis=0
    )


def shards(
    inputs,
    keep_mask,
    lengths,
    slot_order,
    cotangent,
    query_projection,
    query_output,
    query_expand,
    query_contract,
    query_gains,
    query_biases,
    query_offsets,
    momentum_projection,
    momentum_output,
    momentum_expand,
    momentum_contract,
    momentum_gains,
    momentum_biases,
    momentum_offsets,
):
    first_section = lax.axis_index(SECTION) == 0
    shards_of = lax.axis_size(DP)
    crop_count, crop_len, features = inputs.shape[1:]
    rows = features // shards_of
    hidden_size = query_expand.shape[2]
    groups = hidden_size // features
    blocks = features // BLOCK

    def folded(which):
        return [(which, i * rows, 0, features) for i in range(groups)]

    late_from, late_to = 2 * features // 3, 2 * features
    own = packed(
        (query_projection, query_output, query_expand, query_contract)
        + (momentum_output, momentum_projection),
        [(0, 0, 0, 3 * features), (1, 0, 0, features), (2, 0, 0, hidden_size)]
        + folded(3)
        + [(4, 0, 0, features), (5, 0, late_from, late_to - late_from)],
        rows,
    )
    gathered = lax.all_gather(own, DP, axis=0, tiled=True)
    rest = packed(
        (tied(momentum_projection, own), momentum_expand, momentum_contract),
        [(0, 0, 0, late_from), (0, 0, late_to, 3 * features - late_to), (1, 0, 0, hidden_size)]
        + folded(2),
        rows,
    )
    late = lax.all_gather(rest, DP, axis=0, tiled=True)

    sizes = (2 * rows, 6 * rows, groups * rows)
    vectors = jnp.concatenate(
        [
            array[0].reshape(-1)
            for array in (
                query_gains,
                query_biases,
                query_offsets,
                momentum_gains,
                momentum_biases,
                momentum_offsets,
            )
        ]
    )[None]
    levels = shards_of.bit_length() - 1
    for level in range(levels):
        vectors = doubled(vectors, level, swapped(vectors, level))
    vectors = vectors.astype(jnp.float32)

    def vector_rows(start):
        lines = vectors[:, start : start + 8 * rows].reshape(shards_of, 8, rows)
        marks = vectors[:, start + 8 * rows : start + sum(sizes)]
        return jnp.moveaxis(lines, 1, 0).reshape(8, features), marks.reshape(1, hidden_size)

    query_lines, query_offs = vector_rows(0)
    momentum_lines, momentum_offs = vector_rows(sum(sizes))

    inner = 4 * features + hidden_size
    vectors_at = inner + groups * features
    if rows != BLOCK:
        gathered = jnp.concatenate(
            [
                gathered[:, :inner],
                refold(gathered[:, inner:vectors_at], shards_of, features),
                gathered[:, vectors_at:],
            ],
            axis=1,
        )
        late_end = late.shape[1] - groups * features
        late = jnp.concatenate(
            [late[:, :late_end], refold(late[:, late_end:], shards_of, features)], axis=1
        )
    gathered = gathered.reshape(blocks, BLOCK, -1)
    late = late.reshape(blocks, BLOCK, -1)
    query_layout = (
        (PROJ, 0, 0, 3 * features, 0),
        (OUT, 0, 3 * features, features, 0),
        (EXPAND, 0, 4 * features, hidden_size, 0),
    ) + tuple((CONTRACT, 0, inner + i * features, features, i) for i in range(groups))
    late_expand = 3 * features - (late_to - late_from)
    momentum_layout = (
        (PROJ, 0, vectors_at + features, late_to - late_from, late_from),
        (PROJ, 1, 0, late_from, 0),
        (PROJ, 1, late_from, 3 * features - late_to, late_to),
        (OUT, 0, vectors_at, features, 0),
        (EXPAND, 1, late_expand, hidden_size, 0),
    ) + tuple(
        (CONTRACT, 1, late_expand + hidden_size + i * features, features, i)
        for i in range(groups)
    )

    positions = lax.broadcasted_iota(jnp.int32, keep_mask.shape, 2)
    validity = ((positions < lengths[:, :, None]) & ((keep_mask > 0) | (positions == 0))).astype(
        jnp.float32
    )
    across = validity[:, :, None, :]
    down = validity[:, :, :, None]
    in_first = first_section.astype(jnp.int32).reshape(1)
    in_second = 1 - in_first

    def momentum_forward(flag, block_in):
        return forward_block(
            flag,
            block_in,
            across,
            down,
            momentum_lines,
            momentum_offs,
            (gathered, late),
            momentum_layout,
            False,
            1,
            0,
            crop_count,
        )[:2]

    crops = range(crop_count)
    last = crop_count - 1
    started, turned, before = [], [], [momentum_lines, momentum_offs]
    for c in crops:
        started.append(
            forward_block(
                tied(in_first, *before),
                inputs,
                across,
                down,
                query_lines,
                query_offs,
                (gathered,),
                query_layout,
                True,
                0,
                c,
                1,
            )
        )
        before = [started[c][1]]
    passed = [lax.ppermute(started[c][0], SECTION, [(0, 1)]) for c in crops]
    for c in crops:
        turned.append(
            turn_block(
                tied(in_second, *before),
                passed[c],
                cotangent,
                across,
                down,
                query_lines,
                query_offs,
                (gathered,),
                query_layout,
                c,
                started[c][2],
            )
        )
        before = [turned[c][0][0]]
    returned = [lax.ppermute(turned[c][0][3], SECTION, [(1, 0)]) for c in crops]
    ended = [
        backward_block(
            in_first,
            returned[c],
            query_lines,
            (gathered,),
            query_layout,
            started[c][2],
            turned[c][1],
        )
        for c in crops[:last]
    ]
    core = lax.axis_index(DP) & 1 if rows == BLOCK else jnp.int32(0)
    core = jnp.asarray(core, jnp.int32).reshape(1)
    outer = [turned[c][1] | ended[c][1] for c in crops[:last]]

    def operands(name, *ends):
        return [end[name] for end in ends or outer + [turned[last][1]]]

    feed_ends, feed_terms, sums = feed_block(
        tuple((0, 1, i * features, i // 2, i % 2 * features) for i in range(groups)),
        tied(in_first, *[end[0][0] for end in ended]),
        core,
        returned[last],
        query_lines,
        (gathered,),
        query_layout,
        started[last][2],
        turned[last][1],
        operands(ACT) + operands(DBRANCH, *outer) + operands(LOW) + operands(DUPWARD, *outer),
    )
    ends = outer + [turned[last][1] | feed_terms]

    def pairs(sums, contracted=False, small=False):
        return [
            first_state(
                sums[2 * i], sums[2 * i + 1], shards_of, features, contracted, small and not i
            )
            for i in range(len(sums) // 2)
        ]

    chunks = pairs(sums[:4], True) + pairs(sums[4:])
    half = groups // 2
    level_of = [0] * 6

    key_pools, key_ways = [], []

    def advance(i, got):
        chunks[i] = joined(chunks[i], got, level_of[i])
        level_of[i] += 1

    def step(moving, *kernels, passing=()):
        gots = [swapped(chunks[i][1], level_of[i]) for i in moving]
        before = tuple(chunks[i][1] for i in moving)
        for kernel in kernels:
            before = (kernel(*before),)
        passing = [way() for way in passing]
        *gots, done = lax.optimization_barrier((*gots, *passing, *before[:1]))
        for i, got in zip(moving, gots):
            advance(i, got)
        return gots[len(moving) :], done

    def closing(*before):
        turned_parts = [turned[c][0][1] for c in crops] + [turned[c][0][2] for c in crops]
        own_parts = [ended[0][0][0], feed_ends[0], ended[0][0][1], feed_ends[1]]
        terms, sums = closing_block(
            (
                (0, 1, 0, 0, 0),
                (2, 3, 0, 0, features),
                (2, 3, features, 1, 0),
                (2, 3, 2 * features, 1, features),
            ),
            tied(in_first, *before),
            core,
            query_lines,
            turned_parts + own_parts,
            (gathered,),
            query_layout,
            started[last][2],
            feed_terms,
            turned[last][1],
            operands(ATT) + operands(DOUTPUT, *outer) + operands(X_IN) + operands(DMIX, *outer),
        )
        ends[last] = ends[last] | terms
        chunks.extend(pairs(sums, False, True))
        return sums[2]

    def key_first(*before):
        key_out, pool = momentum_forward(tied(in_first, *before), inputs)
        key_ways.append(lax.ppermute(key_out, SECTION, [(0, 1)]))
        key_pools.append(pool)
        return pool

    def key_second(*before):
        return momentum_forward(tied(in_second, *before), key_ways[0])[1]

    def unfinished(*second):
        return [
            i
            for i in range(len(chunks))
            if level_of[i] < levels and (level_of[i] != 1 or i in second)
        ]

    for i in range(4):
        advance(i, swapped(chunks[i][1], 0))
    step([0, 1], key_first)
    both = (lambda: swapped(chunks[4][1], 0), lambda: swapped(chunks[5][1], 0))
    gots, done = step(unfinished(2, 3), closing, key_second, passing=both)
    for i, got in zip((4, 5), gots):
        advance(i, got)

    key_pool = jnp.where(first_section, key_pools[0], done)
    pools = [jnp.where(first_section, started[c][1], turned[c][0][0]) for c in crops]
    pooled = jnp.concatenate([jnp.concatenate(pools, axis=0)[:, None], key_pool[:, None]], axis=1)
    order = (slot_order[:, None] == jnp.arange(crop_count, dtype=jnp.int32)[None, :])[..., None]
    pooled = jnp.sum(jnp.where(order, pooled.reshape(crop_count, -1)[None], 0.0), axis=1)
    ways = [0] + list(range(2, levels)) + [1]
    pooled = pooled[None]
    moves = [(4, 2, 3), (5, 4, 0, 1), (5, 4, 2, 3), (5,)]
    for way, moving in zip(ways, moves + [()] * (levels - len(moves))):
        gots = [swapped(chunks[i][1], level_of[i]) for i in moving]
        *gots, other = lax.optimization_barrier((*gots, swapped(pooled, way)))
        for i, got in zip(moving, gots):
            advance(i, got)
        pooled = doubled(pooled, way, other)
    for i in range(6):
        while level_of[i] < levels:
            advance(i, swapped(chunks[i][1], level_of[i]))
    pooled = pooled.reshape((2,) * levels + (crop_count, 2, features))
    axes = sorted(range(levels), key=lambda j: -ways[levels - 1 - j])
    pooled = jnp.transpose(pooled, tuple(axes) + tuple(range(levels, levels + 3)))
    pooled = jnp.moveaxis(pooled.reshape(-1, 2, features), 1, 0)[None]
    chunks[:4] = [(tied(chunk[0], done),) for chunk in chunks[:4]]
    small = chunks[4][0][:, half * features :]
    chunks[4] = (chunks[4][0][:, : half * features],)
    grad_input = jnp.stack([tied(end[TOTAL], done) for end in ends])[None]
    chunks = [chunk[0] for chunk in chunks]
    small = small.astype(jnp.float32)
    small = (small[:, :12] + small[:, 12:24]).T

    def wide(parts):
        return jnp.concatenate(parts, axis=1).astype(jnp.float32)

    contract_sum = jnp.moveaxis(wide(chunks[:half]).reshape(rows, groups, features), 1, 0)
    expand_sum = wide(chunks[half : 2 * half])
    project_sum = wide(chunks[2 * half :])
    return (
        pooled,
        grad_input,
        project_sum[None, :, features:],
        project_sum[None, :, :features],
        expand_sum[None],
        contract_sum.reshape(1, groups * rows, features),
        small[None, :2],
        small[None, 2:8],
        small[8:].reshape(1, groups * rows),
    )


def solution(mesh):
    in_specs = (
        P(None, DP, None, None),
        P(None, DP, None),
        P(None, DP),
        P(DP),
        P(DP, None, None),
        P(SECTION, DP, None),
        P(SECTION, DP, None),
        P(SECTION, DP, None),
        P(SECTION, DP, None),
        P(SECTION, None, DP),
        P(SECTION, None, DP),
        P(SECTION, DP),
        P(SECTION, DP, None),
        P(SECTION, DP, None),
        P(SECTION, DP, None),
        P(SECTION, DP, None),
        P(SECTION, None, DP),
        P(SECTION, None, DP),
        P(SECTION, DP),
    )
    out_specs = (
        P(SECTION, None, None, None),
        P(SECTION, DP, None, None),
        P(SECTION, DP, None),
        P(SECTION, DP, None),
        P(SECTION, DP, None),
        P(SECTION, DP, None),
        P(SECTION, None, DP),
        P(SECTION, None, DP),
        P(SECTION, DP),
    )
    return jax.shard_map(shards, mesh=mesh, in_specs=in_specs, out_specs=out_specs, check_vma=False)
```

```python
import functools

import jax
import jax.numpy as jnp
from jax import lax
from jax.experimental import pallas as pl
from jax.experimental.pallas import tpu as pltpu
from jax.sharding import PartitionSpec as P

DP, SECTION = "dp", "section"
HD = 64
BLOCK = 48
VMEM_LIMIT = 56 * 1024 * 1024

epsilon = 1e-12
SCALE = HD ** (-0.5)

ANY = pl.BlockSpec(memory_space=pl.ANY)
VMEM = pl.BlockSpec(memory_space=pltpu.VMEM)
SMEM = pl.BlockSpec(memory_space=pltpu.SMEM)


def dot_nn(a, b):
    return jnp.dot(a, b, preferred_element_type=jnp.float32)


def dot_nt(a, b):
    return lax.dot_general(a, b, (((1,), (1,)), ((), ())), preferred_element_type=jnp.float32)


def dot_tn(a, b):
    return lax.dot_general(a, b, (((0,), (0,)), ((), ())), preferred_element_type=jnp.float32)


def gelu_parts(values):
    size = jnp.abs(values)
    inverse = pl.reciprocal(1.0 + (0.3275911 * 0.5**0.5) * size, approx=True)
    series = 0.5 * 1.061405429
    for factor in (-1.453152027, 1.421413741, -0.284496736, 0.254829592):
        series = series * inverse + 0.5 * factor
    bell = jnp.exp(-0.5 * (values * values))
    tail = series * inverse * bell
    phi = jnp.where(values >= 0, 1.0 - tail, tail)
    return values * phi, phi + values * bell * 0.3989422804014327


def normalised(values):
    centred = values - jnp.mean(values, axis=-1, keepdims=True)
    variance = jnp.mean(centred * centred, axis=-1, keepdims=True)
    scale = lax.rsqrt(variance + epsilon)
    return centred * scale, scale


(
    PROJ,
    OUT,
    EXPAND,
    CONTRACT,
    MIX,
    PROBS,
    HAT1,
    HAT2,
    SLOPE,
    STATS,
    ATT,
    LOW,
    ACT,
    TOTAL,
    DBRANCH,
    DUPWARD,
    DOUTPUT,
    DMIX,
    DATT,
    X_IN,
    G_IN,
    SUMS,
) = range(22)
NAMES = (PROJ, OUT, EXPAND, CONTRACT)
SAVED = (MIX, PROBS, HAT1, HAT2, SLOPE, STATS, ATT, LOW, ACT)
UNROLL = 3
TERMS = (TOTAL, DBRANCH, DUPWARD, DOUTPUT, DMIX)


def flat(block):
    return block.reshape(-1, block.shape[-1])


def shape_of(name, rows, features, hidden_size):
    blocks = features // BLOCK
    bf16, f32 = jnp.bfloat16, jnp.float32
    return {
        PROJ: ((blocks, BLOCK, 3 * features), bf16),
        OUT: ((blocks, BLOCK, features), bf16),
        EXPAND: ((blocks, BLOCK, hidden_size), bf16),
        CONTRACT: ((blocks, BLOCK, hidden_size), bf16),
        MIX: ((rows, 3 * features), bf16),
        PROBS: ((features // HD, rows, rows), bf16),
        STATS: ((rows, 128), f32),
        ACT: ((rows, hidden_size), bf16),
        SLOPE: ((rows, hidden_size), bf16),
        DUPWARD: ((rows, hidden_size), bf16),
        DMIX: ((rows, 3 * features), bf16),
        TOTAL: ((rows, features), f32),
        SUMS: ((rows, features), f32),
    }.get(name, ((rows, features), bf16))


def scratch_of(names, *sizes):
    return [pltpu.VMEM(*shape_of(name, *sizes)) for name in names]


def outputs_of(names, *sizes):
    return [jax.ShapeDtypeStruct(*shape_of(name, *sizes)) for name in names]


class Copier:
    def __init__(self, sems):
        self.sems, self.count, self.open = sems, 0, []

    def fetch(self, source, place):
        copy = pltpu.make_async_copy(source, place, self.sems.at[self.count])
        self.count += 1
        copy.start()
        return copy

    def send(self, source, place):
        self.open.append(self.fetch(source, place))

    def finish(self):
        for copy in self.open:
            copy.wait()


class Held:
    def __init__(self, names, buffers, copier, once=None):
        self.buffers, self.pending, self.copier = dict(zip(names, buffers)), {}, copier
        self.once = once

    def fill(self, name, source):
        self.pending[name] = [self.copier.fetch(source, self.buffers[name])]

    def fill_weight(self, wanted, layout, packs):
        buffer = self.buffers[wanted]
        for name, pack, source, width, target in layout:
            if name == wanted:
                block = packs[pack].at[:, :, pl.ds(source, width)]
                place = buffer.at[:, :, pl.ds(target, width)]
                self.pending.setdefault(name, []).append(self.copier.fetch(block, place))

    def __contains__(self, name):
        return name in self.buffers

    def __getitem__(self, name):
        copies = self.pending.pop(name, ())

        def wait():
            for copy in copies:
                copy.wait()

        if copies and self.once is not None:
            pl.when(self.once)(wait)
        else:
            wait()
        return self.buffers[name]


def unfolded(block, features):
    return jnp.concatenate(
        [
            block[i, :, at : at + features]
            for i in range(block.shape[0])
            for at in range(0, block.shape[2], features)
        ],
        axis=0,
    )


def two_heads(pair, head_low):
    zero = jnp.zeros_like(pair)
    return jnp.concatenate(
        [jnp.where(head_low, pair, zero), jnp.where(head_low, zero, pair)], axis=0
    )


def merged_heads(stacked, head_low):
    rows = stacked.shape[0] // 2
    return jnp.where(head_low, stacked[:rows], stacked[rows:])


def low_lanes(rows):
    return lax.broadcasted_iota(jnp.int32, (rows, 2 * HD), 1) < HD


def forward_rows(x, validity, lines, offs, held, done):
    rows, features = x.shape
    saving = PROBS in held
    mix, att, low = held[MIX], held[ATT], held[LOW]
    shift = jnp.concatenate([lines[2:3, :], jnp.zeros((1, features), jnp.float32), lines[3:4, :]], axis=1)
    mix[...] = (dot_nn(x, flat(held[PROJ][...])) + shift).astype(jnp.bfloat16)
    done(MIX)
    head_low = low_lanes(rows)
    valid = jnp.broadcast_to(validity > 0, (2 * rows, rows))

    def pair_step(pair, _):
        at = pl.multiple_of(pair * 2 * HD, 2 * HD)
        q = mix[:, pl.ds(at, 2 * HD)] * jnp.asarray(SCALE, jnp.bfloat16)
        k = mix[:, pl.ds(features + at, 2 * HD)]
        v = mix[:, pl.ds(2 * features + at, 2 * HD)]
        scores = jnp.where(valid, dot_nt(two_heads(q, head_low), k), -1e30)
        top = jnp.max(scores, axis=-1, keepdims=True)
        weight = jnp.exp(scores - top)
        share = 1.0 / jnp.sum(weight, axis=-1, keepdims=True)
        if saving:
            weight = (weight * share).astype(jnp.bfloat16)
            held[PROBS][pl.ds(2 * pair, 2)] = weight.reshape(2, rows, rows)
            mixed = dot_nn(weight, v)
        else:
            mixed = dot_nn(weight.astype(jnp.bfloat16), v) * share
        att[:, pl.ds(at, 2 * HD)] = merged_heads(mixed, head_low).astype(jnp.bfloat16)

    lax.fori_loop(0, features // (2 * HD), pair_step, None, unroll=UNROLL)
    done(PROBS)
    done(ATT)
    total = x.astype(jnp.float32) + dot_nn(att[...], flat(held[OUT][...]))
    hat, scale = normalised(total + lines[4:5, :])
    hidden = hat * lines[0:1, :] + lines[5:6, :]
    low[...] = hidden.astype(jnp.bfloat16)
    if saving:
        held[HAT1][...] = hat.astype(jnp.bfloat16)
        held[STATS][:, 0:1] = scale
    done(LOW)
    done(HAT1)
    halves = 2
    span = offs.shape[1] // halves
    expand, contract = held[EXPAND], held[CONTRACT]
    stack = contract.shape[0] // halves
    sums = held[SUMS]
    sums[...] = hidden + lines[6:7, :]

    def feed_step(half, _):
        columns = pl.ds(pl.multiple_of(half * span, span), span)
        upward = dot_nn(low[...], flat(expand[:, :, columns]))
        value, gradient = gelu_parts(upward + offs[:, columns])
        value = value.astype(jnp.bfloat16)
        if saving:
            held[ACT][:, columns] = value
            held[SLOPE][:, columns] = gradient.astype(jnp.bfloat16)
        sums[...] += dot_nn(value, unfolded(contract[pl.ds(half * stack, stack)], features))

    lax.fori_loop(0, halves, feed_step, None)
    total = sums[...]
    done(ACT)
    done(SLOPE)
    hat, scale = normalised(total)
    if saving:
        held[HAT2][...] = hat.astype(jnp.bfloat16)
        held[STATS][:, 1:2] = scale
    done(HAT2)
    done(STATS)
    return hat * lines[1:2, :] + lines[7:8, :]


def pooled_rows(value, across, down):
    total = jnp.sum(value * down, axis=0, keepdims=True)
    return total / jnp.sum(across, axis=-1, keepdims=True)


def norm_back(gradient, hat, scale, gain):
    weighted = gradient * gain
    mean = jnp.mean(weighted, axis=-1, keepdims=True)
    slant = jnp.mean(weighted * hat, axis=-1, keepdims=True)
    return scale * (weighted - mean - hat * slant)


def column_sum(vec_out, line, values):
    vec_out[line : line + 1, :] = jnp.sum(values, axis=0, keepdims=True)


def backward_feed(gradient, lines, held, vec_out, offs_out, done):
    features = gradient.shape[1]
    hat = held[HAT2][...].astype(jnp.float32)
    column_sum(vec_out, 1, gradient * hat)
    column_sum(vec_out, 7, gradient)
    moved = norm_back(gradient, hat, held[STATS][:, 1:2], lines[1:2, :])
    held[TOTAL][...] = moved
    rounded = moved.astype(jnp.bfloat16)
    held[DBRANCH][...] = rounded
    column_sum(vec_out, 6, rounded.astype(jnp.float32))
    done(DBRANCH)
    groups = offs_out.shape[1] // features
    contract = held[CONTRACT]
    stack = contract.shape[0] // groups
    for group in range(groups):
        columns = pl.ds(group * features, features)
        block = unfolded(contract[group * stack : (group + 1) * stack], features)
        dactive = dot_nt(rounded, block)
        slope = held[SLOPE][:, columns].astype(jnp.float32)
        dup = (dactive * slope).astype(jnp.bfloat16)
        held[DUPWARD][:, columns] = dup
        offs_out[:, columns] = jnp.sum(dup.astype(jnp.float32), axis=0, keepdims=True)
    done(DUPWARD)


def backward_rest(lines, held, vec_out, done):
    rows, features = held[TOTAL].shape
    gradient = held[TOTAL][...] + dot_nt(held[DUPWARD][...], flat(held[EXPAND][...]))
    hat = held[HAT1][...].astype(jnp.float32)
    column_sum(vec_out, 0, gradient * hat)
    column_sum(vec_out, 5, gradient)
    stats, datt, dmix = held[STATS], held[DATT], held[DMIX]
    moved = norm_back(gradient, hat, stats[:, 0:1], lines[0:1, :])
    held[TOTAL][...] = moved
    rounded = moved.astype(jnp.bfloat16)
    held[DOUTPUT][...] = rounded
    column_sum(vec_out, 4, rounded.astype(jnp.float32))
    done(DOUTPUT)
    datt[...] = dot_nt(rounded, flat(held[OUT][...])).astype(jnp.bfloat16)
    head_low = low_lanes(rows)
    mix, probs = held[MIX], held[PROBS]

    def pair_step(pair, _):
        at = pl.multiple_of(pair * 2 * HD, 2 * HD)
        q = mix[:, pl.ds(at, 2 * HD)]
        k = mix[:, pl.ds(features + at, 2 * HD)]
        v = mix[:, pl.ds(2 * features + at, 2 * HD)]
        pull = datt[:, pl.ds(at, 2 * HD)]
        weight = flat(probs[pl.ds(2 * pair, 2)])
        wide = weight.astype(jnp.float32)
        product = dot_nt(two_heads(pull, head_low), v) * wide
        inner = jnp.sum(product, axis=-1, keepdims=True)
        dscores = (product - wide * inner).astype(jnp.bfloat16)
        dq = merged_heads(dot_nn(dscores, k), head_low)
        dmix[:, pl.ds(at, 2 * HD)] = (dq * SCALE).astype(jnp.bfloat16)
        q_turned, pull_turned = q.T, pull.T
        dk, dv = [], []
        for side in range(2):
            lanes = slice(side * HD, (side + 1) * HD)
            part = slice(side * rows, (side + 1) * rows)
            dk.append(dot_nn(q_turned[lanes], dscores[part]))
            dv.append(dot_nn(pull_turned[lanes], weight[part]))
        dk = (jnp.concatenate(dk, axis=0) * SCALE).astype(jnp.bfloat16).T
        dv = jnp.concatenate(dv, axis=0).astype(jnp.bfloat16).T
        dmix[:, pl.ds(features + at, 2 * HD)] = dk
        dmix[:, pl.ds(2 * features + at, 2 * HD)] = dv

    lax.fori_loop(0, features // (2 * HD), pair_step, None, unroll=UNROLL)
    done(DMIX)
    column_sum(vec_out, 2, dmix[:, 0:features].astype(jnp.float32))
    column_sum(vec_out, 3, dmix[:, 2 * features : 3 * features].astype(jnp.float32))
    moved = held[TOTAL][...] + dot_nt(dmix[...], flat(held[PROJ][...]))
    held[TOTAL][...] = moved
    done(TOTAL)
    return moved


def taken(refs, *counts):
    parts, at = [], 0
    for count in counts:
        parts.append(refs[at : at + count])
        at += count
    return parts + [refs[at:]]


FORWARD_HELD = (MIX, ATT, LOW, SUMS)


def forward_kernel(layout, pack_count, view, first, crops, save, *refs):
    names = SAVED + (SUMS,) if save else FORWARD_HELD
    (flag, vrow, vcol, lines, offs, x_hbm), packs, (y_out, pooled_out), saved, refs = taken(
        refs, 6, pack_count, 2, len(SAVED) + 1 if save else 0
    )
    buffers, (x_buf, sems) = taken(refs, len(NAMES + names))
    saved = dict(zip(SAVED, saved[1:])) | {X_IN: saved[:1]}

    @pl.when(flag[0] == 1)
    def _():
        copier = Copier(sems)
        held = Held(NAMES + names, buffers, copier)
        fetches = []
        for crop in range(crops):
            at = (view, first + crop) if len(x_hbm.shape) == 4 else (crop,)
            source = x_hbm.at[at]
            fetches.append(copier.fetch(source, x_buf.at[crop]))
        for name in NAMES:
            held.fill_weight(name, layout, packs)

        def done(name):
            if save:
                copier.send(held[name], saved[name])

        def one(crop, _):
            for at, fetch in enumerate(fetches):
                if crops == 1:
                    fetch.wait()
                else:
                    pl.when(crop == at)(fetch.wait)
            if save:
                copier.send(x_buf.at[crop], saved[X_IN][0])
            across = vrow[view, first + crop]
            value = forward_rows(x_buf[crop], across, lines, offs, held, done)
            y_out[crop] = value.astype(jnp.bfloat16)
            pooled_out[crop] = pooled_rows(value, across, vcol[view, first + crop])

        if crops == 1:
            one(0, None)
        else:

            def looped(crop, _):
                held.once = crop == 0
                one(crop, None)

            lax.fori_loop(0, crops, looped, None)
        copier.finish()


def cost_of(flops):
    return pl.CostEstimate(flops=3 * flops, bytes_accessed=0, transcendentals=0)


def params(kept, first_in, first_out, flops):
    return dict(
        input_output_aliases={first_in + i: first_out + i for i in range(kept)},
        compiler_params=pltpu.CompilerParams(vmem_limit_bytes=VMEM_LIMIT),
        cost_estimate=cost_of(flops),
    )


def block_flops(rows, features, hidden_size):
    return 2 * rows * (4 * features * features + 2 * features * hidden_size)


def forward_block(flag, x, vrow, vcol, lines, offs, packs, layout, save, view, first, crops):
    rows, features = x.shape[-2:]
    sizes = rows, features, offs.shape[-1]
    names = (X_IN,) + SAVED if save else ()
    result = pl.pallas_call(
        functools.partial(forward_kernel, layout, len(packs), view, first, crops, save),
        out_shape=[
            jax.ShapeDtypeStruct((crops, rows, features), jnp.bfloat16),
            jax.ShapeDtypeStruct((crops, 1, features), jnp.float32),
        ]
        + outputs_of(names, *sizes),
        in_specs=[SMEM] + [VMEM] * 4 + [ANY] * (1 + len(packs)),
        out_specs=[VMEM] * 2 + [ANY] * len(names),
        scratch_shapes=scratch_of(NAMES + (SAVED + (SUMS,) if save else FORWARD_HELD), *sizes)
        + [
            pltpu.VMEM((crops, rows, features), jnp.bfloat16),
            pltpu.SemaphoreType.DMA((crops + len(layout) + len(names),)),
        ],
        **params(0, 0, 0, crops * block_flops(*sizes)),
    )(flag, vrow, vcol, lines, offs, x, *packs)
    return result[0], result[1], dict(zip(names, result[2:]))


ENDS = (ATT, LOW, ACT, X_IN)
BACK_HELD = (DBRANCH, DUPWARD, DOUTPUT, DATT, DMIX, TOTAL)


def turn_kernel(layout, pack_count, crop, *refs):
    head, packs, _, outs, ends, terms, refs = taken(
        refs, 7, pack_count, len(ENDS), 4, len(ENDS), len(TERMS)
    )
    flag, vrow, vcol, lines, offs, x_hbm, g_hbm = head
    pooled_out, vec_out, offs_out, dx_low = outs
    names = NAMES + SAVED + BACK_HELD + (SUMS, X_IN, G_IN)
    buffers, (sems,) = taken(refs, len(names))
    places = dict(zip(ENDS + TERMS, ends + terms))

    @pl.when(flag[0] == 1)
    def _():
        copier = Copier(sems)
        held = Held(names, buffers, copier)
        held.fill(X_IN, x_hbm.at[0])
        for name in NAMES:
            held.fill_weight(name, layout, packs)
        held.fill(G_IN, g_hbm.at[crop])

        def done(name):
            if name in places:
                copier.send(held[name], places[name])

        done(X_IN)
        value = forward_rows(held[X_IN][...], vrow[0, crop], lines, offs, held, done)
        pooled_out[0] = pooled_rows(value, vrow[0, crop], vcol[0, crop])
        gradient = held[G_IN][...].astype(jnp.float32) * vcol[0, crop]
        backward_feed(gradient, lines, held, vec_out, offs_out, done)
        dx_low[...] = backward_rest(lines, held, vec_out, done).astype(jnp.bfloat16)
        copier.finish()


def turn_block(flag, x, gradient, vrow, vcol, lines, offs, packs, layout, crop, saved):
    rows, features = x.shape[-2:]
    sizes = rows, features, offs.shape[-1]
    result = pl.pallas_call(
        functools.partial(turn_kernel, layout, len(packs), crop),
        out_shape=[
            jax.ShapeDtypeStruct((1, 1, features), jnp.float32),
            jax.ShapeDtypeStruct((8, features), jnp.float32),
            jax.ShapeDtypeStruct(offs.shape, jnp.float32),
            jax.ShapeDtypeStruct((rows, features), jnp.bfloat16),
        ]
        + outputs_of(ENDS + TERMS, *sizes),
        in_specs=[SMEM] + [VMEM] * 4 + [ANY] * (2 + len(packs) + len(ENDS)),
        out_specs=[VMEM] * 4 + [ANY] * len(ENDS + TERMS),
        scratch_shapes=scratch_of(NAMES + SAVED + BACK_HELD + (SUMS, X_IN, G_IN), *sizes)
        + [pltpu.SemaphoreType.DMA((2 + len(layout) + len(ENDS + TERMS),))],
        **params(len(ENDS), 7 + len(packs), 4, 2 * block_flops(*sizes)),
    )(flag, vrow, vcol, lines, offs, x, gradient, *packs, *[saved[name] for name in ENDS])
    return result[:4], dict(zip(ENDS + TERMS, result[4:]))


BACK_SAVED = (HAT2, STATS, SLOPE, HAT1, MIX, PROBS)
BACK_ORDER = (G_IN, HAT2, STATS, CONTRACT, SLOPE, EXPAND, HAT1, OUT, MIX, PROBS, PROJ)


def backward_kernel(layout, pack_count, *refs):
    (flag, lines, g_hbm), packs, saved, _, outs, terms, refs = taken(
        refs, 3, pack_count, len(BACK_SAVED), len(TERMS), 2, len(TERMS)
    )
    vec_out, offs_out = outs
    names = NAMES + BACK_SAVED + BACK_HELD + (G_IN,)
    buffers, (sems,) = taken(refs, len(names))
    places = dict(zip(TERMS, terms))
    saved = dict(zip(BACK_SAVED, saved)) | {G_IN: g_hbm}

    @pl.when(flag[0] == 1)
    def _():
        copier = Copier(sems)
        held = Held(names, buffers, copier)
        for name in BACK_ORDER:
            if name in NAMES:
                held.fill_weight(name, layout, packs)
            else:
                held.fill(name, saved[name])

        def done(name):
            copier.send(held[name], places[name])

        gradient = held[G_IN][...].astype(jnp.float32)
        backward_feed(gradient, lines, held, vec_out, offs_out, done)
        backward_rest(lines, held, vec_out, done)
        copier.finish()


def backward_block(flag, gradient, lines, packs, layout, saved, terms):
    rows, features = gradient.shape
    hidden_size = saved[SLOPE].shape[-1]
    sizes = rows, features, hidden_size
    result = pl.pallas_call(
        functools.partial(backward_kernel, layout, len(packs)),
        out_shape=[
            jax.ShapeDtypeStruct((8, features), jnp.float32),
            jax.ShapeDtypeStruct((1, hidden_size), jnp.float32),
        ]
        + outputs_of(TERMS, *sizes),
        in_specs=[SMEM, VMEM] + [ANY] * (1 + len(packs) + len(BACK_SAVED) + len(TERMS)),
        out_specs=[VMEM] * 2 + [ANY] * len(TERMS),
        scratch_shapes=scratch_of(NAMES + BACK_SAVED + BACK_HELD + (G_IN,), *sizes)
        + [pltpu.SemaphoreType.DMA((1 + len(layout) + len(BACK_SAVED) + len(TERMS),))],
        **params(
            len(TERMS), 3 + len(packs) + len(BACK_SAVED), 2, block_flops(*sizes)
        ),
    )(
        flag,
        lines,
        gradient,
        *packs,
        *[saved[name] for name in BACK_SAVED],
        *[terms[name] for name in TERMS],
    )
    return result[:2], dict(zip(TERMS, result[2:]))


FEED_SAVED = (HAT2, STATS, SLOPE)
FEED_TERMS = (DBRANCH, DUPWARD)


def feed_kernel(layout, pack_count, *refs):
    (flag, core, lines, g_hbm), packs, saved, _, operands, outs, sums, refs = taken(
        refs, 4, pack_count, len(FEED_SAVED), len(FEED_TERMS), 3, 5, 4
    )
    act0, act1, branch0 = operands
    vec_out, offs_out, total_out, branch_out, upward_out = outs
    names = (CONTRACT,) + FEED_SAVED + FEED_TERMS + (TOTAL, G_IN)
    buffers, (act, branch, pieces, sems, in_sems, out_sems) = taken(refs, len(names))
    places = {DBRANCH: branch_out, DUPWARD: upward_out}
    first_copies, first_arrive = load_pairs(
        (act0, act1, branch0, branch_out), (act, branch), branch.shape[1], in_sems
    )

    @pl.when(flag[0] == 1)
    def _():
        copier = Copier(sems)
        held = Held(names, buffers, copier)
        held.fill(G_IN, g_hbm)
        held.fill(HAT2, saved[0])
        held.fill(STATS, saved[1])
        held.fill_weight(CONTRACT, layout, packs)
        held.fill(SLOPE, saved[2])

        def done(name):
            copier.send(held[name], places[name])

        vec_out[...] = jnp.zeros_like(vec_out)
        gradient = held[G_IN][...].astype(jnp.float32)
        backward_feed(gradient, lines, held, vec_out, offs_out, done)
        copier.send(held[TOTAL], total_out)
        copier.finish()

    contract_products(core, sums, act, branch, pieces, first_copies, first_arrive, out_sems)


def feed_block(flag, core, gradient, lines, packs, layout, saved, terms, operands):
    rows, features = gradient.shape
    hidden_size = saved[SLOPE].shape[-1]
    sizes = rows, features, hidden_size
    names = (TOTAL,) + FEED_TERMS
    groups = hidden_size // features
    blocks = features // BLOCK
    bf16 = jnp.bfloat16
    result = pl.pallas_call(
        functools.partial(feed_kernel, layout, len(packs)),
        out_shape=[
            jax.ShapeDtypeStruct((8, features), jnp.float32),
            jax.ShapeDtypeStruct((1, hidden_size), jnp.float32),
        ]
        + outputs_of(names, *sizes)
        + sum_shapes(2 * features, 2 * features),
        in_specs=[SMEM] * 2
        + [VMEM]
        + [ANY] * (1 + len(packs) + len(FEED_SAVED) + len(FEED_TERMS) + len(operands)),
        out_specs=[VMEM] * 2 + [ANY] * (len(names) + 4),
        scratch_shapes=scratch_of(
            (CONTRACT,) + FEED_SAVED + FEED_TERMS + (TOTAL, G_IN), *sizes
        )
        + [
            pltpu.VMEM((2 * rows, width), bf16)
            for width in (hidden_size, features)
        ]
        + [
            pltpu.VMEM((groups, 2, blocks // 2 // groups, BLOCK, hidden_size), bf16),
            pltpu.SemaphoreType.DMA((1 + len(layout) + len(FEED_SAVED) + len(names),)),
            pltpu.SemaphoreType.DMA((4, groups)),
            pltpu.SemaphoreType.DMA((groups, groups, 2)),
        ],
        **params(
            len(FEED_TERMS),
            4 + len(packs) + len(FEED_SAVED),
            3,
            block_flops(*sizes),
        ),
    )(
        flag,
        core,
        lines,
        gradient,
        *packs,
        *[saved[name] for name in FEED_SAVED],
        *[terms[name] for name in FEED_TERMS],
        *operands,
    )
    return result[:2], dict(zip(names, result[2:])), result[5:]


REST_IN = (DUPWARD, TOTAL, HAT1, STATS, MIX, PROBS)
REST_ORDER = (DUPWARD, EXPAND, TOTAL, HAT1, STATS, OUT, MIX, PROBS, PROJ)
REST_TERMS = (TOTAL, DOUTPUT, DMIX)


REST_WEIGHTS = (PROJ, OUT, EXPAND)


def closing_kernel(plan, layout, pack_count, *refs):
    (flag, core, lines), parts, packs, sources, _, operands, terms, outs, refs = taken(
        refs, 3, 8, pack_count, len(REST_IN), len(REST_TERMS), 6, len(REST_TERMS), 4
    )
    names = REST_WEIGHTS + REST_IN + (DOUTPUT, DMIX, DATT)
    held_buffers, buffers, (vec, sems, *scratch) = taken(refs, len(names), 4)
    places = dict(zip(REST_TERMS, terms))
    sources = dict(zip(REST_IN, sources))

    @pl.when(flag[0] == 1)
    def _():
        copier = Copier(sems)
        held = Held(names, held_buffers, copier)
        for name in REST_ORDER:
            if name in NAMES:
                held.fill_weight(name, layout, packs)
            else:
                held.fill(name, sources[name])

        def done(name):
            copier.send(held[name], places[name])

        vec[...] = jnp.zeros_like(vec)
        backward_rest(lines, held, vec, done)
        copier.finish()

    att0, att1, dout0, x0, x1, dmix0 = operands
    pairs = (att0, att1, dout0, places[DOUTPUT], x0, x1, dmix0, places[DMIX])
    own = (parts[4], parts[5], vec, parts[6], parts[7])
    row_products(plan, core, (flag, tuple(parts[:4]) + own), pairs, outs, buffers, *scratch)


def closing_block(plan, flag, core, lines, parts, packs, layout, saved, feed, terms, operands):
    rows, features = feed[TOTAL].shape
    sizes = rows, features, feed[DUPWARD].shape[-1]
    sources = dict(saved) | {DUPWARD: feed[DUPWARD], TOTAL: feed[TOTAL]}
    names = REST_WEIGHTS + REST_IN + (DOUTPUT, DMIX, DATT)
    pairs = [
        pltpu.VMEM((2 * rows, operand.shape[1]), jnp.bfloat16)
        for operand in (operands[0], operands[2], operands[3], operands[5])
    ]
    result = pl.pallas_call(
        functools.partial(closing_kernel, plan, layout, len(packs)),
        out_shape=outputs_of(REST_TERMS, *sizes)
        + sum_shapes(2 * features + 128, 2 * features),
        in_specs=[SMEM] * 2
        + [VMEM] * (1 + len(parts))
        + [ANY] * (len(packs) + len(REST_IN) + len(REST_TERMS) + len(operands)),
        out_specs=[ANY] * (len(REST_TERMS) + 4),
        scratch_shapes=scratch_of(names, *sizes)
        + pairs
        + [
            pltpu.VMEM((8, features), jnp.float32),
            pltpu.SemaphoreType.DMA((len(layout) + len(REST_IN) + len(REST_TERMS),)),
        ]
        + row_scratch(4, 4, features),
        **params(
            len(REST_TERMS),
            3 + len(parts) + len(packs) + len(REST_IN),
            0,
            block_flops(*sizes) * 3 // 2,
        ),
    )(
        flag,
        core,
        lines,
        *parts,
        *packs,
        *[sources[name] for name in REST_IN],
        *[terms[name] for name in REST_TERMS],
        *operands,
    )
    return dict(zip(REST_TERMS, result)), result[len(REST_TERMS) :]


def load_pairs(sources, buffers, width, sems):
    copies = {}
    for i, buffer in enumerate(buffers):
        rows = buffer.shape[0] // 2
        for column in range(0, buffer.shape[1], width):
            columns = pl.ds(column, width)
            for half in range(2):
                copies.setdefault((i, column), []).append(
                    pltpu.make_async_copy(
                        sources[2 * i + half].at[:, columns],
                        buffer.at[pl.ds(half * rows, rows), columns],
                        sems.at[2 * i + half, column // width],
                    )
                )
    waited = set()

    def arrive(which, column):
        if (which, column) not in waited:
            waited.add((which, column))
            for copy in copies[which, column]:
                copy.wait()

    return copies, arrive


def contract_products(core, outs, act, grad, pieces, copies, arrive, out_sems):
    features = grad.shape[1]
    groups = act.shape[1] // features
    span = outs[0].shape[-1] // features
    for which in [(1, 0)] + [(0, part * features) for part in range(groups)]:
        for copy in copies[which]:
            copy.start()
    arrive(1, 0)
    sends = []
    for part in range(groups):
        columns = pl.ds(part * features, features)
        arrive(0, part * features)
        piece = dot_tn(act[:, columns], grad[...]).astype(jnp.bfloat16)
        for block in range(4):
            for group in range(groups):
                lanes = slice(group * features, (group + 1) * features)
                at = (block * groups + group) * BLOCK
                pieces[part, block % 2, block // 2, :, lanes] = piece[at : at + BLOCK]
        for target in range(groups // span):
            for side in range(2):
                lanes = pl.ds(target * span * features, span * features)
                copy = pltpu.make_async_copy(
                    pieces.at[part, core[0] ^ side, :, :, lanes],
                    outs[2 * target + side].at[:, part % 2, part // 2],
                    out_sems.at[part, target, side],
                )
                copy.start()
                sends.append(copy)
    for copy in sends:
        copy.wait()


def vector_columns(flag, parts, target):
    turned, own, _ = taken(parts, 4, 5)
    chosen = flag[0] == 1
    vec = jnp.where(chosen, own[0][...] + own[1][...] + own[2][...], turned[0][...] + turned[1][...])
    marks = jnp.where(chosen, own[3][...] + own[4][...], turned[2][...] + turned[3][...])
    features = vec.shape[1]
    lane = lax.broadcasted_iota(jnp.int32, (features, 128), 1)
    column = jnp.concatenate([vec.T, jnp.zeros((features, 120), jnp.float32)], axis=1)
    marks = jnp.broadcast_to(marks, (8, marks.shape[1])).T.reshape(features // BLOCK, -1, BLOCK, 8)
    for group in range(marks.shape[1]):
        part = jnp.broadcast_to(marks[:, group].reshape(features, 8)[:, 0:1], column.shape)
        column = jnp.where(lane == 8 + group, part, column)
    coarse = column.astype(jnp.bfloat16)
    fine = pltpu.roll(column - coarse.astype(jnp.float32), 12, 1)
    both = jnp.where(lane < 12, column, jnp.where(lane < 24, fine, 0.0)).astype(jnp.bfloat16)
    for block in range(features // BLOCK):
        place = tuple((block >> level) & 1 for level in range(4))
        target[place] = both[block * BLOCK : (block + 1) * BLOCK]


def row_products(plan, core, vectors, sources, outs, buffers, pieces, small, in_sems, out_sems):
    width = pieces.shape[-1]
    copies, arrive = load_pairs(sources, buffers, width, in_sems)
    needs = [need for entry in plan for need in ((entry[0], 0), (entry[1], entry[2]))]
    for need in dict.fromkeys(needs):
        for copy in copies[need]:
            copy.start()
    sends = []

    def send(source, place, sem):
        copy = pltpu.make_async_copy(source, place, sem)
        copy.start()
        sends.append(copy)

    if vectors:
        vector_columns(*vectors, small)
        for side in range(2):
            place = outs[side].at[:, :, :, :, pl.ds(outs[side].shape[-1] - 128, 128)]
            send(small.at[core[0] ^ side], place, out_sems.at[len(plan), side])
    for part, (left, right, column, target, to) in enumerate(plan):
        arrive(left, 0)
        arrive(right, column)
        piece = dot_tn(buffers[left][...], buffers[right][:, column : column + width])
        piece = piece.astype(jnp.bfloat16)
        for block in range(piece.shape[0] // BLOCK):
            place = tuple((block >> level) & 1 for level in range(4))
            pieces[(part,) + place] = piece[block * BLOCK : (block + 1) * BLOCK]
        for side in range(2):
            place = outs[2 * target + side].at[:, :, :, :, pl.ds(to, width)]
            send(pieces.at[part, core[0] ^ side], place, out_sems.at[part, side])
    for copy in sends:
        copy.wait()


def row_scratch(parts, pairs, features):
    return [
        pltpu.VMEM((parts, 2, 2, 2, 2, BLOCK, features), jnp.bfloat16),
        pltpu.VMEM((2, 2, 2, 2, BLOCK, 128), jnp.bfloat16),
        pltpu.SemaphoreType.DMA((2 * pairs, 4)),
        pltpu.SemaphoreType.DMA((parts + 1, 2)),
    ]


def sum_shapes(*widths):
    return [
        jax.ShapeDtypeStruct((2, 2, 2, BLOCK, width), jnp.bfloat16)
        for width in widths
        for _ in range(2)
    ]


def rows_kernel(plan, count, core, *refs):
    sources, outs, buffers, scratch = taken(refs, 2 * count, len(refs) - 3 * count - 4, count)
    row_products(plan, core, (), sources, outs, buffers, *scratch)


def rows_block(plan, core, operands, *widths):
    rows, features = operands[0].shape
    count = len(operands) // 2
    return pl.pallas_call(
        functools.partial(rows_kernel, plan, count),
        out_shape=sum_shapes(*widths),
        in_specs=[SMEM] + [ANY] * len(operands),
        out_specs=[ANY] * (2 * len(widths)),
        scratch_shapes=[
            pltpu.VMEM((2 * rows, operand.shape[1]), jnp.bfloat16) for operand in operands[::2]
        ]
        + row_scratch(len(plan), count, features),
        **params(0, 0, 0, 4 * len(plan) * features * features * 512),
    )(core, *operands)


def pack_kernel(plan, *refs):
    target = refs[-1]
    for source, row, column, width, place in plan:
        block = refs[source][0, row : row + target.shape[0], column : column + width]
        target[:, place : place + width] = block


def packed(arrays, pieces, rows):
    width = sum(piece[3] for piece in pieces)
    if rows % 16:
        return jnp.concatenate(
            [arrays[i][0, r : r + rows, c : c + w] for i, r, c, w in pieces], axis=1
        )
    plan, place = [], 0
    for piece in pieces:
        plan.append(piece + (place,))
        place += piece[3]
    return pl.pallas_call(
        functools.partial(pack_kernel, tuple(plan)),
        out_shape=jax.ShapeDtypeStruct((rows, width), jnp.bfloat16),
        in_specs=[VMEM] * len(arrays),
        out_specs=VMEM,
    )(*arrays)


def refold(columns, shards_of, features):
    rows = features // shards_of
    if rows == BLOCK:
        return columns
    natural = jnp.moveaxis(columns.reshape(shards_of, rows, -1, features), 2, 1)
    natural = natural.reshape(features // BLOCK, -1, BLOCK, features)
    return jnp.moveaxis(natural, 1, 2).reshape(features, -1)


def unfold(blocks, shards_of, features):
    rows = features // shards_of
    if rows == BLOCK:
        return blocks
    natural = jnp.moveaxis(blocks.reshape(features // BLOCK, BLOCK, -1, features), 2, 1)
    natural = natural.reshape(shards_of, -1, rows, features)
    return jnp.moveaxis(natural, 1, 2).reshape(shards_of, rows, -1)


def swapped(block, level):
    route = [(i, i ^ (1 << level)) for i in range(lax.axis_size(DP))]
    return lax.ppermute(block, DP, route)


def added(first, second):
    return (first.astype(jnp.float32) + second.astype(jnp.float32)).astype(jnp.bfloat16)


def tied(value, *others):
    return lax.optimization_barrier((value,) + others)[0]


def bit(level):
    return (lax.axis_index(DP) >> level) & 1


def by_bits(block, levels):
    block = block.reshape((2,) * levels + block.shape[1:])
    return jnp.transpose(block, tuple(range(levels))[::-1] + tuple(range(levels, block.ndim)))


def outgoing(block, level):
    return lax.dynamic_index_in_dim(block, 1 - bit(level), 0, keepdims=False)


def joined(state, got, level, after=()):
    block = state[0]
    if isinstance(block, tuple):
        keep = block[0]
    else:
        keep = lax.dynamic_index_in_dim(block, tied(bit(level), *after), 0, keepdims=False)
    total = added(keep, got)
    if level + 1 == lax.axis_size(DP).bit_length() - 1:
        return total, total
    return total, outgoing(total, level + 1)


def halved(state, level):
    return joined(state, swapped(state[1], level), level)


def first_state(keep, send, shards_of, features, contracted, small):
    levels = shards_of.bit_length() - 1
    if features == BLOCK * shards_of:
        return (keep,), send
    blocks = jnp.transpose(jnp.stack([keep, send]), (3, 2, 1, 0, 4, 5))
    blocks = blocks.reshape((-1,) + blocks.shape[4:])
    if contracted:
        blocks = unfold(blocks, shards_of, features)
    else:
        blocks = blocks.reshape(shards_of, features // shards_of, -1)
    if small:
        lines = blocks[:, :, 2 * features :].reshape(features, 128)
        marks = jnp.stack([lines[:, 8:12], lines[:, 20:24]]).reshape(2, -1, BLOCK, 4)
        marks = jnp.moveaxis(marks, 3, 2).reshape(2, shards_of, 4, -1)
        marks = jnp.moveaxis(marks, 2, 3).reshape(2, features, 4)
        lines = jnp.concatenate([lines[:, :8], marks[0], lines[:, 12:20], marks[1]], axis=1)
        lines = jnp.pad(lines, ((0, 0), (0, 104))).reshape(shards_of, -1, 128)
        blocks = jnp.concatenate([blocks[:, :, : 2 * features], lines], axis=2)
    blocks = by_bits(blocks, levels)
    return blocks, outgoing(blocks, 0)


def doubled(block, level, other):
    upper = bit(level) == 1
    return jnp.concatenate(
        [jnp.where(upper, other, block), jnp.where(upper, block, other)], axis=0
    )


def shards(
    inputs,
    keep_mask,
    lengths,
    slot_order,
    cotangent,
    query_projection,
    query_output,
    query_expand,
    query_contract,
    query_gains,
    query_biases,
    query_offsets,
    momentum_projection,
    momentum_output,
    momentum_expand,
    momentum_contract,
    momentum_gains,
    momentum_biases,
    momentum_offsets,
):
    first_section = lax.axis_index(SECTION) == 0
    shards_of = lax.axis_size(DP)
    crop_count, crop_len, features = inputs.shape[1:]
    rows = features // shards_of
    hidden_size = query_expand.shape[2]
    groups = hidden_size // features
    blocks = features // BLOCK

    def folded(which):
        return [(which, i * rows, 0, features) for i in range(groups)]

    late_from, late_to = 2 * features // 3, 2 * features
    own = packed(
        (query_projection, query_output, query_expand, query_contract)
        + (momentum_output, momentum_projection),
        [(0, 0, 0, 3 * features), (1, 0, 0, features), (2, 0, 0, hidden_size)]
        + folded(3)
        + [(4, 0, 0, features), (5, 0, late_from, late_to - late_from)],
        rows,
    )
    gathered = lax.all_gather(own, DP, axis=0, tiled=True)
    rest = packed(
        (tied(momentum_projection, own), momentum_expand, momentum_contract),
        [(0, 0, 0, late_from), (0, 0, late_to, 3 * features - late_to), (1, 0, 0, hidden_size)]
        + folded(2),
        rows,
    )
    late = lax.all_gather(rest, DP, axis=0, tiled=True)

    sizes = (2 * rows, 6 * rows, groups * rows)
    vectors = jnp.concatenate(
        [
            array[0].reshape(-1)
            for array in (
                query_gains,
                query_biases,
                query_offsets,
                momentum_gains,
                momentum_biases,
                momentum_offsets,
            )
        ]
    )[None]
    levels = shards_of.bit_length() - 1
    for level in range(levels):
        vectors = doubled(vectors, level, swapped(vectors, level))
    vectors = vectors.astype(jnp.float32)

    def vector_rows(start):
        lines = vectors[:, start : start + 8 * rows].reshape(shards_of, 8, rows)
        marks = vectors[:, start + 8 * rows : start + sum(sizes)]
        return jnp.moveaxis(lines, 1, 0).reshape(8, features), marks.reshape(1, hidden_size)

    query_lines, query_offs = vector_rows(0)
    momentum_lines, momentum_offs = vector_rows(sum(sizes))

    inner = 4 * features + hidden_size
    vectors_at = inner + groups * features
    if rows != BLOCK:
        gathered = jnp.concatenate(
            [
                gathered[:, :inner],
                refold(gathered[:, inner:vectors_at], shards_of, features),
                gathered[:, vectors_at:],
            ],
            axis=1,
        )
        late_end = late.shape[1] - groups * features
        late = jnp.concatenate(
            [late[:, :late_end], refold(late[:, late_end:], shards_of, features)], axis=1
        )
    gathered = gathered.reshape(blocks, BLOCK, -1)
    late = late.reshape(blocks, BLOCK, -1)
    query_layout = (
        (PROJ, 0, 0, 3 * features, 0),
        (OUT, 0, 3 * features, features, 0),
        (EXPAND, 0, 4 * features, hidden_size, 0),
        (CONTRACT, 0, inner, hidden_size, 0),
    )
    late_expand = 3 * features - (late_to - late_from)
    momentum_layout = (
        (PROJ, 0, vectors_at + features, late_to - late_from, late_from),
        (PROJ, 1, 0, late_from, 0),
        (PROJ, 1, late_from, 3 * features - late_to, late_to),
        (OUT, 0, vectors_at, features, 0),
        (EXPAND, 1, late_expand, hidden_size, 0),
        (CONTRACT, 1, late_expand + hidden_size, hidden_size, 0),
    )

    positions = lax.broadcasted_iota(jnp.int32, keep_mask.shape, 2)
    validity = ((positions < lengths[:, :, None]) & ((keep_mask > 0) | (positions == 0))).astype(
        jnp.float32
    )
    across = validity[:, :, None, :]
    down = validity[:, :, :, None]
    in_first = first_section.astype(jnp.int32).reshape(1)
    in_second = 1 - in_first

    def momentum_forward(flag, block_in):
        return forward_block(
            flag,
            block_in,
            across,
            down,
            momentum_lines,
            momentum_offs,
            (gathered, late),
            momentum_layout,
            False,
            1,
            0,
            crop_count,
        )[:2]

    crops = range(crop_count)
    last = crop_count - 1
    started, turned, before = [], [], [momentum_lines, momentum_offs]
    for c in crops:
        started.append(
            forward_block(
                tied(in_first, *before),
                inputs,
                across,
                down,
                query_lines,
                query_offs,
                (gathered,),
                query_layout,
                True,
                0,
                c,
                1,
            )
        )
        before = [started[c][1]]
    passed = [lax.ppermute(started[c][0], SECTION, [(0, 1)]) for c in crops]
    for c in crops:
        turned.append(
            turn_block(
                tied(in_second, *before),
                passed[c],
                cotangent,
                across,
                down,
                query_lines,
                query_offs,
                (gathered,),
                query_layout,
                c,
                started[c][2],
            )
        )
        before = [turned[c][0][0]]
    returned = [lax.ppermute(turned[c][0][3], SECTION, [(1, 0)]) for c in crops]
    ended = [
        backward_block(
            in_first,
            returned[c],
            query_lines,
            (gathered,),
            query_layout,
            started[c][2],
            turned[c][1],
        )
        for c in crops[:last]
    ]
    core = lax.axis_index(DP) & 1 if rows == BLOCK else jnp.int32(0)
    core = jnp.asarray(core, jnp.int32).reshape(1)
    outer = [turned[c][1] | ended[c][1] for c in crops[:last]]

    def operands(name, *ends):
        return [end[name] for end in ends or outer + [turned[last][1]]]

    feed_ends, feed_terms, sums = feed_block(
        tied(in_first, *[end[0][0] for end in ended]),
        core,
        returned[last],
        query_lines,
        (gathered,),
        query_layout,
        started[last][2],
        turned[last][1],
        operands(ACT) + operands(DBRANCH, *outer),
    )
    ends = outer + [turned[last][1] | feed_terms]

    def pairs(sums, contracted=False, small=False):
        return [
            first_state(
                sums[2 * i], sums[2 * i + 1], shards_of, features, contracted, small and not i
            )
            for i in range(len(sums) // 2)
        ]

    chunks = pairs(sums, True)
    first = [swapped(chunk[1], 0) for chunk in chunks]
    sums = rows_block(
        tuple((0, 1, i * features, i // 2, i % 2 * features) for i in range(groups)),
        tied(core, feed_ends[0]),
        operands(LOW) + [end[DUPWARD] for end in ends],
        2 * features,
        2 * features,
    )
    chunks += pairs(sums)
    *first, _ = lax.optimization_barrier((*first, sums[0]))
    half = groups // 2
    level_of = [0] * 6

    key_pools, key_ways = [], []

    def advance(i, got, after=()):
        chunks[i] = joined(chunks[i], got, level_of[i], after)
        level_of[i] += 1

    def wide(parts):
        return jnp.concatenate(parts, axis=1).astype(jnp.float32)

    def finished():
        contract_sum = jnp.moveaxis(
            wide([chunk[0] for chunk in chunks[:half]]).reshape(rows, groups, features), 1, 0
        )
        last_columns = chunks[4][0]
        small = last_columns[:, half * features :].astype(jnp.float32)
        small = (small[:, :12] + small[:, 12:24]).T
        return (
            last_columns[None, :, :features].astype(jnp.float32),
            wide([chunk[0] for chunk in chunks[half : 2 * half]])[None],
            contract_sum.reshape(1, groups * rows, features),
            small[None, :2],
            small[None, 2:8],
            small[8:].reshape(1, groups * rows),
        )

    def step(moving, *kernels, passing=()):
        gots = [swapped(chunks[i][1], level_of[i]) for i in moving]
        before = tuple(chunks[i][1] for i in moving)
        for kernel in kernels:
            before = (kernel(*before),)
        passing = [way() for way in passing]
        *gots, done = lax.optimization_barrier((*gots, *passing, *before[:1]))
        for i, got in zip(moving, gots):
            advance(i, got)
        return gots[len(moving) :], done

    def closing(*before):
        turned_parts = [turned[c][0][1] for c in crops] + [turned[c][0][2] for c in crops]
        own_parts = [ended[0][0][0], feed_ends[0], ended[0][0][1], feed_ends[1]]
        terms, sums = closing_block(
            (
                (0, 1, 0, 0, 0),
                (2, 3, 0, 0, features),
                (2, 3, features, 1, 0),
                (2, 3, 2 * features, 1, features),
            ),
            tied(in_first, *before),
            core,
            query_lines,
            turned_parts + own_parts,
            (gathered,),
            query_layout,
            started[last][2],
            feed_terms,
            turned[last][1],
            operands(ATT) + operands(DOUTPUT, *outer) + operands(X_IN) + operands(DMIX, *outer),
        )
        ends[last] = ends[last] | terms
        chunks.extend(pairs(sums, False, True))
        return sums[2]

    def key_first(*before):
        key_out, pool = momentum_forward(tied(in_first, *before), inputs)
        key_ways.append(lax.ppermute(key_out, SECTION, [(0, 1)]))
        key_pools.append(pool)
        return pool

    def key_second(*before):
        return momentum_forward(tied(in_second, *before), key_ways[0])[1]

    def unfinished(*second):
        return [
            i
            for i in range(len(chunks))
            if level_of[i] < levels and (level_of[i] != 1 or i in second)
        ]

    for i, got in enumerate(first):
        advance(i, got)
    for i in (2, 3):
        advance(i, swapped(chunks[i][1], 0))
    step([0, 1], key_first)
    both = (lambda: swapped(chunks[4][1], 0), lambda: swapped(chunks[5][1], 0))
    gots, done = step(unfinished(2, 3), closing, key_second, passing=both)
    for i, got in zip((4, 5), gots):
        advance(i, got)

    key_pool = jnp.where(first_section, key_pools[0], done)
    pools = [jnp.where(first_section, started[c][1], turned[c][0][0]) for c in crops]
    pooled = jnp.concatenate([jnp.concatenate(pools, axis=0)[:, None], key_pool[:, None]], axis=1)
    order = (slot_order[:, None] == jnp.arange(crop_count, dtype=jnp.int32)[None, :])[..., None]
    pooled = jnp.sum(jnp.where(order, pooled.reshape(crop_count, -1)[None], 0.0), axis=1)
    ways = [0] + list(range(2, levels)) + [1]
    pooled = pooled[None]
    moves = [(4, 2, 3), (5, 4, 0, 1), (5, 4, 2, 3), (5,)]
    for way, moving in zip(ways, moves + [()] * (levels - len(moves))):
        gots = [swapped(chunks[i][1], level_of[i]) for i in moving]
        *gots, other = lax.optimization_barrier((*gots, swapped(pooled, way)))
        for i, got in zip(moving, gots):
            advance(i, got, finished() if moving == (5,) and level_of[4] == levels else ())
        pooled = doubled(pooled, way, other)
    for i in range(6):
        while level_of[i] < levels:
            advance(i, swapped(chunks[i][1], level_of[i]))
    pooled = pooled.reshape((2,) * levels + (crop_count, 2, features))
    axes = sorted(range(levels), key=lambda j: -ways[levels - 1 - j])
    pooled = jnp.transpose(pooled, tuple(axes) + tuple(range(levels, levels + 3)))
    pooled = jnp.moveaxis(pooled.reshape(-1, 2, features), 1, 0)[None]
    grad_input = jnp.stack([tied(end[TOTAL], done) for end in ends])[None]
    first_features, *others = finished()
    project_sum = wide([chunks[4][0][:, features : half * features], chunks[5][0]])
    return (pooled, grad_input, project_sum[None], first_features, *others)


def solution(mesh):
    in_specs = (
        P(None, DP, None, None),
        P(None, DP, None),
        P(None, DP),
        P(DP),
        P(DP, None, None),
        P(SECTION, DP, None),
        P(SECTION, DP, None),
        P(SECTION, DP, None),
        P(SECTION, DP, None),
        P(SECTION, None, DP),
        P(SECTION, None, DP),
        P(SECTION, DP),
        P(SECTION, DP, None),
        P(SECTION, DP, None),
        P(SECTION, DP, None),
        P(SECTION, DP, None),
        P(SECTION, None, DP),
        P(SECTION, None, DP),
        P(SECTION, DP),
    )
    out_specs = (
        P(SECTION, None, None, None),
        P(SECTION, DP, None, None),
        P(SECTION, DP, None),
        P(SECTION, DP, None),
        P(SECTION, DP, None),
        P(SECTION, DP, None),
        P(SECTION, None, DP),
        P(SECTION, None, DP),
        P(SECTION, DP),
    )
    return jax.shard_map(shards, mesh=mesh, in_specs=in_specs, out_specs=out_specs, check_vma=False)
```

```python
import functools

import jax
import jax.numpy as jnp
from jax import lax
from jax.experimental import pallas as pl
from jax.experimental.pallas import tpu as pltpu
from jax.sharding import PartitionSpec as P

DP, SECTION = "dp", "section"
HD = 64
BLOCK = 48
VMEM_LIMIT = 56 * 1024 * 1024

epsilon = 1e-12
SCALE = HD ** (-0.5)

ANY = pl.BlockSpec(memory_space=pl.ANY)
VMEM = pl.BlockSpec(memory_space=pltpu.VMEM)
SMEM = pl.BlockSpec(memory_space=pltpu.SMEM)


def dot_nn(a, b):
    return jnp.dot(a, b, preferred_element_type=jnp.float32)


def dot_nt(a, b):
    return lax.dot_general(a, b, (((1,), (1,)), ((), ())), preferred_element_type=jnp.float32)


def dot_tn(a, b):
    return lax.dot_general(a, b, (((0,), (0,)), ((), ())), preferred_element_type=jnp.float32)


def gelu_parts(values):
    size = jnp.abs(values)
    inverse = pl.reciprocal(1.0 + (0.3275911 * 0.5**0.5) * size, approx=True)
    series = 0.5 * 1.061405429
    for factor in (-1.453152027, 1.421413741, -0.284496736, 0.254829592):
        series = series * inverse + 0.5 * factor
    bell = jnp.exp(-0.5 * (values * values))
    tail = series * inverse * bell
    phi = jnp.where(values >= 0, 1.0 - tail, tail)
    return values * phi, phi + values * bell * 0.3989422804014327


def normalised(values):
    centred = values - jnp.mean(values, axis=-1, keepdims=True)
    variance = jnp.mean(centred * centred, axis=-1, keepdims=True)
    scale = lax.rsqrt(variance + epsilon)
    return centred * scale, scale


(
    PROJ,
    OUT,
    EXPAND,
    CONTRACT,
    MIX,
    PROBS,
    HAT1,
    HAT2,
    SLOPE,
    STATS,
    ATT,
    LOW,
    ACT,
    TOTAL,
    DBRANCH,
    DUPWARD,
    DOUTPUT,
    DMIX,
    DATT,
    X_IN,
    G_IN,
    SUMS,
) = range(22)
NAMES = (PROJ, OUT, EXPAND, CONTRACT)
SAVED = (MIX, PROBS, HAT1, HAT2, SLOPE, STATS, ATT, LOW, ACT)
UNROLL = 3
TERMS = (TOTAL, DBRANCH, DUPWARD, DOUTPUT, DMIX)


def flat(block):
    return block.reshape(-1, block.shape[-1])


def shape_of(name, rows, features, hidden_size):
    blocks = features // BLOCK
    bf16, f32 = jnp.bfloat16, jnp.float32
    return {
        PROJ: ((blocks, BLOCK, 3 * features), bf16),
        OUT: ((blocks, BLOCK, features), bf16),
        EXPAND: ((blocks, BLOCK, hidden_size), bf16),
        CONTRACT: ((blocks, BLOCK, hidden_size), bf16),
        MIX: ((rows, 3 * features), bf16),
        PROBS: ((features // HD, rows, rows), bf16),
        STATS: ((rows, 128), f32),
        ACT: ((rows, hidden_size), bf16),
        SLOPE: ((rows, hidden_size), bf16),
        DUPWARD: ((rows, hidden_size), bf16),
        DMIX: ((rows, 3 * features), bf16),
        TOTAL: ((rows, features), f32),
        SUMS: ((rows, features), f32),
    }.get(name, ((rows, features), bf16))


def scratch_of(names, *sizes):
    return [pltpu.VMEM(*shape_of(name, *sizes)) for name in names]


def outputs_of(names, *sizes):
    return [jax.ShapeDtypeStruct(*shape_of(name, *sizes)) for name in names]


class Copier:
    def __init__(self, sems):
        self.sems, self.count, self.open = sems, 0, []

    def fetch(self, source, place):
        copy = pltpu.make_async_copy(source, place, self.sems.at[self.count])
        self.count += 1
        copy.start()
        return copy

    def send(self, source, place):
        self.open.append(self.fetch(source, place))

    def finish(self):
        for copy in self.open:
            copy.wait()


class Held:
    def __init__(self, names, buffers, copier, once=None):
        self.buffers, self.pending, self.copier = dict(zip(names, buffers)), {}, copier
        self.once = once

    def fill(self, name, source):
        self.pending[name] = [self.copier.fetch(source, self.buffers[name])]

    def fill_weight(self, wanted, layout, packs):
        buffer = self.buffers[wanted]
        for name, pack, source, width, target in layout:
            if name == wanted:
                block = packs[pack].at[:, :, pl.ds(source, width)]
                place = buffer.at[:, :, pl.ds(target, width)]
                self.pending.setdefault(name, []).append(self.copier.fetch(block, place))

    def __contains__(self, name):
        return name in self.buffers

    def __getitem__(self, name):
        copies = self.pending.pop(name, ())

        def wait():
            for copy in copies:
                copy.wait()

        if copies and self.once is not None:
            pl.when(self.once)(wait)
        else:
            wait()
        return self.buffers[name]


def unfolded(block, features):
    return jnp.concatenate(
        [
            block[i, :, at : at + features]
            for i in range(block.shape[0])
            for at in range(0, block.shape[2], features)
        ],
        axis=0,
    )


def two_heads(pair, head_low):
    zero = jnp.zeros_like(pair)
    return jnp.concatenate(
        [jnp.where(head_low, pair, zero), jnp.where(head_low, zero, pair)], axis=0
    )


def merged_heads(stacked, head_low):
    rows = stacked.shape[0] // 2
    return jnp.where(head_low, stacked[:rows], stacked[rows:])


def low_lanes(rows):
    return lax.broadcasted_iota(jnp.int32, (rows, 2 * HD), 1) < HD


def forward_rows(x, validity, lines, offs, held, done, during=None):
    rows, features = x.shape
    saving = PROBS in held
    mix, att, low = held[MIX], held[ATT], held[LOW]
    shift = jnp.concatenate([lines[2:3, :], jnp.zeros((1, features), jnp.float32), lines[3:4, :]], axis=1)
    mix[...] = (dot_nn(x, flat(held[PROJ][...])) + shift).astype(jnp.bfloat16)
    done(MIX)
    head_low = low_lanes(rows)
    valid = jnp.broadcast_to(validity > 0, (2 * rows, rows))

    def pair_step(pair, _):
        at = pl.multiple_of(pair * 2 * HD, 2 * HD)
        q = mix[:, pl.ds(at, 2 * HD)] * jnp.asarray(SCALE, jnp.bfloat16)
        k = mix[:, pl.ds(features + at, 2 * HD)]
        v = mix[:, pl.ds(2 * features + at, 2 * HD)]
        scores = jnp.where(valid, dot_nt(two_heads(q, head_low), k), -1e30)
        top = jnp.max(scores, axis=-1, keepdims=True)
        weight = jnp.exp(scores - top)
        share = 1.0 / jnp.sum(weight, axis=-1, keepdims=True)
        if saving:
            weight = (weight * share).astype(jnp.bfloat16)
            held[PROBS][pl.ds(2 * pair, 2)] = weight.reshape(2, rows, rows)
            mixed = dot_nn(weight, v)
        else:
            mixed = dot_nn(weight.astype(jnp.bfloat16), v) * share
        att[:, pl.ds(at, 2 * HD)] = merged_heads(mixed, head_low).astype(jnp.bfloat16)

    lax.fori_loop(0, features // (2 * HD), pair_step, None, unroll=UNROLL)
    done(PROBS)
    done(ATT)
    total = x.astype(jnp.float32) + dot_nn(att[...], flat(held[OUT][...]))
    hat, scale = normalised(total + lines[4:5, :])
    hidden = hat * lines[0:1, :] + lines[5:6, :]
    low[...] = hidden.astype(jnp.bfloat16)
    if saving:
        held[HAT1][...] = hat.astype(jnp.bfloat16)
        held[STATS][:, 0:1] = scale
    done(LOW)
    done(HAT1)
    halves = 2
    span = offs.shape[1] // halves
    expand, contract = held[EXPAND], held[CONTRACT]
    stack = contract.shape[0] // halves
    sums = held[SUMS]
    sums[...] = hidden + lines[6:7, :]

    def feed_step(half, _):
        columns = pl.ds(pl.multiple_of(half * span, span), span)
        upward = dot_nn(low[...], flat(expand[:, :, columns]))
        value, gradient = gelu_parts(upward + offs[:, columns])
        value = value.astype(jnp.bfloat16)
        if saving:
            held[ACT][:, columns] = value
            held[SLOPE][:, columns] = gradient.astype(jnp.bfloat16)
        if during is not None:
            during(half, columns)
        sums[...] += dot_nn(value, unfolded(contract[pl.ds(half * stack, stack)], features))

    lax.fori_loop(0, halves, feed_step, None)
    total = sums[...]
    done(ACT)
    done(SLOPE)
    hat, scale = normalised(total)
    if saving:
        held[HAT2][...] = hat.astype(jnp.bfloat16)
        held[STATS][:, 1:2] = scale
    done(HAT2)
    done(STATS)
    return hat * lines[1:2, :] + lines[7:8, :]


def pooled_rows(value, across, down):
    total = jnp.sum(value * down, axis=0, keepdims=True)
    return total / jnp.sum(across, axis=-1, keepdims=True)


def norm_back(gradient, hat, scale, gain):
    weighted = gradient * gain
    mean = jnp.mean(weighted, axis=-1, keepdims=True)
    slant = jnp.mean(weighted * hat, axis=-1, keepdims=True)
    return scale * (weighted - mean - hat * slant)


def column_sum(vec_out, line, values):
    vec_out[line : line + 1, :] = jnp.sum(values, axis=0, keepdims=True)


def backward_feed(gradient, lines, held, vec_out, offs_out, done):
    features = gradient.shape[1]
    hat = held[HAT2][...].astype(jnp.float32)
    column_sum(vec_out, 1, gradient * hat)
    column_sum(vec_out, 7, gradient)
    moved = norm_back(gradient, hat, held[STATS][:, 1:2], lines[1:2, :])
    held[TOTAL][...] = moved
    rounded = moved.astype(jnp.bfloat16)
    held[DBRANCH][...] = rounded
    column_sum(vec_out, 6, rounded.astype(jnp.float32))
    done(DBRANCH)
    groups = offs_out.shape[1] // features
    contract = held[CONTRACT]
    stack = contract.shape[0] // groups
    for group in range(groups):
        columns = pl.ds(group * features, features)
        block = unfolded(contract[group * stack : (group + 1) * stack], features)
        dactive = dot_nt(rounded, block)
        slope = held[SLOPE][:, columns].astype(jnp.float32)
        dup = (dactive * slope).astype(jnp.bfloat16)
        held[DUPWARD][:, columns] = dup
        offs_out[:, columns] = jnp.sum(dup.astype(jnp.float32), axis=0, keepdims=True)
    done(DUPWARD)


def backward_rest(lines, held, vec_out, done):
    rows, features = held[TOTAL].shape
    gradient = held[TOTAL][...] + dot_nt(held[DUPWARD][...], flat(held[EXPAND][...]))
    hat = held[HAT1][...].astype(jnp.float32)
    column_sum(vec_out, 0, gradient * hat)
    column_sum(vec_out, 5, gradient)
    stats, datt, dmix = held[STATS], held[DATT], held[DMIX]
    moved = norm_back(gradient, hat, stats[:, 0:1], lines[0:1, :])
    held[TOTAL][...] = moved
    rounded = moved.astype(jnp.bfloat16)
    held[DOUTPUT][...] = rounded
    column_sum(vec_out, 4, rounded.astype(jnp.float32))
    done(DOUTPUT)
    datt[...] = dot_nt(rounded, flat(held[OUT][...])).astype(jnp.bfloat16)
    head_low = low_lanes(rows)
    mix, probs = held[MIX], held[PROBS]

    def pair_step(pair, _):
        at = pl.multiple_of(pair * 2 * HD, 2 * HD)
        q = mix[:, pl.ds(at, 2 * HD)]
        k = mix[:, pl.ds(features + at, 2 * HD)]
        v = mix[:, pl.ds(2 * features + at, 2 * HD)]
        pull = datt[:, pl.ds(at, 2 * HD)]
        weight = flat(probs[pl.ds(2 * pair, 2)])
        wide = weight.astype(jnp.float32)
        product = dot_nt(two_heads(pull, head_low), v) * wide
        inner = jnp.sum(product, axis=-1, keepdims=True)
        dscores = (product - wide * inner).astype(jnp.bfloat16)
        dq = merged_heads(dot_nn(dscores, k), head_low)
        dmix[:, pl.ds(at, 2 * HD)] = (dq * SCALE).astype(jnp.bfloat16)
        q_turned, pull_turned = q.T, pull.T
        dk, dv = [], []
        for side in range(2):
            lanes = slice(side * HD, (side + 1) * HD)
            part = slice(side * rows, (side + 1) * rows)
            dk.append(dot_nn(q_turned[lanes], dscores[part]))
            dv.append(dot_nn(pull_turned[lanes], weight[part]))
        dk = (jnp.concatenate(dk, axis=0) * SCALE).astype(jnp.bfloat16).T
        dv = jnp.concatenate(dv, axis=0).astype(jnp.bfloat16).T
        dmix[:, pl.ds(features + at, 2 * HD)] = dk
        dmix[:, pl.ds(2 * features + at, 2 * HD)] = dv

    lax.fori_loop(0, features // (2 * HD), pair_step, None, unroll=UNROLL)
    done(DMIX)
    column_sum(vec_out, 2, dmix[:, 0:features].astype(jnp.float32))
    column_sum(vec_out, 3, dmix[:, 2 * features : 3 * features].astype(jnp.float32))
    moved = held[TOTAL][...] + dot_nt(dmix[...], flat(held[PROJ][...]))
    held[TOTAL][...] = moved
    done(TOTAL)
    return moved


def taken(refs, *counts):
    parts, at = [], 0
    for count in counts:
        parts.append(refs[at : at + count])
        at += count
    return parts + [refs[at:]]


FORWARD_HELD = (MIX, ATT, LOW, SUMS)
PARTED = (ACT, SLOPE)


def forward_kernel(layout, pack_count, view, first, crops, save, *refs):
    names = SAVED + (SUMS,) if save else FORWARD_HELD
    (flag, vrow, vcol, lines, offs, x_hbm), packs, (y_out, pooled_out), saved, refs = taken(
        refs, 6, pack_count, 2, len(SAVED) + 1 if save else 0
    )
    buffers, (x_buf, sems) = taken(refs, len(NAMES + names))
    saved = dict(zip(SAVED, saved[1:])) | {X_IN: saved[:1]}

    @pl.when(flag[0] == 1)
    def _():
        copier = Copier(sems)
        held = Held(NAMES + names, buffers, copier)
        fetches = []
        for crop in range(crops):
            at = (view, first + crop) if len(x_hbm.shape) == 4 else (crop,)
            source = x_hbm.at[at]
            fetches.append(copier.fetch(source, x_buf.at[crop]))
        for name in NAMES:
            held.fill_weight(name, layout, packs)

        def done(name):
            if save and name not in PARTED:
                copier.send(held[name], saved[name])

        def parts(half, columns):
            return [
                pltpu.make_async_copy(
                    held[name].at[:, columns],
                    saved[name].at[:, columns],
                    sems.at[sems.shape[0] - 4 + 2 * half + i],
                )
                for i, name in enumerate(PARTED)
            ]

        def during(half, columns):
            for copy in parts(half, columns):
                copy.start()

        def one(crop, _):
            for at, fetch in enumerate(fetches):
                if crops == 1:
                    fetch.wait()
                else:
                    pl.when(crop == at)(fetch.wait)
            if save:
                copier.send(x_buf.at[crop], saved[X_IN][0])
            across = vrow[view, first + crop]
            value = forward_rows(
                x_buf[crop], across, lines, offs, held, done, during if save else None
            )
            y_out[crop] = value.astype(jnp.bfloat16)
            pooled_out[crop] = pooled_rows(value, across, vcol[view, first + crop])

        if crops == 1:
            one(0, None)
        else:

            def looped(crop, _):
                held.once = crop == 0
                one(crop, None)

            lax.fori_loop(0, crops, looped, None)
        if save:
            span = offs.shape[1] // 2
            for half in range(2):
                copier.open.extend(parts(half, pl.ds(half * span, span)))
        copier.finish()


def cost_of(flops):
    return pl.CostEstimate(flops=3 * flops, bytes_accessed=0, transcendentals=0)


def params(kept, first_in, first_out, flops):
    return dict(
        input_output_aliases={first_in + i: first_out + i for i in range(kept)},
        compiler_params=pltpu.CompilerParams(vmem_limit_bytes=VMEM_LIMIT),
        cost_estimate=cost_of(flops),
    )


def block_flops(rows, features, hidden_size):
    return 2 * rows * (4 * features * features + 2 * features * hidden_size)


def forward_block(flag, x, vrow, vcol, lines, offs, packs, layout, save, view, first, crops):
    rows, features = x.shape[-2:]
    sizes = rows, features, offs.shape[-1]
    names = (X_IN,) + SAVED if save else ()
    result = pl.pallas_call(
        functools.partial(forward_kernel, layout, len(packs), view, first, crops, save),
        out_shape=[
            jax.ShapeDtypeStruct((crops, rows, features), jnp.bfloat16),
            jax.ShapeDtypeStruct((crops, 1, features), jnp.float32),
        ]
        + outputs_of(names, *sizes),
        in_specs=[SMEM] + [VMEM] * 4 + [ANY] * (1 + len(packs)),
        out_specs=[VMEM] * 2 + [ANY] * len(names),
        scratch_shapes=scratch_of(NAMES + (SAVED + (SUMS,) if save else FORWARD_HELD), *sizes)
        + [
            pltpu.VMEM((crops, rows, features), jnp.bfloat16),
            pltpu.SemaphoreType.DMA((crops + len(layout) + len(names) + 4,)),
        ],
        **params(0, 0, 0, crops * block_flops(*sizes)),
    )(flag, vrow, vcol, lines, offs, x, *packs)
    return result[0], result[1], dict(zip(names, result[2:]))


ENDS = (ATT, LOW, ACT, X_IN)
BACK_HELD = (DBRANCH, DUPWARD, DOUTPUT, DATT, DMIX, TOTAL)


def turn_kernel(layout, pack_count, crop, *refs):
    head, packs, _, outs, ends, terms, refs = taken(
        refs, 7, pack_count, len(ENDS), 4, len(ENDS), len(TERMS)
    )
    flag, vrow, vcol, lines, offs, x_hbm, g_hbm = head
    pooled_out, vec_out, offs_out, dx_low = outs
    names = NAMES + SAVED + BACK_HELD + (SUMS, X_IN, G_IN)
    buffers, (sems,) = taken(refs, len(names))
    places = dict(zip(ENDS + TERMS, ends + terms))

    @pl.when(flag[0] == 1)
    def _():
        copier = Copier(sems)
        held = Held(names, buffers, copier)
        held.fill(X_IN, x_hbm.at[0])
        for name in NAMES:
            held.fill_weight(name, layout, packs)
        held.fill(G_IN, g_hbm.at[crop])

        def done(name):
            if name in places:
                copier.send(held[name], places[name])

        done(X_IN)
        value = forward_rows(held[X_IN][...], vrow[0, crop], lines, offs, held, done)
        pooled_out[0] = pooled_rows(value, vrow[0, crop], vcol[0, crop])
        gradient = held[G_IN][...].astype(jnp.float32) * vcol[0, crop]
        backward_feed(gradient, lines, held, vec_out, offs_out, done)
        dx_low[...] = backward_rest(lines, held, vec_out, done).astype(jnp.bfloat16)
        copier.finish()


def turn_block(flag, x, gradient, vrow, vcol, lines, offs, packs, layout, crop, saved):
    rows, features = x.shape[-2:]
    sizes = rows, features, offs.shape[-1]
    result = pl.pallas_call(
        functools.partial(turn_kernel, layout, len(packs), crop),
        out_shape=[
            jax.ShapeDtypeStruct((1, 1, features), jnp.float32),
            jax.ShapeDtypeStruct((8, features), jnp.float32),
            jax.ShapeDtypeStruct(offs.shape, jnp.float32),
            jax.ShapeDtypeStruct((rows, features), jnp.bfloat16),
        ]
        + outputs_of(ENDS + TERMS, *sizes),
        in_specs=[SMEM] + [VMEM] * 4 + [ANY] * (2 + len(packs) + len(ENDS)),
        out_specs=[VMEM] * 4 + [ANY] * len(ENDS + TERMS),
        scratch_shapes=scratch_of(NAMES + SAVED + BACK_HELD + (SUMS, X_IN, G_IN), *sizes)
        + [pltpu.SemaphoreType.DMA((2 + len(layout) + len(ENDS + TERMS),))],
        **params(len(ENDS), 7 + len(packs), 4, 2 * block_flops(*sizes)),
    )(flag, vrow, vcol, lines, offs, x, gradient, *packs, *[saved[name] for name in ENDS])
    return result[:4], dict(zip(ENDS + TERMS, result[4:]))


BACK_SAVED = (HAT2, STATS, SLOPE, HAT1, MIX, PROBS)
BACK_ORDER = (G_IN, HAT2, STATS, CONTRACT, SLOPE, EXPAND, HAT1, OUT, MIX, PROBS, PROJ)


def backward_kernel(layout, pack_count, *refs):
    (flag, lines, g_hbm), packs, saved, _, outs, terms, refs = taken(
        refs, 3, pack_count, len(BACK_SAVED), len(TERMS), 2, len(TERMS)
    )
    vec_out, offs_out = outs
    names = NAMES + BACK_SAVED + BACK_HELD + (G_IN,)
    buffers, (sems,) = taken(refs, len(names))
    places = dict(zip(TERMS, terms))
    saved = dict(zip(BACK_SAVED, saved)) | {G_IN: g_hbm}

    @pl.when(flag[0] == 1)
    def _():
        copier = Copier(sems)
        held = Held(names, buffers, copier)
        for name in BACK_ORDER:
            if name in NAMES:
                held.fill_weight(name, layout, packs)
            else:
                held.fill(name, saved[name])

        def done(name):
            copier.send(held[name], places[name])

        gradient = held[G_IN][...].astype(jnp.float32)
        backward_feed(gradient, lines, held, vec_out, offs_out, done)
        backward_rest(lines, held, vec_out, done)
        copier.finish()


def backward_block(flag, gradient, lines, packs, layout, saved, terms):
    rows, features = gradient.shape
    hidden_size = saved[SLOPE].shape[-1]
    sizes = rows, features, hidden_size
    result = pl.pallas_call(
        functools.partial(backward_kernel, layout, len(packs)),
        out_shape=[
            jax.ShapeDtypeStruct((8, features), jnp.float32),
            jax.ShapeDtypeStruct((1, hidden_size), jnp.float32),
        ]
        + outputs_of(TERMS, *sizes),
        in_specs=[SMEM, VMEM] + [ANY] * (1 + len(packs) + len(BACK_SAVED) + len(TERMS)),
        out_specs=[VMEM] * 2 + [ANY] * len(TERMS),
        scratch_shapes=scratch_of(NAMES + BACK_SAVED + BACK_HELD + (G_IN,), *sizes)
        + [pltpu.SemaphoreType.DMA((1 + len(layout) + len(BACK_SAVED) + len(TERMS),))],
        **params(
            len(TERMS), 3 + len(packs) + len(BACK_SAVED), 2, block_flops(*sizes)
        ),
    )(
        flag,
        lines,
        gradient,
        *packs,
        *[saved[name] for name in BACK_SAVED],
        *[terms[name] for name in TERMS],
    )
    return result[:2], dict(zip(TERMS, result[2:]))


FEED_SAVED = (HAT2, STATS, SLOPE)
FEED_TERMS = (DBRANCH, DUPWARD)


def feed_kernel(layout, pack_count, *refs):
    (flag, core, lines, g_hbm), packs, saved, _, operands, outs, sums, refs = taken(
        refs, 4, pack_count, len(FEED_SAVED), len(FEED_TERMS), 3, 5, 4
    )
    act0, act1, branch0 = operands
    vec_out, offs_out, total_out, branch_out, upward_out = outs
    names = (CONTRACT,) + FEED_SAVED + FEED_TERMS + (TOTAL, G_IN)
    buffers, (act, branch, pieces, sems, in_sems, out_sems) = taken(refs, len(names))
    places = {DBRANCH: branch_out, DUPWARD: upward_out}
    first_copies, first_arrive = load_pairs(
        (act0, act1, branch0, branch_out), (act, branch), branch.shape[1], in_sems
    )

    @pl.when(flag[0] == 1)
    def _():
        copier = Copier(sems)
        held = Held(names, buffers, copier)
        held.fill(G_IN, g_hbm)
        held.fill(HAT2, saved[0])
        held.fill(STATS, saved[1])
        held.fill_weight(CONTRACT, layout, packs)
        held.fill(SLOPE, saved[2])

        def done(name):
            copier.send(held[name], places[name])

        vec_out[...] = jnp.zeros_like(vec_out)
        gradient = held[G_IN][...].astype(jnp.float32)
        backward_feed(gradient, lines, held, vec_out, offs_out, done)
        copier.send(held[TOTAL], total_out)
        copier.finish()

    contract_products(core, sums, act, branch, pieces, first_copies, first_arrive, out_sems)


def feed_block(flag, core, gradient, lines, packs, layout, saved, terms, operands):
    rows, features = gradient.shape
    hidden_size = saved[SLOPE].shape[-1]
    sizes = rows, features, hidden_size
    names = (TOTAL,) + FEED_TERMS
    groups = hidden_size // features
    blocks = features // BLOCK
    bf16 = jnp.bfloat16
    result = pl.pallas_call(
        functools.partial(feed_kernel, layout, len(packs)),
        out_shape=[
            jax.ShapeDtypeStruct((8, features), jnp.float32),
            jax.ShapeDtypeStruct((1, hidden_size), jnp.float32),
        ]
        + outputs_of(names, *sizes)
        + sum_shapes(2 * features, 2 * features),
        in_specs=[SMEM] * 2
        + [VMEM]
        + [ANY] * (1 + len(packs) + len(FEED_SAVED) + len(FEED_TERMS) + len(operands)),
        out_specs=[VMEM] * 2 + [ANY] * (len(names) + 4),
        scratch_shapes=scratch_of(
            (CONTRACT,) + FEED_SAVED + FEED_TERMS + (TOTAL, G_IN), *sizes
        )
        + [
            pltpu.VMEM((2 * rows, width), bf16)
            for width in (hidden_size, features)
        ]
        + [
            pltpu.VMEM((groups, 2, blocks // 2 // groups, BLOCK, hidden_size), bf16),
            pltpu.SemaphoreType.DMA((1 + len(layout) + len(FEED_SAVED) + len(names),)),
            pltpu.SemaphoreType.DMA((4, groups)),
            pltpu.SemaphoreType.DMA((groups, groups, 2)),
        ],
        **params(
            len(FEED_TERMS),
            4 + len(packs) + len(FEED_SAVED),
            3,
            block_flops(*sizes),
        ),
    )(
        flag,
        core,
        lines,
        gradient,
        *packs,
        *[saved[name] for name in FEED_SAVED],
        *[terms[name] for name in FEED_TERMS],
        *operands,
    )
    return result[:2], dict(zip(names, result[2:])), result[5:]


REST_IN = (DUPWARD, TOTAL, HAT1, STATS, MIX, PROBS)
REST_ORDER = (DUPWARD, EXPAND, TOTAL, HAT1, STATS, OUT, MIX, PROBS, PROJ)
REST_TERMS = (TOTAL, DOUTPUT, DMIX)


REST_WEIGHTS = (PROJ, OUT, EXPAND)


def closing_kernel(plan, layout, pack_count, *refs):
    (flag, core, lines), parts, packs, sources, _, operands, terms, outs, refs = taken(
        refs, 3, 8, pack_count, len(REST_IN), len(REST_TERMS), 6, len(REST_TERMS), 4
    )
    names = REST_WEIGHTS + REST_IN + (DOUTPUT, DMIX, DATT)
    held_buffers, buffers, (vec, sems, *scratch) = taken(refs, len(names), 4)
    places = dict(zip(REST_TERMS, terms))
    sources = dict(zip(REST_IN, sources))

    @pl.when(flag[0] == 1)
    def _():
        copier = Copier(sems)
        held = Held(names, held_buffers, copier)
        for name in REST_ORDER:
            if name in NAMES:
                held.fill_weight(name, layout, packs)
            else:
                held.fill(name, sources[name])

        def done(name):
            copier.send(held[name], places[name])

        vec[...] = jnp.zeros_like(vec)
        backward_rest(lines, held, vec, done)
        copier.finish()

    att0, att1, dout0, x0, x1, dmix0 = operands
    pairs = (att0, att1, dout0, places[DOUTPUT], x0, x1, dmix0, places[DMIX])
    own = (parts[4], parts[5], vec, parts[6], parts[7])
    row_products(plan, core, (flag, tuple(parts[:4]) + own), pairs, outs, buffers, *scratch)


def closing_block(plan, flag, core, lines, parts, packs, layout, saved, feed, terms, operands):
    rows, features = feed[TOTAL].shape
    sizes = rows, features, feed[DUPWARD].shape[-1]
    sources = dict(saved) | {DUPWARD: feed[DUPWARD], TOTAL: feed[TOTAL]}
    names = REST_WEIGHTS + REST_IN + (DOUTPUT, DMIX, DATT)
    pairs = [
        pltpu.VMEM((2 * rows, operand.shape[1]), jnp.bfloat16)
        for operand in (operands[0], operands[2], operands[3], operands[5])
    ]
    result = pl.pallas_call(
        functools.partial(closing_kernel, plan, layout, len(packs)),
        out_shape=outputs_of(REST_TERMS, *sizes)
        + sum_shapes(2 * features + 128, 2 * features),
        in_specs=[SMEM] * 2
        + [VMEM] * (1 + len(parts))
        + [ANY] * (len(packs) + len(REST_IN) + len(REST_TERMS) + len(operands)),
        out_specs=[ANY] * (len(REST_TERMS) + 4),
        scratch_shapes=scratch_of(names, *sizes)
        + pairs
        + [
            pltpu.VMEM((8, features), jnp.float32),
            pltpu.SemaphoreType.DMA((len(layout) + len(REST_IN) + len(REST_TERMS),)),
        ]
        + row_scratch(4, 4, features),
        **params(
            len(REST_TERMS),
            3 + len(parts) + len(packs) + len(REST_IN),
            0,
            block_flops(*sizes) * 3 // 2,
        ),
    )(
        flag,
        core,
        lines,
        *parts,
        *packs,
        *[sources[name] for name in REST_IN],
        *[terms[name] for name in REST_TERMS],
        *operands,
    )
    return dict(zip(REST_TERMS, result)), result[len(REST_TERMS) :]


def load_pairs(sources, buffers, width, sems):
    copies = {}
    for i, buffer in enumerate(buffers):
        rows = buffer.shape[0] // 2
        for column in range(0, buffer.shape[1], width):
            columns = pl.ds(column, width)
            for half in range(2):
                copies.setdefault((i, column), []).append(
                    pltpu.make_async_copy(
                        sources[2 * i + half].at[:, columns],
                        buffer.at[pl.ds(half * rows, rows), columns],
                        sems.at[2 * i + half, column // width],
                    )
                )
    waited = set()

    def arrive(which, column):
        if (which, column) not in waited:
            waited.add((which, column))
            for copy in copies[which, column]:
                copy.wait()

    return copies, arrive


def contract_products(core, outs, act, grad, pieces, copies, arrive, out_sems):
    features = grad.shape[1]
    groups = act.shape[1] // features
    span = outs[0].shape[-1] // features
    for which in [(1, 0)] + [(0, part * features) for part in range(groups)]:
        for copy in copies[which]:
            copy.start()
    arrive(1, 0)
    sends = []
    for part in range(groups):
        columns = pl.ds(part * features, features)
        arrive(0, part * features)
        piece = dot_tn(act[:, columns], grad[...]).astype(jnp.bfloat16)
        for block in range(4):
            for group in range(groups):
                lanes = slice(group * features, (group + 1) * features)
                at = (block * groups + group) * BLOCK
                pieces[part, block % 2, block // 2, :, lanes] = piece[at : at + BLOCK]
        for target in range(groups // span):
            for side in range(2):
                lanes = pl.ds(target * span * features, span * features)
                copy = pltpu.make_async_copy(
                    pieces.at[part, core[0] ^ side, :, :, lanes],
                    outs[2 * target + side].at[:, part % 2, part // 2],
                    out_sems.at[part, target, side],
                )
                copy.start()
                sends.append(copy)
    for copy in sends:
        copy.wait()


def vector_columns(flag, parts, target):
    turned, own, _ = taken(parts, 4, 5)
    chosen = flag[0] == 1
    vec = jnp.where(chosen, own[0][...] + own[1][...] + own[2][...], turned[0][...] + turned[1][...])
    marks = jnp.where(chosen, own[3][...] + own[4][...], turned[2][...] + turned[3][...])
    features = vec.shape[1]
    lane = lax.broadcasted_iota(jnp.int32, (features, 128), 1)
    column = jnp.concatenate([vec.T, jnp.zeros((features, 120), jnp.float32)], axis=1)
    marks = jnp.broadcast_to(marks, (8, marks.shape[1])).T.reshape(features // BLOCK, -1, BLOCK, 8)
    for group in range(marks.shape[1]):
        part = jnp.broadcast_to(marks[:, group].reshape(features, 8)[:, 0:1], column.shape)
        column = jnp.where(lane == 8 + group, part, column)
    coarse = column.astype(jnp.bfloat16)
    fine = pltpu.roll(column - coarse.astype(jnp.float32), 12, 1)
    both = jnp.where(lane < 12, column, jnp.where(lane < 24, fine, 0.0)).astype(jnp.bfloat16)
    for block in range(features // BLOCK):
        place = tuple((block >> level) & 1 for level in range(4))
        target[place] = both[block * BLOCK : (block + 1) * BLOCK]


def row_products(plan, core, vectors, sources, outs, buffers, pieces, small, in_sems, out_sems):
    width = pieces.shape[-1]
    copies, arrive = load_pairs(sources, buffers, width, in_sems)
    needs = [need for entry in plan for need in ((entry[0], 0), (entry[1], entry[2]))]
    for need in dict.fromkeys(needs):
        for copy in copies[need]:
            copy.start()
    sends = []

    def send(source, place, sem):
        copy = pltpu.make_async_copy(source, place, sem)
        copy.start()
        sends.append(copy)

    if vectors:
        vector_columns(*vectors, small)
        for side in range(2):
            place = outs[side].at[:, :, :, :, pl.ds(outs[side].shape[-1] - 128, 128)]
            send(small.at[core[0] ^ side], place, out_sems.at[len(plan), side])
    for part, (left, right, column, target, to) in enumerate(plan):
        arrive(left, 0)
        arrive(right, column)
        piece = dot_tn(buffers[left][...], buffers[right][:, column : column + width])
        piece = piece.astype(jnp.bfloat16)
        for block in range(piece.shape[0] // BLOCK):
            place = tuple((block >> level) & 1 for level in range(4))
            pieces[(part,) + place] = piece[block * BLOCK : (block + 1) * BLOCK]
        for side in range(2):
            place = outs[2 * target + side].at[:, :, :, :, pl.ds(to, width)]
            send(pieces.at[part, core[0] ^ side], place, out_sems.at[part, side])
    for copy in sends:
        copy.wait()


def row_scratch(parts, pairs, features):
    return [
        pltpu.VMEM((parts, 2, 2, 2, 2, BLOCK, features), jnp.bfloat16),
        pltpu.VMEM((2, 2, 2, 2, BLOCK, 128), jnp.bfloat16),
        pltpu.SemaphoreType.DMA((2 * pairs, 4)),
        pltpu.SemaphoreType.DMA((parts + 1, 2)),
    ]


def sum_shapes(*widths):
    return [
        jax.ShapeDtypeStruct((2, 2, 2, BLOCK, width), jnp.bfloat16)
        for width in widths
        for _ in range(2)
    ]


def rows_kernel(plan, count, core, *refs):
    sources, outs, buffers, scratch = taken(refs, 2 * count, len(refs) - 3 * count - 4, count)
    row_products(plan, core, (), sources, outs, buffers, *scratch)


def rows_block(plan, core, operands, *widths):
    rows, features = operands[0].shape
    count = len(operands) // 2
    return pl.pallas_call(
        functools.partial(rows_kernel, plan, count),
        out_shape=sum_shapes(*widths),
        in_specs=[SMEM] + [ANY] * len(operands),
        out_specs=[ANY] * (2 * len(widths)),
        scratch_shapes=[
            pltpu.VMEM((2 * rows, operand.shape[1]), jnp.bfloat16) for operand in operands[::2]
        ]
        + row_scratch(len(plan), count, features),
        **params(0, 0, 0, 4 * len(plan) * features * features * 512),
    )(core, *operands)


def pack_kernel(plan, *refs):
    target = refs[-1]
    for source, row, column, width, place in plan:
        block = refs[source][0, row : row + target.shape[0], column : column + width]
        target[:, place : place + width] = block


def packed(arrays, pieces, rows):
    width = sum(piece[3] for piece in pieces)
    if rows % 16:
        return jnp.concatenate(
            [arrays[i][0, r : r + rows, c : c + w] for i, r, c, w in pieces], axis=1
        )
    plan, place = [], 0
    for piece in pieces:
        plan.append(piece + (place,))
        place += piece[3]
    return pl.pallas_call(
        functools.partial(pack_kernel, tuple(plan)),
        out_shape=jax.ShapeDtypeStruct((rows, width), jnp.bfloat16),
        in_specs=[VMEM] * len(arrays),
        out_specs=VMEM,
    )(*arrays)


def refold(columns, shards_of, features):
    rows = features // shards_of
    if rows == BLOCK:
        return columns
    natural = jnp.moveaxis(columns.reshape(shards_of, rows, -1, features), 2, 1)
    natural = natural.reshape(features // BLOCK, -1, BLOCK, features)
    return jnp.moveaxis(natural, 1, 2).reshape(features, -1)


def unfold(blocks, shards_of, features):
    rows = features // shards_of
    if rows == BLOCK:
        return blocks
    natural = jnp.moveaxis(blocks.reshape(features // BLOCK, BLOCK, -1, features), 2, 1)
    natural = natural.reshape(shards_of, -1, rows, features)
    return jnp.moveaxis(natural, 1, 2).reshape(shards_of, rows, -1)


def swapped(block, level):
    route = [(i, i ^ (1 << level)) for i in range(lax.axis_size(DP))]
    return lax.ppermute(block, DP, route)


def added(first, second):
    return (first.astype(jnp.float32) + second.astype(jnp.float32)).astype(jnp.bfloat16)


def tied(value, *others):
    return lax.optimization_barrier((value,) + others)[0]


def bit(level):
    return (lax.axis_index(DP) >> level) & 1


def by_bits(block, levels):
    block = block.reshape((2,) * levels + block.shape[1:])
    return jnp.transpose(block, tuple(range(levels))[::-1] + tuple(range(levels, block.ndim)))


def outgoing(block, level):
    return lax.dynamic_index_in_dim(block, 1 - bit(level), 0, keepdims=False)


def joined(state, got, level, after=()):
    block = state[0]
    if isinstance(block, tuple):
        keep = block[0]
    else:
        keep = lax.dynamic_index_in_dim(block, tied(bit(level), *after), 0, keepdims=False)
    total = added(keep, got)
    if level + 1 == lax.axis_size(DP).bit_length() - 1:
        return total, total
    return total, outgoing(total, level + 1)


def halved(state, level):
    return joined(state, swapped(state[1], level), level)


def first_state(keep, send, shards_of, features, contracted, small):
    levels = shards_of.bit_length() - 1
    if features == BLOCK * shards_of:
        return (keep,), send
    blocks = jnp.transpose(jnp.stack([keep, send]), (3, 2, 1, 0, 4, 5))
    blocks = blocks.reshape((-1,) + blocks.shape[4:])
    if contracted:
        blocks = unfold(blocks, shards_of, features)
    else:
        blocks = blocks.reshape(shards_of, features // shards_of, -1)
    if small:
        lines = blocks[:, :, 2 * features :].reshape(features, 128)
        marks = jnp.stack([lines[:, 8:12], lines[:, 20:24]]).reshape(2, -1, BLOCK, 4)
        marks = jnp.moveaxis(marks, 3, 2).reshape(2, shards_of, 4, -1)
        marks = jnp.moveaxis(marks, 2, 3).reshape(2, features, 4)
        lines = jnp.concatenate([lines[:, :8], marks[0], lines[:, 12:20], marks[1]], axis=1)
        lines = jnp.pad(lines, ((0, 0), (0, 104))).reshape(shards_of, -1, 128)
        blocks = jnp.concatenate([blocks[:, :, : 2 * features], lines], axis=2)
    blocks = by_bits(blocks, levels)
    return blocks, outgoing(blocks, 0)


def doubled(block, level, other):
    upper = bit(level) == 1
    return jnp.concatenate(
        [jnp.where(upper, other, block), jnp.where(upper, block, other)], axis=0
    )


def shards(
    inputs,
    keep_mask,
    lengths,
    slot_order,
    cotangent,
    query_projection,
    query_output,
    query_expand,
    query_contract,
    query_gains,
    query_biases,
    query_offsets,
    momentum_projection,
    momentum_output,
    momentum_expand,
    momentum_contract,
    momentum_gains,
    momentum_biases,
    momentum_offsets,
):
    first_section = lax.axis_index(SECTION) == 0
    shards_of = lax.axis_size(DP)
    crop_count, crop_len, features = inputs.shape[1:]
    rows = features // shards_of
    hidden_size = query_expand.shape[2]
    groups = hidden_size // features
    blocks = features // BLOCK

    def folded(which):
        return [(which, i * rows, 0, features) for i in range(groups)]

    late_from, late_to = 2 * features // 3, 2 * features
    own = packed(
        (query_projection, query_output, query_expand, query_contract)
        + (momentum_output, momentum_projection),
        [(0, 0, 0, 3 * features), (1, 0, 0, features), (2, 0, 0, hidden_size)]
        + folded(3)
        + [(4, 0, 0, features), (5, 0, late_from, late_to - late_from)],
        rows,
    )
    gathered = lax.all_gather(own, DP, axis=0, tiled=True)
    rest = packed(
        (tied(momentum_projection, own), momentum_expand, momentum_contract),
        [(0, 0, 0, late_from), (0, 0, late_to, 3 * features - late_to), (1, 0, 0, hidden_size)]
        + folded(2),
        rows,
    )
    late = lax.all_gather(rest, DP, axis=0, tiled=True)

    sizes = (2 * rows, 6 * rows, groups * rows)
    vectors = jnp.concatenate(
        [
            array[0].reshape(-1)
            for array in (
                query_gains,
                query_biases,
                query_offsets,
                momentum_gains,
                momentum_biases,
                momentum_offsets,
            )
        ]
    )[None]
    levels = shards_of.bit_length() - 1
    for level in range(levels):
        vectors = doubled(vectors, level, swapped(vectors, level))
    vectors = vectors.astype(jnp.float32)

    def vector_rows(start):
        lines = vectors[:, start : start + 8 * rows].reshape(shards_of, 8, rows)
        marks = vectors[:, start + 8 * rows : start + sum(sizes)]
        return jnp.moveaxis(lines, 1, 0).reshape(8, features), marks.reshape(1, hidden_size)

    query_lines, query_offs = vector_rows(0)
    momentum_lines, momentum_offs = vector_rows(sum(sizes))

    inner = 4 * features + hidden_size
    vectors_at = inner + groups * features
    if rows != BLOCK:
        gathered = jnp.concatenate(
            [
                gathered[:, :inner],
                refold(gathered[:, inner:vectors_at], shards_of, features),
                gathered[:, vectors_at:],
            ],
            axis=1,
        )
        late_end = late.shape[1] - groups * features
        late = jnp.concatenate(
            [late[:, :late_end], refold(late[:, late_end:], shards_of, features)], axis=1
        )
    gathered = gathered.reshape(blocks, BLOCK, -1)
    late = late.reshape(blocks, BLOCK, -1)
    query_layout = (
        (PROJ, 0, 0, 3 * features, 0),
        (OUT, 0, 3 * features, features, 0),
        (EXPAND, 0, 4 * features, hidden_size, 0),
        (CONTRACT, 0, inner, hidden_size, 0),
    )
    late_expand = 3 * features - (late_to - late_from)
    momentum_layout = (
        (PROJ, 0, vectors_at + features, late_to - late_from, late_from),
        (PROJ, 1, 0, late_from, 0),
        (PROJ, 1, late_from, 3 * features - late_to, late_to),
        (OUT, 0, vectors_at, features, 0),
        (EXPAND, 1, late_expand, hidden_size, 0),
        (CONTRACT, 1, late_expand + hidden_size, hidden_size, 0),
    )

    positions = lax.broadcasted_iota(jnp.int32, keep_mask.shape, 2)
    validity = ((positions < lengths[:, :, None]) & ((keep_mask > 0) | (positions == 0))).astype(
        jnp.float32
    )
    across = validity[:, :, None, :]
    down = validity[:, :, :, None]
    in_first = first_section.astype(jnp.int32).reshape(1)
    in_second = 1 - in_first

    def momentum_forward(flag, block_in):
        return forward_block(
            flag,
            block_in,
            across,
            down,
            momentum_lines,
            momentum_offs,
            (gathered, late),
            momentum_layout,
            False,
            1,
            0,
            crop_count,
        )[:2]

    crops = range(crop_count)
    last = crop_count - 1
    started, turned, before = [], [], [momentum_lines, momentum_offs]
    for c in crops:
        started.append(
            forward_block(
                tied(in_first, *before),
                inputs,
                across,
                down,
                query_lines,
                query_offs,
                (gathered,),
                query_layout,
                True,
                0,
                c,
                1,
            )
        )
        before = [started[c][1]]
    passed = [lax.ppermute(started[c][0], SECTION, [(0, 1)]) for c in crops]
    for c in crops:
        turned.append(
            turn_block(
                tied(in_second, *before),
                passed[c],
                cotangent,
                across,
                down,
                query_lines,
                query_offs,
                (gathered,),
                query_layout,
                c,
                started[c][2],
            )
        )
        before = [turned[c][0][0]]
    returned = [lax.ppermute(turned[c][0][3], SECTION, [(1, 0)]) for c in crops]
    ended = [
        backward_block(
            in_first,
            returned[c],
            query_lines,
            (gathered,),
            query_layout,
            started[c][2],
            turned[c][1],
        )
        for c in crops[:last]
    ]
    core = lax.axis_index(DP) & 1 if rows == BLOCK else jnp.int32(0)
    core = jnp.asarray(core, jnp.int32).reshape(1)
    outer = [turned[c][1] | ended[c][1] for c in crops[:last]]

    def operands(name, *ends):
        return [end[name] for end in ends or outer + [turned[last][1]]]

    feed_ends, feed_terms, sums = feed_block(
        tied(in_first, *[end[0][0] for end in ended]),
        core,
        returned[last],
        query_lines,
        (gathered,),
        query_layout,
        started[last][2],
        turned[last][1],
        operands(ACT) + operands(DBRANCH, *outer),
    )
    ends = outer + [turned[last][1] | feed_terms]

    def pairs(sums, contracted=False, small=False):
        return [
            first_state(
                sums[2 * i], sums[2 * i + 1], shards_of, features, contracted, small and not i
            )
            for i in range(len(sums) // 2)
        ]

    chunks = pairs(sums, True)
    first = [swapped(chunk[1], 0) for chunk in chunks]
    sums = rows_block(
        tuple((0, 1, i * features, i // 2, i % 2 * features) for i in range(groups)),
        tied(core, feed_ends[0]),
        operands(LOW) + [end[DUPWARD] for end in ends],
        2 * features,
        2 * features,
    )
    chunks += pairs(sums)
    *first, _ = lax.optimization_barrier((*first, sums[0]))
    half = groups // 2
    level_of = [0] * 6

    key_pools, key_ways = [], []

    def advance(i, got, after=()):
        chunks[i] = joined(chunks[i], got, level_of[i], after)
        level_of[i] += 1

    def wide(parts):
        return jnp.concatenate(parts, axis=1).astype(jnp.float32)

    def finished():
        contract_sum = jnp.moveaxis(
            wide([chunk[0] for chunk in chunks[:half]]).reshape(rows, groups, features), 1, 0
        )
        last_columns = chunks[4][0]
        small = last_columns[:, half * features :].astype(jnp.float32)
        small = (small[:, :12] + small[:, 12:24]).T
        return (
            last_columns[None, :, :features].astype(jnp.float32),
            wide([chunk[0] for chunk in chunks[half : 2 * half]])[None],
            contract_sum.reshape(1, groups * rows, features),
            small[None, :2],
            small[None, 2:8],
            small[8:].reshape(1, groups * rows),
        )

    def step(moving, *kernels, passing=()):
        gots = [swapped(chunks[i][1], level_of[i]) for i in moving]
        before = tuple(chunks[i][1] for i in moving)
        for kernel in kernels:
            before = (kernel(*before),)
        passing = [way() for way in passing]
        *gots, done = lax.optimization_barrier((*gots, *passing, *before[:1]))
        for i, got in zip(moving, gots):
            advance(i, got)
        return gots[len(moving) :], done

    def closing(*before):
        turned_parts = [turned[c][0][1] for c in crops] + [turned[c][0][2] for c in crops]
        own_parts = [ended[0][0][0], feed_ends[0], ended[0][0][1], feed_ends[1]]
        terms, sums = closing_block(
            (
                (0, 1, 0, 0, 0),
                (2, 3, 0, 0, features),
                (2, 3, features, 1, 0),
                (2, 3, 2 * features, 1, features),
            ),
            tied(in_first, *before),
            core,
            query_lines,
            turned_parts + own_parts,
            (gathered,),
            query_layout,
            started[last][2],
            feed_terms,
            turned[last][1],
            operands(ATT) + operands(DOUTPUT, *outer) + operands(X_IN) + operands(DMIX, *outer),
        )
        ends[last] = ends[last] | terms
        chunks.extend(pairs(sums, False, True))
        return sums[2]

    def key_first(*before):
        key_out, pool = momentum_forward(tied(in_first, *before), inputs)
        key_ways.append(lax.ppermute(key_out, SECTION, [(0, 1)]))
        key_pools.append(pool)
        return pool

    def key_second(*before):
        return momentum_forward(tied(in_second, *before), key_ways[0])[1]

    def unfinished(*second):
        return [
            i
            for i in range(len(chunks))
            if level_of[i] < levels and (level_of[i] != 1 or i in second)
        ]

    for i, got in enumerate(first):
        advance(i, got)
    for i in (2, 3):
        advance(i, swapped(chunks[i][1], 0))
    step([0, 1], key_first)
    both = (lambda: swapped(chunks[4][1], 0), lambda: swapped(chunks[5][1], 0))
    gots, done = step(unfinished(2, 3), closing, key_second, passing=both)
    for i, got in zip((4, 5), gots):
        advance(i, got)

    key_pool = jnp.where(first_section, key_pools[0], done)
    pools = [jnp.where(first_section, started[c][1], turned[c][0][0]) for c in crops]
    pooled = jnp.concatenate([jnp.concatenate(pools, axis=0)[:, None], key_pool[:, None]], axis=1)
    order = (slot_order[:, None] == jnp.arange(crop_count, dtype=jnp.int32)[None, :])[..., None]
    pooled = jnp.sum(jnp.where(order, pooled.reshape(crop_count, -1)[None], 0.0), axis=1)
    ways = [0] + list(range(2, levels)) + [1]
    pooled = pooled[None]
    moves = [(4, 2, 3), (5, 4, 0, 1), (5, 4, 2, 3), (5,)]
    for way, moving in zip(ways, moves + [()] * (levels - len(moves))):
        gots = [swapped(chunks[i][1], level_of[i]) for i in moving]
        *gots, other = lax.optimization_barrier((*gots, swapped(pooled, way)))
        for i, got in zip(moving, gots):
            advance(i, got, finished() if moving == (5,) and level_of[4] == levels else ())
        pooled = doubled(pooled, way, other)
    for i in range(6):
        while level_of[i] < levels:
            advance(i, swapped(chunks[i][1], level_of[i]))
    pooled = pooled.reshape((2,) * levels + (crop_count, 2, features))
    axes = sorted(range(levels), key=lambda j: -ways[levels - 1 - j])
    pooled = jnp.transpose(pooled, tuple(axes) + tuple(range(levels, levels + 3)))
    pooled = jnp.moveaxis(pooled.reshape(-1, 2, features), 1, 0)[None]
    grad_input = jnp.stack([tied(end[TOTAL], done) for end in ends])[None]
    first_features, *others = finished()
    project_sum = wide([chunks[4][0][:, features : half * features], chunks[5][0]])
    return (pooled, grad_input, project_sum[None], first_features, *others)


def solution(mesh):
    in_specs = (
        P(None, DP, None, None),
        P(None, DP, None),
        P(None, DP),
        P(DP),
        P(DP, None, None),
        P(SECTION, DP, None),
        P(SECTION, DP, None),
        P(SECTION, DP, None),
        P(SECTION, DP, None),
        P(SECTION, None, DP),
        P(SECTION, None, DP),
        P(SECTION, DP),
        P(SECTION, DP, None),
        P(SECTION, DP, None),
        P(SECTION, DP, None),
        P(SECTION, DP, None),
        P(SECTION, None, DP),
        P(SECTION, None, DP),
        P(SECTION, DP),
    )
    out_specs = (
        P(SECTION, None, None, None),
        P(SECTION, DP, None, None),
        P(SECTION, DP, None),
        P(SECTION, DP, None),
        P(SECTION, DP, None),
        P(SECTION, DP, None),
        P(SECTION, None, DP),
        P(SECTION, None, DP),
        P(SECTION, DP),
    )
    return jax.shard_map(shards, mesh=mesh, in_specs=in_specs, out_specs=out_specs, check_vma=False)
```
